32 devices in a mesh: sec: 4 (over y, x), lat: 4 (over z), col: 2 (over core).
Axes of the slice: x: 2, y: 2, z: 4, core: 2. Of those that a mesh axis runs over, the one named last changes fastest.
Arguments:
- physical_state: bfloat16 [32, 64, 5120], P(('sec', 'lat', 'col')), may hold values from -6 to 6
- parallel_lengths: int32 [32], P(('sec', 'lat', 'col')), may hold values from 20 to 5120, as said below
- zonal_mode_assignment: int32 [856], replicated, may hold values from 0 to 640, as said below
- weighted_associated_polynomials: bfloat16 [856, 640, 32], P('lat', None, ('sec', 'col')), may hold values from -1 to 1
- marine_tracer_state: float32 [8, 128, 4096], P(None, ('sec', 'lat', 'col')), may hold values from -6 to 6
- lateral_diffusivity: float32 [128, 4096], P(('sec', 'lat', 'col')), may hold values from 0.015 to 0.15
- depthwise_diffusivity: float32 [128, 4096], P(('sec', 'lat', 'col')), may hold values from 0.02 to 0.2
- water_indicator: int32 [128, 4096], P(('sec', 'lat', 'col')), may hold values 0 or 1
- overlying_parallel: int32 [128], P(('sec', 'lat', 'col')), may hold values from 0 to 31, as said below
- underlying_marine_parallel: int32 [32], P(('sec', 'lat', 'col')), may hold values from 0 to 127, as said below
Outputs:
- harmonic_amounts: float32 [640, 856, 128], P(('sec', 'col'), 'lat')
- ocean_next: float32 [8, 128, 4096], P(None, ('sec', 'lat', 'col'))
The draws below stay inside these ranges and needn't reach their ends.
Inputs may be any that keep to these rules, and one draw needn't show every extreme that they name: `parallel_lengths`: row j holds 20 + 4 * min(max(b + s * j, 0), 1275) points, with s = 42 and one offset b from (5100) // 4 - s * (31) to 0; the first row holds 20 points and the last 5120. `zonal_mode_assignment`: every wavenumber below 640 sits in exactly one slot; the other slots hold 640, meaning empty; slots s with equal s // 214 form a block, at least one block has all its slots taken. overlying_parallel[r] lies between (r // 4 - 1) * 1 and (r // 4 + 2) - 1; some rows reach the lower end and some the upper end. underlying_marine_parallel[j] lies between (j - 1) * 4 and (j + 2) * 4 - 1; some rows reach the lower end and some the upper end.
All inputs are finite; a program needn't handle non-finite values. No bound on the sum of `water_indicator` on one device may be relied on, other than what follows from the above.
Results may differ from the reference program's by a relative error of at most 0.004.
Values may be sent and summed in bfloat16 or wider, within the bound.
A program may use at most 256 MiB of HBM per device.

```python
import math
import jax
import jax.numpy as jnp
from jax import lax

NLON = 5120
M = 640
STRATA = 16
RD = 1
ORD = 4
MARINE_POINTS = 4096
DEPTH_LAYERS = 8
OSTEPS = 4
ROWS = 32
MARINE_LINES = 128
MSLOT = 214
SLOTS = 856
N_LAT = 4
N_COL = 2


def draw_parallel_lengths(key, part):
    equator_index = (NLON - 20) // 4
    stride_rows = (equator_index + ROWS - 1) // (ROWS - 1)
    bottom_stratum = equator_index - stride_rows * (ROWS - 1)
    offset = jax.random.randint(key, (), bottom_stratum, 1)
    latitude = offset + stride_rows * jnp.arange(ROWS, dtype=jnp.int32)
    latitude = jnp.clip(latitude, 0, equator_index)
    return (20 + 4 * latitude).astype(jnp.int32)


def draw_zonal_mode_assignment(key, part):
    key_full, key_order, key_wave = jax.random.split(key, 3)
    full_block = jax.random.randint(key_full, (), 0, SLOTS // MSLOT)
    scores = jax.random.permutation(key_order, SLOTS).astype(jnp.int32)
    owners = jnp.arange(SLOTS, dtype=jnp.int32) // MSLOT
    scores = scores + SLOTS * (owners != full_block).astype(jnp.int32)
    ranking = jnp.argsort(jnp.argsort(scores, stable=True), stable=True).astype(jnp.int32)
    wave_order = jax.random.permutation(key_wave, M).astype(jnp.int32)
    return jnp.where(ranking < M, wave_order[jnp.minimum(ranking, M - 1)], M).astype(jnp.int32)


def neighbour_rows(key, count, own_each, other_each, other_total, every_block):
    index_all = jnp.arange(count, dtype=jnp.int32)
    block_index = index_all // own_each
    base_row = block_index * other_each
    offset = jax.random.randint(key, (count,), -other_each, 2 * other_each)
    chosen = base_row + offset
    first_row = index_all % own_each == 0
    last_row = index_all % own_each == own_each - 1
    if every_block:
        lower_pick = first_row
        upper_pick = last_row & jnp.logical_not(first_row)
    else:
        lower_pick = first_row & (block_index % 2 == 0)
        upper_pick = last_row & (block_index % 4 == 1)
    chosen = jnp.where(lower_pick, base_row - other_each, chosen)
    chosen = jnp.where(upper_pick, base_row + 2 * other_each - 1, chosen)
    return jnp.clip(chosen, 0, other_total - 1).astype(jnp.int32)


def draw_overlying_parallel(key, part):
    return neighbour_rows(key, MARINE_LINES, ORD, RD, ROWS, True)


def draw_underlying_marine_parallel(key, part):
    return neighbour_rows(key, ROWS, RD, ORD, MARINE_LINES, False)


def touch_ends(values, stream_key, least, high):
    shape = values.shape
    place = [jax.random.randint(jax.random.fold_in(stream_key, axis), (), 0, shape[axis]) for axis in range(len(shape))]
    values = values.at[tuple(place)].set(least)
    longest = shape.index(max(shape))
    place[longest] = (place[longest] + 1) % shape[longest]
    return values.at[tuple(place)].set(high)


def block_scale(stream_key, shape, shards, low, top_value):
    def one(position, blocks):
        heights = jax.random.uniform(jax.random.fold_in(jax.random.fold_in(stream_key, 6), position), (blocks,), jnp.float32, low / len(shards), top_value / len(shards))
        return jnp.repeat(jnp.exp(heights), shape[position] // blocks).reshape((-1,) + (1,) * (len(shape) - position - 1))

    level = one(*shards[0])
    for cut in shards[1:]:
        level = level * one(*cut)
    return level


def normal_values(stream_key, extent, scale, most, pieces=(), kind=jnp.bfloat16):
    loudness = block_scale(stream_key, extent, pieces, -0.22, 0.18) if pieces else 1.0
    entries = jax.random.normal(stream_key, extent, jnp.float32) * scale * loudness
    return jnp.minimum(jnp.maximum(entries, -most), most).astype(kind)


def setup_inputs(seed: int = 0) -> dict:
    splits = jax.random.split(jax.random.key(seed), 11)
    physical_state = normal_values(splits[0], (ROWS, 4 * STRATA, NLON), 1.0, 6.0, ((0, 32),))
    parallel_lengths = draw_parallel_lengths(jax.random.fold_in(splits[10], 71), 0)
    zonal_mode_assignment = draw_zonal_mode_assignment(jax.random.fold_in(splits[10], 71), 0)
    weighted_associated_polynomials = normal_values(splits[3], (SLOTS, M, ROWS), ROWS ** -0.5, 1.0, ((0, 4), (2, 8)))
    marine_tracer_state = normal_values(splits[4], (DEPTH_LAYERS, MARINE_LINES, MARINE_POINTS), 1.0, 6.0, ((1, 32),), jnp.float32)
    lateral_diffusivity = jnp.clip(jnp.exp(math.log(0.15) - 2.3025852 * jax.random.uniform(splits[5], (MARINE_LINES, MARINE_POINTS), jnp.float32) ** block_scale(splits[5], (MARINE_LINES, MARINE_POINTS), ((0, 32),), -0.2, 0.2)), 0.015, 0.15)
    depthwise_diffusivity = jnp.clip(jnp.exp(math.log(0.2) - 2.3025851 * jax.random.uniform(splits[6], (MARINE_LINES, MARINE_POINTS), jnp.float32) ** block_scale(splits[6], (MARINE_LINES, MARINE_POINTS), ((0, 32),), -0.2, 0.2)), 0.02, 0.2)
    water_indicator = touch_ends((jax.random.randint(splits[7], (MARINE_LINES, MARINE_POINTS), 0, 5) < 4).astype(jnp.int32), jax.random.fold_in(splits[7], 1), 0, 1)
    overlying_parallel = draw_overlying_parallel(jax.random.fold_in(splits[10], 71), 0)
    underlying_marine_parallel = draw_underlying_marine_parallel(jax.random.fold_in(splits[10], 71), 0)
    return dict(physical_state=physical_state, parallel_lengths=parallel_lengths, zonal_mode_assignment=zonal_mode_assignment, weighted_associated_polynomials=weighted_associated_polynomials, marine_tracer_state=marine_tracer_state, lateral_diffusivity=lateral_diffusivity, depthwise_diffusivity=depthwise_diffusivity, water_indicator=water_indicator, overlying_parallel=overlying_parallel, underlying_marine_parallel=underlying_marine_parallel)


two_pi = 6.283185307179586
thermal_transfer_factor = 0.8
force_coef = 0.1

def fourier_table(row_points, wave_count, grid_width):
    wave_index = jnp.arange(wave_count, dtype=jnp.int32)
    positions = jnp.arange(grid_width, dtype=jnp.int32)
    points_float = row_points.astype(jnp.float32)
    angle_unit = jnp.float32(two_pi) / points_float
    residue = wave_index[:, None] * positions[None, :] % row_points
    angle = residue.astype(jnp.float32) * angle_unit
    inside = (positions[None, :] < row_points) & (wave_index[:, None] < row_points // 2)
    norm_factor = 1.0 / jnp.sqrt(points_float)
    real_part = jnp.where(inside, jnp.cos(angle) * norm_factor, 0.0)
    imag_part = jnp.where(inside, -jnp.sin(angle) * norm_factor, 0.0)
    return jnp.stack([real_part, imag_part]).astype(jnp.bfloat16)

def transform_order(row_total, lat_count, col_count, rows_each):
    index_all = jnp.arange(row_total, dtype=jnp.int32)
    group_rows = lat_count * rows_each
    group_id = index_all // group_rows
    within = index_all % group_rows
    return ((group_id // col_count * lat_count + within // rows_each) * col_count + group_id % col_count) * rows_each + within % rows_each

def advance_coupled_model(bordered_array, meridian_exchange_factor, zonal_exchange_factor, depthwise_exchange_factor, boundary_warming_term):
    centre = bordered_array[:, 1:-1]
    meridional = meridian_exchange_factor[1:] * (bordered_array[:, 2:] - centre) - meridian_exchange_factor[:-1] * (centre - bordered_array[:, :-2])
    east_flux = zonal_exchange_factor * (jnp.roll(centre, -1, axis=2) - centre)
    zonal_div = east_flux - jnp.roll(east_flux, 1, axis=2)
    vertical_flux = depthwise_exchange_factor * (centre[1:] - centre[:-1])
    zero_layer = jnp.zeros_like(vertical_flux[:1])
    vertical = jnp.concatenate([vertical_flux, zero_layer], 0) - jnp.concatenate([zero_layer, vertical_flux], 0)
    forced = jnp.concatenate([boundary_warming_term[None], jnp.zeros_like(centre[1:])], 0)
    return centre + meridional + zonal_div + vertical + forced

def reference(physical_state, parallel_lengths, zonal_mode_assignment, weighted_associated_polynomials, marine_tracer_state, lateral_diffusivity, depthwise_diffusivity, water_indicator, overlying_parallel, underlying_marine_parallel):
    vector_width = 8 * STRATA

    def row_transform(row_pair):
        fourier_matrix = fourier_table(row_pair[1], M, NLON).astype(jnp.float32)
        result = jnp.einsum('pmi,vi->mpv', fourier_matrix, row_pair[0].astype(jnp.float32), precision=lax.Precision.HIGHEST)
        return result.reshape(M, vector_width).astype(jnp.bfloat16)
    fourier = lax.map(row_transform, (physical_state, parallel_lengths))
    row_order = transform_order(ROWS, N_LAT, N_COL, RD)
    sorted_rows = jnp.take(fourier, row_order, axis=0)
    degrees = jnp.arange(M, dtype=jnp.int32)

    def slot_block(block_index):
        waves_here = lax.dynamic_slice_in_dim(zonal_mode_assignment, block_index * MSLOT, MSLOT)
        chosen = jnp.take(sorted_rows, jnp.clip(waves_here, 0, M - 1), axis=1).astype(jnp.float32)
        values = lax.dynamic_slice_in_dim(weighted_associated_polynomials, block_index * MSLOT, MSLOT, 0).astype(jnp.float32)
        summed = jnp.einsum('snq,qsv->nsv', values, chosen, precision=lax.Precision.HIGHEST)
        return jnp.where(degrees[:, None, None] >= waves_here[None, :, None], summed, 0.0)
    blocks = lax.map(slot_block, jnp.arange(N_LAT, dtype=jnp.int32))
    harmonic_amounts = jnp.transpose(blocks, (1, 0, 2, 3)).reshape(M, SLOTS, vector_width)
    skin_warmth_parallels = jnp.take(marine_tracer_state[0], underlying_marine_parallel, axis=0)
    grid_points = jnp.arange(NLON, dtype=jnp.int32)
    sea_column_index = jnp.minimum(grid_points[None, :] * MARINE_POINTS // parallel_lengths[:, None], MARINE_POINTS - 1)
    skin_warmth_mapped_upward = jnp.take_along_axis(skin_warmth_parallels, sea_column_index, axis=1)
    bottom_stratum = STRATA - 1
    zonal_wind = physical_state[:, bottom_stratum].astype(jnp.float32)
    meridional_wind = physical_state[:, STRATA + bottom_stratum].astype(jnp.float32)
    lowest_layer_warmth = physical_state[:, 2 * STRATA + bottom_stratum].astype(jnp.float32)
    breeze_speed = jnp.sqrt(zonal_wind * zonal_wind + meridional_wind * meridional_wind + 1.0)
    boundary_energy_exchange = thermal_transfer_factor * breeze_speed * (skin_warmth_mapped_upward - lowest_layer_warmth)
    ocean_points = jnp.arange(MARINE_POINTS, dtype=jnp.int32)
    grid_column = ocean_points[None, :] * parallel_lengths[:, None] // MARINE_POINTS
    flux_rows = jnp.take_along_axis(boundary_energy_exchange, grid_column, axis=1)
    forcing = jnp.take(flux_rows, overlying_parallel, axis=0)
    water_share = water_indicator.astype(jnp.float32)
    sea_pad = jnp.pad(water_share, ((1, 1), (0, 0)))
    kappa_pad = jnp.pad(lateral_diffusivity, ((1, 1), (0, 0)))
    meridian_exchange_factor = 0.5 * (kappa_pad[:-1] + kappa_pad[1:]) * sea_pad[:-1] * sea_pad[1:]
    zonal_exchange_factor = 0.5 * (lateral_diffusivity + jnp.roll(lateral_diffusivity, -1, axis=1)) * water_share * jnp.roll(water_share, -1, axis=1)
    depthwise_exchange_factor = depthwise_diffusivity * water_share
    boundary_warming_term = force_coef * water_share * forcing
    thermal_state = marine_tracer_state
    for iteration in range(OSTEPS):
        bordered_array = jnp.pad(thermal_state, ((0, 0), (1, 1), (0, 0)))
        thermal_state = advance_coupled_model(bordered_array, meridian_exchange_factor, zonal_exchange_factor, depthwise_exchange_factor, boundary_warming_term)
    return (harmonic_amounts, thermal_state)
```

```python
import functools

import jax
import jax.numpy as jnp
from jax import lax
from jax.experimental import pallas as pl
from jax.experimental.pallas import tpu as pltpu
from jax.sharding import PartitionSpec as P

OSTEPS = 4
LOW = 8
CHUNK = 256
SLOT_PAD = 16

two_pi = 6.283185307179586
thermal_transfer_factor = 0.8
force_coef = 0.1

GROUP = ("sec", "col")
LINE = ("sec", "lat", "col")


def angle_tables(points, wave_count, grid_width):
    low = jnp.arange(LOW, dtype=jnp.float32)
    mid = jnp.arange(CHUNK // LOW, dtype=jnp.float32) * LOW
    high = jnp.arange(grid_width // CHUNK, dtype=jnp.float32) * CHUNK
    place = jnp.concatenate([low, mid, high])
    count = points.astype(jnp.float32)
    product = place[:, None] * jnp.arange(wave_count, dtype=jnp.float32)[None, :]
    residue = product - jnp.round(product / count) * count
    angle = residue * (jnp.float32(two_pi) / count)
    scale = jnp.where(jnp.arange(place.shape[0]) >= LOW + CHUNK // LOW, 1.0 / jnp.sqrt(count), 1.0)
    return jnp.stack([jnp.cos(angle), -jnp.sin(angle)]) * scale[None, :, None]


MESH = pl.DeviceIdType.MESH


def place_of(index, lat_count, col_count):
    return {
        "sec": index // (lat_count * col_count),
        "lat": index // col_count % lat_count,
        "col": index % col_count,
    }


def exchange_kernel(
    sizes,
    points_ref,
    table_ref,
    slots_ref,
    x_ref,
    weight_ref,
    *refs,
):
    sec_count, lat_count, col_count = sizes
    halo, coef_out, weight_out, before, after = refs[:5]
    (base_ref, acc_ref, mine_ref, local_sem, weight_send, weight_recv, halo_send, halo_recv,
     lat_send, lat_recv, sec_send, sec_recv, col_send, col_recv) = refs[5:]
    groups = sec_count * col_count
    devices = groups * lat_count
    sec, lat, col = (lax.axis_index(name) for name in LINE)
    group = sec * col_count + col
    line = (sec * lat_count + lat) * col_count + col
    following = place_of((line + 1) % devices, lat_count, col_count)
    previous = place_of((line + devices - 1) % devices, lat_count, col_count)

    def group_place(step):
        other = (group + step) % groups
        return other, {"sec": other // col_count, "lat": lat, "col": other % col_count}

    def lat_place(step):
        other = (lat + step) % lat_count
        return other, {"sec": sec, "lat": other, "col": col}

    barrier = pltpu.get_barrier_semaphore()
    for place in (following, previous):
        pl.semaphore_signal(barrier, inc=1, device_id=place, device_id_type=MESH)

    @pl.loop(1, groups)
    def _(step):
        pl.semaphore_signal(barrier, inc=1, device_id=group_place(step)[1], device_id_type=MESH)

    @pl.loop(1, lat_count)
    def _(step):
        pl.semaphore_signal(barrier, inc=1, device_id=lat_place(step)[1], device_id_type=MESH)

    pl.semaphore_wait(barrier, groups + lat_count)

    def weight_copy(step):
        other, place = group_place(step)
        return pltpu.make_async_remote_copy(
            src_ref=weight_ref.at[other],
            dst_ref=weight_out.at[group],
            send_sem=weight_send.at[step],
            recv_sem=weight_recv.at[step],
            device_id=place,
            device_id_type=MESH,
        )

    def halo_copy(side):
        return pltpu.make_async_remote_copy(
            src_ref=halo,
            dst_ref=(before, after)[side],
            send_sem=halo_send.at[side],
            recv_sem=halo_recv.at[side],
            device_id=(following, previous)[side],
            device_id_type=MESH,
        )

    has_next, has_previous = line < devices - 1, line > 0

    def lat_copy(step):
        other, place = lat_place(step)
        return pltpu.make_async_remote_copy(
            src_ref=mine_ref.at[other],
            dst_ref=coef_out.at[group, lat],
            send_sem=lat_send.at[step],
            recv_sem=lat_recv.at[step],
            device_id=place,
            device_id_type=MESH,
        )

    def sec_copy(step):
        return pltpu.make_async_remote_copy(
            src_ref=coef_out.at[group],
            dst_ref=coef_out.at[group],
            send_sem=sec_send.at[step],
            recv_sem=sec_recv.at[step],
            device_id={"sec": (sec + step) % sec_count, "lat": lat, "col": col},
            device_id_type=MESH,
        )

    def col_copy(back, step):
        block = (sec + sec_count - back) % sec_count * col_count + col
        return pltpu.make_async_remote_copy(
            src_ref=coef_out.at[block],
            dst_ref=coef_out.at[block],
            send_sem=col_send.at[back, step],
            recv_sem=col_recv.at[back, step],
            device_id={"sec": sec, "lat": lat, "col": (col + step) % col_count},
            device_id_type=MESH,
        )

    own_weights = pltpu.make_async_copy(weight_ref.at[group], weight_out.at[group], local_sem.at[0])
    own_weights.start()

    @pl.loop(1, groups)
    def _(step):
        weight_copy(step).start()

    @pl.when(has_next)
    def _():
        halo_copy(0).start()

    @pl.when(has_previous)
    def _():
        halo_copy(1).start()

    points = points_ref[0]
    waves = table_ref.shape[2]
    fields = x_ref.shape[0]
    chunks = x_ref.shape[1] // CHUNK
    low_c, low_s = table_ref[0, :LOW], table_ref[1, :LOW]
    for b in range(CHUNK // LOW):
        mid_c = table_ref[0, LOW + b : LOW + b + 1]
        mid_s = table_ref[1, LOW + b : LOW + b + 1]
        base_ref[0, b * LOW : (b + 1) * LOW] = low_c * mid_c - low_s * mid_s
        base_ref[1, b * LOW : (b + 1) * LOW] = low_c * mid_s + low_s * mid_c
    acc_ref[...] = jnp.zeros_like(acc_ref)
    top = LOW + CHUNK // LOW

    @pl.loop(0, chunks)
    def _(a):
        start = pl.multiple_of(a * CHUNK, CHUNK)
        position = start + lax.broadcasted_iota(jnp.int32, (fields, CHUNK), 1)
        block = x_ref[:, pl.ds(start, CHUNK)].astype(jnp.float32)
        block = jnp.where(position < points, block, 0.0).astype(jnp.bfloat16)
        high_c = table_ref[0, pl.ds(top + a, 1)]
        high_s = table_ref[1, pl.ds(top + a, 1)]
        for w in range(0, waves, 128):
            cut = slice(w, w + 128)
            base_c, base_s = base_ref[0, :, cut], base_ref[1, :, cut]
            turn_c, turn_s = high_c[:, cut], high_s[:, cut]
            real = (base_c * turn_c - base_s * turn_s).astype(jnp.bfloat16)
            imag = (base_c * turn_s + base_s * turn_c).astype(jnp.bfloat16)
            both = jnp.concatenate([real, imag], axis=1)
            part = jnp.dot(block, both, preferred_element_type=jnp.float32)
            acc_ref[:fields, cut] += part[:, :128]
            acc_ref[fields:, cut] += part[:, 128:]

    wave = lax.broadcasted_iota(jnp.int32, acc_ref.shape, 1)
    coefs = jnp.where(wave < points // 2, acc_ref[...], 0.0).astype(jnp.bfloat16)
    padded = mine_ref.shape[1]

    def fill(other):
        held = slots_ref[pl.ds(pl.multiple_of(other * padded, 16), padded)]
        pick = held == lax.broadcasted_iota(jnp.int32, (padded, waves), 1)
        pick = jnp.where(pick, 1.0, 0.0).astype(jnp.bfloat16)
        mine_ref[other] = lax.dot_general(
            pick, coefs, (((1,), (1,)), ((), ())), preferred_element_type=jnp.float32
        ).astype(jnp.bfloat16)

    @pl.loop(1, lat_count)
    def _(step):
        fill((lat + step) % lat_count)
        lat_copy(step).start()

    fill(lat)
    own_coefs = pltpu.make_async_copy(mine_ref.at[lat], coef_out.at[group, lat], local_sem.at[1])
    own_coefs.start()
    own_coefs.wait()

    @pl.loop(1, lat_count)
    def _(step):
        lat_copy(step).wait_recv()

    @pl.loop(1, sec_count)
    def _(step):
        sec_copy(step).start()

    @pl.loop(1, col_count)
    def _(step):
        col_copy(0, step).start()

    @pl.loop(1, sec_count)
    def _(back):
        sec_copy(back).wait_recv()

        @pl.loop(1, col_count)
        def _(step):
            col_copy(back, step).start()

    @pl.when(has_next)
    def _():
        halo_copy(0).wait_send()
        halo_copy(1).wait_recv()

    @pl.when(has_previous)
    def _():
        halo_copy(1).wait_send()
        halo_copy(0).wait_recv()

    own_weights.wait()

    @pl.loop(1, groups)
    def _(step):
        weight_copy(step).wait()

    @pl.loop(1, lat_count)
    def _(step):
        lat_copy(step).wait_send()

    @pl.loop(1, sec_count)
    def _(step):
        sec_copy(step).wait_send()

    @pl.loop(0, sec_count)
    def _(back):
        @pl.loop(1, col_count)
        def _(step):
            col_copy(back, step).wait()


def exchange(sizes, points, table, slots, state, weights, halo):
    fields, width = state.shape
    waves = table.shape[2]
    sec_count, lat_count, col_count = sizes
    groups = sec_count * col_count
    padded = weights.shape[1]
    anywhere = pl.BlockSpec(memory_space=pl.ANY)
    inside = pl.BlockSpec(memory_space=pltpu.VMEM)
    halo_shape = jax.ShapeDtypeStruct(halo.shape, halo.dtype)
    out = pl.pallas_call(
        functools.partial(exchange_kernel, sizes),
        out_shape=[
            jax.ShapeDtypeStruct((groups, lat_count, padded, 2 * fields), jnp.bfloat16),
            jax.ShapeDtypeStruct(weights.shape, jnp.bfloat16),
            halo_shape,
            halo_shape,
        ],
        in_specs=[pl.BlockSpec(memory_space=pltpu.SMEM), inside, inside, inside, anywhere, anywhere],
        out_specs=[anywhere] * 4,
        scratch_shapes=[
            pltpu.VMEM((2, CHUNK, waves), jnp.float32),
            pltpu.VMEM((2 * fields, waves), jnp.float32),
            pltpu.VMEM((lat_count, padded, 2 * fields), jnp.bfloat16),
            pltpu.SemaphoreType.DMA((2,)),
            pltpu.SemaphoreType.DMA((groups,)),
            pltpu.SemaphoreType.DMA((groups,)),
            pltpu.SemaphoreType.DMA((2,)),
            pltpu.SemaphoreType.DMA((2,)),
            pltpu.SemaphoreType.DMA((lat_count,)),
            pltpu.SemaphoreType.DMA((lat_count,)),
            pltpu.SemaphoreType.DMA((sec_count,)),
            pltpu.SemaphoreType.DMA((sec_count,)),
            pltpu.SemaphoreType.DMA((sec_count, col_count)),
            pltpu.SemaphoreType.DMA((sec_count, col_count)),
        ],
        compiler_params=pltpu.CompilerParams(
            vmem_limit_bytes=24 * 2**20, collective_id=0, has_side_effects=True
        ),
        cost_estimate=pl.CostEstimate(
            flops=4 * fields * waves * width, bytes_accessed=8 * 2**20, transcendentals=0
        ),
    )(points, table, slots, state, weights, halo)
    return out


REACH = (-2, -1, 1, 2)


def flux_kernel(sizes, row_ref, out_ref, send_sem, recv_sem):
    sec_count, lat_count, col_count = sizes
    devices = sec_count * lat_count * col_count
    sec, lat, col = (lax.axis_index(name) for name in LINE)
    line = (sec * lat_count + lat) * col_count + col
    places = [place_of((line + devices - step) % devices, lat_count, col_count) for step in REACH]
    barrier = pltpu.get_barrier_semaphore()
    for place in places:
        pl.semaphore_signal(barrier, inc=1, device_id=place, device_id_type=MESH)
    pl.semaphore_wait(barrier, len(REACH))
    copies = [
        pltpu.make_async_remote_copy(
            src_ref=row_ref,
            dst_ref=out_ref.at[k],
            send_sem=send_sem.at[k],
            recv_sem=recv_sem.at[k],
            device_id=place,
            device_id_type=MESH,
        )
        for k, place in enumerate(places)
    ]
    for copy in copies:
        copy.start()
    for copy in copies:
        copy.wait()


def near_rows(sizes, row):
    shape = (8, row.shape[0] // 8)
    out = pl.pallas_call(
        functools.partial(flux_kernel, sizes),
        out_shape=jax.ShapeDtypeStruct((len(REACH),) + shape, row.dtype),
        in_specs=[pl.BlockSpec(memory_space=pltpu.VMEM)],
        out_specs=pl.BlockSpec(memory_space=pltpu.VMEM),
        scratch_shapes=[pltpu.SemaphoreType.DMA((len(REACH),))] * 2,
        compiler_params=pltpu.CompilerParams(
            vmem_limit_bytes=2**20, collective_id=1, has_side_effects=True
        ),
    )(row.reshape(shape))
    return out.reshape(len(REACH), row.shape[0])


def legendre_kernel(degree_ref, slots_ref, weight_ref, coef_ref, out_ref):
    groups, lines, pair, width = coef_ref.shape
    rows = groups * lines
    packed = weight_ref.shape[2]
    degrees = out_ref.shape[1]
    first = degree_ref[0]
    for half in range(pair // 8):
        cut = slice(half * 8, half * 8 + 8)
        held = weight_ref[:, cut, :].astype(jnp.float32).reshape(groups * 8, packed)
        parts = [
            pltpu.roll(held, (packed - q * degrees) % packed, 1)[:, :128] if q else held[:, :128]
            for q in range(lines)
        ]
        values = jnp.concatenate(parts, axis=0).T[:degrees]
        lane_slot = lax.broadcasted_iota(jnp.int32, (degrees, rows * 8), 1) % 8
        coefs = jnp.concatenate(
            [
                coef_ref[:, q, cut, :].astype(jnp.float32).reshape(groups * 8, width)
                for q in range(lines)
            ],
            axis=0,
        ).astype(jnp.bfloat16)
        degree = first + lax.broadcasted_iota(jnp.int32, (degrees, width), 0)
        for s in range(8):
            wave = slots_ref[pl.program_id(0) * pair + half * 8 + s]
            left = jnp.where(lane_slot == s, values, 0.0).astype(jnp.bfloat16)
            summed = jnp.dot(left, coefs, preferred_element_type=jnp.float32)
            out_ref[half * 8 + s] = jnp.where(degree >= wave, summed, 0.0)


def legendre(weights, coefs, slots, first_degree, slot_count, degrees):
    groups, lines, padded, width = coefs.shape
    rows = groups * lines
    return pl.pallas_call(
        legendre_kernel,
        grid=(padded // SLOT_PAD,),
        out_shape=jax.ShapeDtypeStruct((slot_count, degrees, width), jnp.float32),
        in_specs=[
            pl.BlockSpec(memory_space=pltpu.SMEM),
            pl.BlockSpec(memory_space=pltpu.SMEM),
            pl.BlockSpec((groups, SLOT_PAD, weights.shape[2]), lambda i: (0, i, 0)),
            pl.BlockSpec((groups, lines, SLOT_PAD, width), lambda i: (0, 0, i, 0)),
        ],
        out_specs=pl.BlockSpec((SLOT_PAD, degrees, width), lambda i: (i, 0, 0)),
        compiler_params=pltpu.CompilerParams(vmem_limit_bytes=(8 if rows <= 64 else 32) * 2**20),
        cost_estimate=pl.CostEstimate(
            flops=2 * rows * padded * width * degrees * 8,
            bytes_accessed=4 * slot_count * degrees * width + 4 * rows * padded * width,
            transcendentals=0,
        ),
    )(first_degree, slots, weights, coefs)


def split_two(values):
    top = lax.reduce_precision(values, 8, 7)
    return [top.astype(jnp.bfloat16), (values - top).astype(jnp.bfloat16)]


def pick_points(arrays, index):
    length = arrays[0].shape[0]
    tiles = -(-length // 128)
    matrix = jnp.stack(arrays).reshape(len(arrays), tiles, 128)
    chosen = (jnp.arange(tiles, dtype=jnp.int32)[:, None] == index[None, :] // 128).astype(jnp.bfloat16)
    spread = jnp.einsum("kta,tx->kax", matrix, chosen, preferred_element_type=jnp.float32)
    lane = jnp.arange(128, dtype=jnp.int32)[:, None] == index[None, :] % 128
    return jnp.where(lane[None], spread, 0.0).sum(axis=1)


def advance_coupled_model(
    bordered_array,
    meridian_exchange_factor,
    zonal_exchange_factor,
    depthwise_exchange_factor,
    boundary_warming_term,
):
    centre = bordered_array[:, 1:-1]
    meridional = meridian_exchange_factor[1:] * (
        bordered_array[:, 2:] - centre
    ) - meridian_exchange_factor[:-1] * (centre - bordered_array[:, :-2])
    east_flux = zonal_exchange_factor * (jnp.roll(centre, -1, axis=2) - centre)
    zonal_div = east_flux - jnp.roll(east_flux, 1, axis=2)
    vertical_flux = depthwise_exchange_factor * (centre[1:] - centre[:-1])
    zero_layer = jnp.zeros_like(vertical_flux[:1])
    vertical = jnp.concatenate([vertical_flux, zero_layer], 0) - jnp.concatenate(
        [zero_layer, vertical_flux], 0
    )
    forced = jnp.concatenate([boundary_warming_term[None], jnp.zeros_like(centre[1:])], 0)
    return centre + meridional + zonal_div + vertical + forced


def body(
    physical_state,
    parallel_lengths,
    zonal_mode_assignment,
    weighted_associated_polynomials,
    marine_tracer_state,
    lateral_diffusivity,
    depthwise_diffusivity,
    water_indicator,
    overlying_parallel,
    underlying_marine_parallel,
):
    lat_count = lax.axis_size("lat")
    groups = lax.axis_size("sec") * lax.axis_size("col")
    devices = groups * lat_count
    grid_width = physical_state.shape[2]
    strata = physical_state.shape[1] // 4
    slot_count, wave_count, row_count = weighted_associated_polynomials.shape
    block_degrees = wave_count // groups
    padded = -(-slot_count // SLOT_PAD) * SLOT_PAD
    linear_index = (
        lax.axis_index("sec") * lat_count + lax.axis_index("lat")
    ) * lax.axis_size("col") + lax.axis_index("col")
    group_index = lax.axis_index("sec") * lax.axis_size("col") + lax.axis_index("col")
    points = parallel_lengths[0]

    rows = marine_tracer_state.shape[1]
    span = marine_tracer_state.shape[2]
    layers = marine_tracer_state.shape[0]
    relative = overlying_parallel - linear_index
    payload = jnp.concatenate(
        [
            marine_tracer_state,
            lateral_diffusivity[None],
            depthwise_diffusivity[None],
            water_indicator.astype(jnp.float32)[None],
            jnp.broadcast_to(relative.astype(jnp.float32)[:, None], (rows, span))[None],
        ],
        axis=0,
    )
    halo = payload.astype(jnp.bfloat16).reshape((layers + 4) * rows, span)

    send = weighted_associated_polynomials.reshape(slot_count, groups, block_degrees, row_count)
    send = jnp.transpose(send, (1, 0, 3, 2)).reshape(groups, slot_count, row_count * block_degrees)
    lanes = -(-send.shape[2] // 128) * 128
    send = jnp.pad(send, ((0, 0), (0, padded - slot_count), (0, lanes - send.shape[2])))
    slots = zonal_mode_assignment.reshape(lat_count, slot_count)
    slots = jnp.pad(slots, ((0, 0), (0, padded - slot_count)), constant_values=wave_count)
    coefs, weights, before, after = exchange(
        (lax.axis_size("sec"), lat_count, lax.axis_size("col")),
        parallel_lengths,
        angle_tables(points, wave_count, grid_width),
        slots.reshape(-1, 1),
        physical_state[0],
        send,
        halo,
    )
    first, last = linear_index == 0, linear_index == devices - 1
    before = jnp.where(first, jnp.zeros_like(before), before).astype(jnp.float32)
    after = jnp.where(last, jnp.zeros_like(after), after).astype(jnp.float32)
    before = before.reshape(payload.shape)
    after = after.reshape(payload.shape)

    surface = jnp.concatenate([before[0], marine_tracer_state[0], after[0]], axis=0)
    under = underlying_marine_parallel[0] - (linear_index - 1) * rows
    skin = jnp.where(jnp.arange(3 * rows)[:, None] == under, surface, 0.0).sum(axis=0)
    ocean_points = jnp.arange(span, dtype=jnp.int32)
    column = ocean_points * points // span
    sea_column = jnp.minimum(column * span // points, span - 1)
    skin_hi, skin_lo = split_two(skin)
    mapped = pick_points([skin_hi, skin_lo], sea_column)
    bottom = strata - 1
    zonal_wind = physical_state[0, bottom].astype(jnp.float32)
    meridional_wind = physical_state[0, strata + bottom].astype(jnp.float32)
    speed = thermal_transfer_factor * jnp.sqrt(
        zonal_wind * zonal_wind + meridional_wind * meridional_wind + 1.0
    )
    speed_hi, speed_lo = split_two(speed)
    picked = pick_points([speed_hi, speed_lo, physical_state[0, 2 * strata + bottom]], column)
    flux = (picked[0] + picked[1]) * (mapped[0] + mapped[1] - picked[2])
    near = near_rows((lax.axis_size("sec"), lat_count, lax.axis_size("col")), flux)
    flux_near = {0: flux, **{step: near[k] for k, step in enumerate(REACH)}}

    whole = jnp.concatenate([before, payload, after], axis=1)
    thermal = whole[:layers]
    kappa, depth, sea, relative = (whole[layers + k] for k in range(4))
    owner = jnp.arange(3 * rows, dtype=jnp.int32)[:, None] // rows - 1
    target = relative + owner.astype(jnp.float32)
    forcing = jnp.zeros_like(sea)
    for step, row in flux_near.items():
        forcing = jnp.where(target == step, row[None], forcing)
    source = force_coef * sea * forcing
    depthwise = depth * sea
    faces = 0.5 * (kappa[:-1] + kappa[1:]) * sea[:-1] * sea[1:]
    east = 0.5 * (kappa + jnp.roll(kappa, -1, axis=1)) * sea * jnp.roll(sea, -1, axis=1)
    total = 3 * rows
    for iteration in range(OSTEPS):
        a, b = iteration + 1, total - iteration - 1
        thermal = advance_coupled_model(
            thermal, faces[a - 1 : b], east[a:b], depthwise[a:b], source[a:b]
        )

    own_waves = lax.dynamic_slice_in_dim(
        slots.reshape(-1), lax.axis_index("lat") * padded, padded
    )
    first_degree = jnp.reshape(group_index * block_degrees, (1,)).astype(jnp.int32)
    harmonic = legendre(weights, coefs, own_waves, first_degree, slot_count, block_degrees)
    return (jnp.transpose(harmonic, (1, 0, 2)), thermal)


def fast_kernel(
    sizes,
    points_ref,
    over_ref,
    under_ref,
    table_ref,
    slots_ref,
    x_ref,
    weight_ref,
    kappa_ref,
    depth_ref,
    water_ref,
    ocean_ref,
    coef_out,
    weight_out,
    thermal_out,
    msg_ref,
    base_ref,
    xm_ref,
    z_ref,
    coefs_ref,
    mine_ref,
    halo_ref,
    before_ref,
    after_ref,
    plane_ref,
    heat_ref,
    face_ref,
    east_ref,
    down_ref,
    source_ref,
    local_ref,
    flux_ref,
    ocean_sem,
    local_sem,
    weight_send,
    weight_recv,
    halo_send,
    halo_recv,
    flux_send,
    flux_recv,
    lat_send,
    lat_recv,
    direct_send,
    direct_recv,
    diag_send,
    diag_recv,
    chip_send,
    chip_recv,
):
    sec_count, lat_count, col_count = sizes
    groups = sec_count * col_count
    devices = groups * lat_count
    sec, lat, col = (lax.axis_index(name) for name in LINE)
    group = sec * col_count + col
    line = (sec * lat_count + lat) * col_count + col
    rows, layers, span = thermal_out.shape
    following = place_of((line + 1) % devices, lat_count, col_count)
    previous = place_of((line + devices - 1) % devices, lat_count, col_count)
    has_next, has_previous = line < devices - 1, line > 0
    sides = (sec + 1 - 2 * (sec % 2), (sec + 2) % 4)
    corner = 3 - sec

    ocean_copies = [
        pltpu.make_async_copy(ocean_ref.at[:, r, :], heat_ref.at[0, rows + r], ocean_sem.at[r])
        for r in range(rows)
    ]
    for copy in ocean_copies:
        copy.start()

    def group_place(step):
        other = (group + step) % groups
        return other, {"sec": other // col_count, "lat": lat, "col": other % col_count}

    def lat_place(step):
        other = (lat + step) % lat_count
        return other, {"sec": sec, "lat": other, "col": col}

    flux_places = [place_of((line + devices - step) % devices, lat_count, col_count) for step in REACH]
    barrier = pltpu.get_barrier_semaphore()
    for place in flux_places:
        pl.semaphore_signal(barrier, inc=1, device_id=place, device_id_type=MESH)

    @pl.loop(1, groups)
    def _(step):
        pl.semaphore_signal(barrier, inc=1, device_id=group_place(step)[1], device_id_type=MESH)

    @pl.loop(1, lat_count)
    def _(step):
        pl.semaphore_signal(barrier, inc=1, device_id=lat_place(step)[1], device_id_type=MESH)

    def weight_copy(step):
        other, place = group_place(step)
        return pltpu.make_async_remote_copy(
            src_ref=msg_ref.at[other],
            dst_ref=weight_out.at[group],
            send_sem=weight_send.at[step],
            recv_sem=weight_recv.at[step],
            device_id=place,
            device_id_type=MESH,
        )

    def halo_copy(side):
        return pltpu.make_async_remote_copy(
            src_ref=halo_ref,
            dst_ref=(before_ref, after_ref)[side],
            send_sem=halo_send.at[side],
            recv_sem=halo_recv.at[side],
            device_id=(following, previous)[side],
            device_id_type=MESH,
        )

    def flux_copy(k):
        return pltpu.make_async_remote_copy(
            src_ref=flux_ref.at[len(REACH)],
            dst_ref=flux_ref.at[k],
            send_sem=flux_send.at[k],
            recv_sem=flux_recv.at[k],
            device_id=flux_places[k],
            device_id_type=MESH,
        )

    def lat_copy(step):
        other, place = lat_place(step)
        return pltpu.make_async_remote_copy(
            src_ref=mine_ref.at[other],
            dst_ref=coef_out.at[group, lat],
            send_sem=lat_send.at[step],
            recv_sem=lat_recv.at[step],
            device_id=place,
            device_id_type=MESH,
        )

    def direct_copy(side, line_row):
        piece = coef_out.at[group, line_row]
        return pltpu.make_async_remote_copy(
            src_ref=piece,
            dst_ref=piece,
            send_sem=direct_send.at[side, line_row],
            recv_sem=direct_recv.at[side, line_row],
            device_id={"sec": sides[side], "lat": lat, "col": col},
            device_id_type=MESH,
        )

    def diag_copy(side, line_row):
        piece = coef_out.at[sides[side] * col_count + col, line_row]
        return pltpu.make_async_remote_copy(
            src_ref=piece,
            dst_ref=piece,
            send_sem=diag_send.at[line_row],
            recv_sem=diag_recv.at[line_row],
            device_id={"sec": sides[1 - side], "lat": lat, "col": col},
            device_id_type=MESH,
        )

    def chip_copy(which, line_row):
        origin = (sec, sides[0], sides[1], corner)[which]
        piece = coef_out.at[origin * col_count + col, line_row]
        return pltpu.make_async_remote_copy(
            src_ref=piece,
            dst_ref=piece,
            send_sem=chip_send.at[which, line_row],
            recv_sem=chip_recv.at[which, line_row],
            device_id={"sec": sec, "lat": lat, "col": 1 - col},
            device_id_type=MESH,
        )

    band = msg_ref.shape[1]
    degrees = msg_ref.shape[2] // groups
    halves = weight_ref.shape[1] // band
    for g in range(groups):
        for p in range(groups):
            t, h = p // halves, p % halves
            msg_ref[g, :, p * degrees : (p + 1) * degrees] = weight_ref[
                t, h * band : (h + 1) * band, g * degrees : (g + 1) * degrees
            ]

    pl.semaphore_wait(barrier, len(REACH) + groups - 1 + lat_count - 1)

    @pl.loop(1, groups)
    def _(step):
        weight_copy(step).start()

    own_weights = pltpu.make_async_copy(msg_ref.at[group], weight_out.at[group], local_sem.at[0])
    own_weights.start()

    sea = water_ref[...].astype(jnp.float32)
    plane_ref[0:rows] = kappa_ref[...] * sea
    plane_ref[rows : 2 * rows] = depth_ref[...] * sea
    row_index = lax.broadcasted_iota(jnp.int32, (rows, span), 0)
    relative = jnp.zeros((rows, span), jnp.float32)
    for r in range(rows):
        relative = jnp.where(row_index == r, (over_ref[r] - line).astype(jnp.float32), relative)
    plane_ref[2 * rows : 3 * rows] = relative
    plane_ref[3 * rows : 4 * rows] = relative
    halo_ref[rows * layers :] = plane_ref[...].astype(jnp.bfloat16)
    for copy in ocean_copies:
        copy.wait()
    for r in range(0, rows, 2):
        pair = jnp.concatenate([heat_ref[0, rows + r], heat_ref[0, rows + r + 1]], axis=0)
        halo_ref[r * layers : (r + 2) * layers] = pair.astype(jnp.bfloat16)

    @pl.when(has_next)
    def _():
        halo_copy(0).start()

    @pl.when(has_previous)
    def _():
        halo_copy(1).start()

    points = points_ref[0]
    waves = table_ref.shape[2]
    fields = x_ref.shape[0]
    chunks = x_ref.shape[1] // CHUNK
    low_c, low_s = table_ref[0, :LOW], table_ref[1, :LOW]
    for w in range(waves // 128):
        cut = slice(w * 128, w * 128 + 128)
        for b in range(0, CHUNK // LOW, 2):
            real, imag = [], []
            for q in (b, b + 1):
                mid_c = table_ref[0, LOW + q : LOW + q + 1, cut]
                mid_s = table_ref[1, LOW + q : LOW + q + 1, cut]
                real.append(low_c[:, cut] * mid_c - low_s[:, cut] * mid_s)
                imag.append(low_c[:, cut] * mid_s + low_s[:, cut] * mid_c)
            real = jnp.concatenate(real, axis=0).astype(jnp.bfloat16)
            imag = jnp.concatenate(imag, axis=0).astype(jnp.bfloat16)
            base_ref[w, b * LOW : (b + 2) * LOW, :128] = real
            base_ref[w, b * LOW : (b + 2) * LOW, 128:] = imag
    for a in range(chunks):
        position = a * CHUNK + lax.broadcasted_iota(jnp.int32, (fields, CHUNK), 1)
        block = x_ref[:, a * CHUNK : (a + 1) * CHUNK].astype(jnp.float32)
        xm_ref[a * fields : (a + 1) * fields] = jnp.where(position < points, block, 0.0).astype(
            jnp.bfloat16
        )
    top = LOW + CHUNK // LOW
    for w in range(waves // 128):
        cut = slice(w * 128, w * 128 + 128)
        z_ref[...] = jnp.dot(xm_ref[...], base_ref[w], preferred_element_type=jnp.float32)
        real = jnp.zeros((fields, 128), jnp.float32)
        imag = jnp.zeros((fields, 128), jnp.float32)
        for a in range(chunks):
            turn_c = table_ref[0, top + a : top + a + 1, cut]
            turn_s = table_ref[1, top + a : top + a + 1, cut]
            part_r = z_ref[a * fields : (a + 1) * fields, :128]
            part_i = z_ref[a * fields : (a + 1) * fields, 128:]
            real = real + part_r * turn_c - part_i * turn_s
            imag = imag + part_r * turn_s + part_i * turn_c
        wave = w * 128 + lax.broadcasted_iota(jnp.int32, (fields, 128), 1)
        kept = wave < points // 2
        coefs_ref[:fields, cut] = jnp.where(kept, real, 0.0).astype(jnp.bfloat16)
        coefs_ref[fields:, cut] = jnp.where(kept, imag, 0.0).astype(jnp.bfloat16)
    padded = mine_ref.shape[1]

    def fill(other):
        held = slots_ref[pl.ds(pl.multiple_of(other * padded, 16), padded)]
        pick = held == lax.broadcasted_iota(jnp.int32, (padded, waves), 1)
        pick = jnp.where(pick, 1.0, 0.0).astype(jnp.bfloat16)
        mine_ref[other] = lax.dot_general(
            pick, coefs_ref[...], (((1,), (1,)), ((), ())), preferred_element_type=jnp.float32
        ).astype(jnp.bfloat16)

    @pl.loop(1, lat_count)
    def _(step):
        fill((lat + step) % lat_count)
        lat_copy(step).start()

    fill(lat)
    own_coefs = pltpu.make_async_copy(mine_ref.at[lat], coef_out.at[group, lat], local_sem.at[1])
    own_coefs.start()

    def spread_piece(line_row):
        direct_copy(0, line_row).start()
        direct_copy(1, line_row).start()
        chip_copy(0, line_row).start()

    own_coefs.wait()
    spread_piece(lat)

    strata = fields // 4
    bottom = strata - 1
    wide = 512
    shift = span.bit_length() - 1

    def halves_of(value):
        upper = value.astype(jnp.bfloat16).astype(jnp.float32)
        return upper, value - upper

    def columns_of(start):
        place = start + lax.broadcasted_iota(jnp.int32, (1, wide), 1)
        return lax.shift_right_logical(place * points, shift)

    def pick(table, index):
        tiles = table.shape[1]
        one = lax.broadcasted_iota(jnp.int32, (tiles, wide), 0) == lax.shift_right_logical(index, 7)
        one = jnp.where(one, 1.0, 0.0).astype(jnp.bfloat16)
        lane = lax.broadcasted_iota(jnp.int32, (128, wide), 0) == (index & 127)
        spread = jnp.dot(table, one, preferred_element_type=jnp.float32)
        return [
            jnp.sum(jnp.where(lane, spread[k * 128 : (k + 1) * 128], 0.0), axis=0, keepdims=True)
            for k in range(table.shape[0] // 128)
        ]

    def table_of(values):
        tiles = values[0].shape[1] // 128
        return jnp.concatenate([v.reshape(tiles, 128).T for v in values], axis=0).astype(jnp.bfloat16)

    zonal = x_ref[bottom : bottom + 1].astype(jnp.float32)
    meridional = x_ref[strata + bottom : strata + bottom + 1].astype(jnp.float32)
    air = x_ref[2 * strata + bottom : 2 * strata + bottom + 1].astype(jnp.float32)
    speed = thermal_transfer_factor * jnp.sqrt(zonal * zonal + meridional * meridional + 1.0)
    table = table_of([*halves_of(speed), air])

    @pl.loop(0, span // wide)
    def _(k):
        start = pl.multiple_of(k * wide, wide)
        upper, lower, below = pick(table, columns_of(start))
        local_ref[0:1, pl.ds(start, wide)] = upper + lower
        local_ref[1:2, pl.ds(start, wide)] = below

    @pl.when(has_next)
    def _():
        halo_copy(0).wait_send()
        halo_copy(1).wait_recv()

    @pl.when(has_previous)
    def _():
        halo_copy(1).wait_send()
        halo_copy(0).wait_recv()

    @pl.when(jnp.logical_not(has_next))
    def _():
        after_ref[...] = jnp.zeros_like(after_ref)

    @pl.when(jnp.logical_not(has_previous))
    def _():
        before_ref[...] = jnp.zeros_like(before_ref)

    for r in range(0, rows, 2):
        for start, held in ((0, before_ref), (2 * rows, after_ref)):
            pair = held[r * layers : (r + 2) * layers].astype(jnp.float32)
            heat_ref[0, start + r] = pair[:layers]
            heat_ref[0, start + r + 1] = pair[layers:]

    under = under_ref[0] - (line - 1) * rows
    skin = jnp.zeros((1, span), jnp.float32)
    for r in range(3 * rows):
        skin = jnp.where(under == r, heat_ref[0, r, 0:1, :], skin)
    skin_table = table_of(halves_of(skin))
    inverse = 1.0 / jnp.full((1, wide), points, jnp.int32).astype(jnp.float32)

    @pl.loop(0, span // wide)
    def _(k):
        start = pl.multiple_of(k * wide, wide)
        scaled = columns_of(start) << shift
        index = (scaled.astype(jnp.float32) * inverse).astype(jnp.int32)
        rest = scaled - index * points
        index = jnp.where(rest < 0, index - 1, jnp.where(rest >= points, index + 1, index))
        index = jnp.minimum(index, span - 1)
        upper, lower = pick(skin_table, index)
        cut = pl.ds(start, wide)
        flux_ref[len(REACH), 0:1, cut] = local_ref[0:1, cut] * (upper + lower - local_ref[1:2, cut])

    for k in range(len(REACH)):
        flux_copy(k).start()

    @pl.loop(1, lat_count)
    def _(step):
        lat_copy(step).wait_recv()
        spread_piece((lat + lat_count - step) % lat_count)

    edges = [before_ref[rows * layers :].astype(jnp.float32), after_ref[rows * layers :].astype(jnp.float32)]
    centre = plane_ref[...]
    kappa = jnp.concatenate([edges[0][:rows], centre[:rows], edges[1][:rows]], axis=0)
    depth = jnp.concatenate([edges[0][rows : 2 * rows], centre[rows : 2 * rows], edges[1][rows : 2 * rows]], axis=0)
    reach = jnp.concatenate(
        [edges[0][2 * rows : 3 * rows] - 1.0, centre[2 * rows : 3 * rows], edges[1][2 * rows : 3 * rows] + 1.0],
        axis=0,
    )
    total = 3 * rows
    layer = lax.broadcasted_iota(jnp.int32, (layers, span), 0)
    beside = pltpu.roll(kappa, span - 1, 1)
    east = jnp.where((kappa > 0.0) & (beside > 0.0), 0.5 * (kappa + beside), 0.0)
    upper, lower = kappa[:-1], kappa[1:]
    faces = jnp.where((upper > 0.0) & (lower > 0.0), 0.5 * (upper + lower), 0.0)
    for r in range(1, total):
        face_ref[r] = jnp.broadcast_to(faces[r - 1 : r], (layers, span))
    for r in range(1, total - 1):
        east_ref[r] = jnp.broadcast_to(east[r : r + 1], (layers, span))
        down_ref[r] = jnp.where(layer < layers - 1, depth[r : r + 1], 0.0)

    for k in range(len(REACH)):
        flux_copy(k).wait()
    forcing = jnp.zeros_like(kappa)
    for k, step in enumerate(REACH + (0,)):
        forcing = jnp.where(reach == float(step), flux_ref[k], forcing)
    forcing = jnp.where(kappa > 0.0, force_coef * forcing, 0.0)
    for r in range(1, total - 1):
        source_ref[r] = jnp.where(layer == 0, forcing[r : r + 1], 0.0)

    for step in range(OSTEPS):
        held, made = step % 2, (step + 1) % 2

        @pl.loop(step + 1, total - step - 1)
        def _(r):
            mid = heat_ref[held, r]
            flow = face_ref[r + 1] * (heat_ref[held, r + 1] - mid) - face_ref[r] * (mid - heat_ref[held, r - 1])
            lateral = east_ref[r] * (pltpu.roll(mid, span - 1, 1) - mid)
            flow = flow + (lateral - pltpu.roll(lateral, 1, 1))
            sinking = down_ref[r] * (pltpu.roll(mid, layers - 1, 0) - mid)
            flow = flow + (sinking - pltpu.roll(sinking, 1, 0))
            fresh = mid + flow + source_ref[r]
            if step < OSTEPS - 1:
                heat_ref[made, r] = fresh
            else:
                thermal_out[r - rows] = fresh

    @pl.loop(0, lat_count)
    def _(step):
        line_row = (lat + lat_count - step) % lat_count
        direct_copy(0, line_row).wait_recv()

        @pl.when(line_row % 2 == 0)
        def _():
            diag_copy(0, line_row).start()

        chip_copy(1, line_row).start()
        direct_copy(1, line_row).wait_recv()

        @pl.when(line_row % 2 == 1)
        def _():
            diag_copy(1, line_row).start()

        chip_copy(2, line_row).start()

    @pl.loop(0, lat_count)
    def _(step):
        line_row = (lat + lat_count - step) % lat_count
        diag_copy(0, line_row).wait_recv()
        chip_copy(3, line_row).start()

    own_weights.wait()

    @pl.loop(1, lat_count)
    def _(step):
        lat_copy(step).wait_send()

    @pl.loop(0, lat_count)
    def _(line_row):
        direct_copy(0, line_row).wait_send()
        direct_copy(1, line_row).wait_send()
        diag_copy(0, line_row).wait_send()
        for which in range(4):
            chip_copy(which, line_row).wait_send()

    @pl.loop(1, groups)
    def _(step):
        weight_copy(step).wait()

    @pl.loop(0, lat_count)
    def _(line_row):
        for which in range(4):
            chip_copy(which, line_row).wait_recv()


def fast_exchange(sizes, points, over, under, table, slots, state, weights, kappa, depth, water, ocean):
    sec_count, lat_count, col_count = sizes
    groups = sec_count * col_count
    fields, width = state.shape
    waves = table.shape[2]
    layers, rows, span = ocean.shape
    padded = weights.shape[1]
    band = lat_count * padded // groups
    chunks = width // CHUNK
    halo_rows = rows * (layers + 4)
    anywhere = pl.BlockSpec(memory_space=pl.ANY)
    inside = pl.BlockSpec(memory_space=pltpu.VMEM)
    scalar = pl.BlockSpec(memory_space=pltpu.SMEM)
    near = len(REACH)
    dma = pltpu.SemaphoreType.DMA
    return pl.pallas_call(
        functools.partial(fast_kernel, sizes),
        out_shape=[
            jax.ShapeDtypeStruct((groups, lat_count, padded, 2 * fields), jnp.bfloat16),
            jax.ShapeDtypeStruct((groups, band, waves), jnp.bfloat16),
            jax.ShapeDtypeStruct((rows, layers, span), jnp.float32),
        ],
        in_specs=[scalar, scalar, scalar] + [inside] * 7 + [anywhere],
        out_specs=[inside] * 3,
        scratch_shapes=[
            pltpu.VMEM((groups, band, waves), jnp.bfloat16),
            pltpu.VMEM((waves // 128, CHUNK, 256), jnp.bfloat16),
            pltpu.VMEM((chunks * fields, CHUNK), jnp.bfloat16),
            pltpu.VMEM((chunks * fields, 256), jnp.float32),
            pltpu.VMEM((2 * fields, waves), jnp.bfloat16),
            pltpu.VMEM((lat_count, padded, 2 * fields), jnp.bfloat16),
            pltpu.VMEM((halo_rows, span), jnp.bfloat16),
            pltpu.VMEM((halo_rows, span), jnp.bfloat16),
            pltpu.VMEM((halo_rows, span), jnp.bfloat16),
            pltpu.VMEM((4 * rows, span), jnp.float32),
            pltpu.VMEM((2, 3 * rows, layers, span), jnp.float32),
            pltpu.VMEM((3 * rows, layers, span), jnp.float32),
            pltpu.VMEM((3 * rows, layers, span), jnp.float32),
            pltpu.VMEM((3 * rows, layers, span), jnp.float32),
            pltpu.VMEM((3 * rows, layers, span), jnp.float32),
            pltpu.VMEM((2, span), jnp.float32),
            pltpu.VMEM((near + 1, 1, span), jnp.float32),
            dma((rows,)),
            dma((2,)),
            dma((groups,)),
            dma((groups,)),
            dma((2,)),
            dma((2,)),
            dma((near,)),
            dma((near,)),
            dma((lat_count,)),
            dma((lat_count,)),
            dma((2, lat_count)),
            dma((2, lat_count)),
            dma((lat_count,)),
            dma((lat_count,)),
            dma((4, lat_count)),
            dma((4, lat_count)),
        ],
        compiler_params=pltpu.CompilerParams(
            vmem_limit_bytes=48 * 2**20, collective_id=2, has_side_effects=True
        ),
        cost_estimate=pl.CostEstimate(
            flops=4 * fields * waves * width, bytes_accessed=8 * 2**20, transcendentals=0
        ),
    )(points, over, under, table, slots, state, weights, kappa, depth, water, ocean)


def fast_legendre_kernel(
    degree_ref, slots_ref, weight_ref, coef_ref, ocean_ref, out_ref, ocean_out, turned_ref, ocean_sem
):
    groups, lines, _, width = coef_ref.shape
    degrees = out_ref.shape[1]
    rows = ocean_ref.shape[0]
    halves = pl.num_programs(1)
    major, half = pl.program_id(0), pl.program_id(1)
    block = half * pl.num_programs(0) + major
    copies = [
        pltpu.make_async_copy(ocean_ref.at[r], ocean_out.at[:, r, :], ocean_sem.at[r]) for r in range(rows)
    ]

    @pl.when((major == 0) & (half == 0))
    def _():
        for copy in copies:
            copy.start()

    @pl.when(half == 0)
    def _():
        held = weight_ref[:, pl.ds(pl.multiple_of(major * 16, 16), 16), :]
        turned_ref[...] = held.reshape(groups * 16, held.shape[2]).T

    values = jnp.concatenate(
        [
            turned_ref[pl.ds(pl.multiple_of((t * halves + half) * degrees, 16), degrees), :]
            for t in range(lines)
        ],
        axis=1,
    )
    cut = pl.ds(pl.multiple_of(block * 16, 16), 16)
    coefs = jnp.concatenate(
        [coef_ref[:, t, cut, :].reshape(groups * 16, width) for t in range(lines)], axis=0
    )
    odd = lax.broadcasted_iota(jnp.int32, coefs.shape, 0) % 2 == 1
    nothing = jnp.zeros_like(coefs)
    both = jnp.concatenate([jnp.where(odd, nothing, coefs), jnp.where(odd, coefs, nothing)], axis=1)
    lane_pair = lax.broadcasted_iota(jnp.int32, values.shape, 1) % 16 // 2
    left = jnp.concatenate(
        [jnp.where(lane_pair == j, values, jnp.zeros_like(values)) for j in range(8)], axis=0
    )
    summed = jnp.dot(left, both, preferred_element_type=jnp.float32)
    degree = degree_ref[0] + lax.broadcasted_iota(jnp.int32, (degrees, width), 0)
    for s in range(16):
        wave = slots_ref[block * 16 + s]
        part = summed[s // 2 * degrees : (s // 2 + 1) * degrees, s % 2 * width : (s % 2 + 1) * width]
        out_ref[s] = jnp.where(degree >= wave, part, 0.0)

    @pl.when((major == pl.num_programs(0) - 1) & (half == halves - 1))
    def _():
        for copy in copies:
            copy.wait()


def fast_legendre(weights, coefs, ocean, slots, first_degree, slot_count, degrees):
    groups, lines, padded, width = coefs.shape
    band = weights.shape[1]
    rows, layers, span = ocean.shape
    halves = padded // band
    inside = pl.BlockSpec(memory_space=pltpu.VMEM)
    scalar = pl.BlockSpec(memory_space=pltpu.SMEM)
    anywhere = pl.BlockSpec(memory_space=pl.ANY)
    return pl.pallas_call(
        fast_legendre_kernel,
        grid=(band // 16, halves),
        out_shape=[
            jax.ShapeDtypeStruct((slot_count, degrees, width), jnp.float32),
            jax.ShapeDtypeStruct((layers, rows, span), jnp.float32),
        ],
        in_specs=[scalar, scalar, inside, inside, anywhere],
        out_specs=[
            pl.BlockSpec((16, degrees, width), lambda i, h: (h * (band // 16) + i, 0, 0)),
            anywhere,
        ],
        scratch_shapes=[
            pltpu.VMEM((weights.shape[2], groups * 16), jnp.bfloat16),
            pltpu.SemaphoreType.DMA((rows,)),
        ],
        compiler_params=pltpu.CompilerParams(vmem_limit_bytes=24 * 2**20),
        cost_estimate=pl.CostEstimate(
            flops=2 * groups * lines * padded * width * degrees * 8,
            bytes_accessed=4 * slot_count * degrees * width,
            transcendentals=0,
        ),
    )(first_degree, slots, weights, coefs, ocean)


def fast_body(
    physical_state,
    parallel_lengths,
    zonal_mode_assignment,
    weighted_associated_polynomials,
    marine_tracer_state,
    lateral_diffusivity,
    depthwise_diffusivity,
    water_indicator,
    overlying_parallel,
    underlying_marine_parallel,
):
    sizes = tuple(lax.axis_size(name) for name in LINE)
    sec_count, lat_count, col_count = sizes
    groups = sec_count * col_count
    grid_width = physical_state.shape[2]
    slot_count, wave_count, _ = weighted_associated_polynomials.shape
    block_degrees = wave_count // groups
    padded = -(-slot_count // 32) * 32
    group_index = lax.axis_index("sec") * col_count + lax.axis_index("col")
    weights = jnp.transpose(weighted_associated_polynomials, (2, 0, 1))
    weights = jnp.pad(weights, ((0, 0), (0, padded - slot_count), (0, 0)))
    slots = zonal_mode_assignment.reshape(lat_count, slot_count)
    slots = jnp.pad(slots, ((0, 0), (0, padded - slot_count)), constant_values=wave_count)
    coefs, packed, ocean = fast_exchange(
        sizes,
        parallel_lengths,
        overlying_parallel,
        underlying_marine_parallel,
        angle_tables(parallel_lengths[0], wave_count, grid_width),
        slots.reshape(-1, 1),
        physical_state[0],
        weights,
        lateral_diffusivity,
        depthwise_diffusivity,
        water_indicator,
        marine_tracer_state,
    )
    own_waves = lax.dynamic_slice_in_dim(slots.reshape(-1), lax.axis_index("lat") * padded, padded)
    first_degree = jnp.reshape(group_index * block_degrees, (1,)).astype(jnp.int32)
    harmonic, thermal = fast_legendre(
        packed, coefs, ocean, own_waves, first_degree, slot_count, block_degrees
    )
    return (jnp.transpose(harmonic, (1, 0, 2)), thermal)


def compact(mesh):
    return mesh.shape["sec"] == 4 and mesh.shape["lat"] == 4 and mesh.shape["col"] == 2


def solution(mesh):
    return jax.shard_map(
        fast_body if compact(mesh) else body,
        mesh=mesh,
        in_specs=(
            P(LINE, None, None),
            P(LINE),
            P(),
            P("lat", None, GROUP),
            P(None, LINE, None),
            P(LINE, None),
            P(LINE, None),
            P(LINE, None),
            P(LINE),
            P(LINE),
        ),
        out_specs=(P(GROUP, "lat", None), P(None, LINE, None)),
        check_vma=False,
    )
```

```python
import functools

import jax
import jax.numpy as jnp
from jax import lax
from jax.experimental import pallas as pl
from jax.experimental.pallas import tpu as pltpu
from jax.sharding import PartitionSpec as P

OSTEPS = 4
LOW = 8
CHUNK = 256
SLOT_PAD = 16

two_pi = 6.283185307179586
thermal_transfer_factor = 0.8
force_coef = 0.1

GROUP = ("sec", "col")
LINE = ("sec", "lat", "col")


def angle_tables(points, wave_count, grid_width):
    low = jnp.arange(LOW, dtype=jnp.float32)
    mid = jnp.arange(CHUNK // LOW, dtype=jnp.float32) * LOW
    high = jnp.arange(grid_width // CHUNK, dtype=jnp.float32) * CHUNK
    place = jnp.concatenate([low, mid, high])
    count = points.astype(jnp.float32)
    product = place[:, None] * jnp.arange(wave_count, dtype=jnp.float32)[None, :]
    residue = product - jnp.round(product / count) * count
    angle = residue * (jnp.float32(two_pi) / count)
    scale = jnp.where(jnp.arange(place.shape[0]) >= LOW + CHUNK // LOW, 1.0 / jnp.sqrt(count), 1.0)
    return jnp.stack([jnp.cos(angle), -jnp.sin(angle)]) * scale[None, :, None]


MESH = pl.DeviceIdType.MESH


def place_of(index, lat_count, col_count):
    return {
        "sec": index // (lat_count * col_count),
        "lat": index // col_count % lat_count,
        "col": index % col_count,
    }


def exchange_kernel(
    sizes,
    points_ref,
    table_ref,
    slots_ref,
    x_ref,
    weight_ref,
    *refs,
):
    sec_count, lat_count, col_count = sizes
    halo, coef_out, weight_out, before, after = refs[:5]
    (base_ref, acc_ref, mine_ref, local_sem, weight_send, weight_recv, halo_send, halo_recv,
     lat_send, lat_recv, sec_send, sec_recv, col_send, col_recv) = refs[5:]
    groups = sec_count * col_count
    devices = groups * lat_count
    sec, lat, col = (lax.axis_index(name) for name in LINE)
    group = sec * col_count + col
    line = (sec * lat_count + lat) * col_count + col
    following = place_of((line + 1) % devices, lat_count, col_count)
    previous = place_of((line + devices - 1) % devices, lat_count, col_count)

    def group_place(step):
        other = (group + step) % groups
        return other, {"sec": other // col_count, "lat": lat, "col": other % col_count}

    def lat_place(step):
        other = (lat + step) % lat_count
        return other, {"sec": sec, "lat": other, "col": col}

    barrier = pltpu.get_barrier_semaphore()
    for place in (following, previous):
        pl.semaphore_signal(barrier, inc=1, device_id=place, device_id_type=MESH)

    @pl.loop(1, groups)
    def _(step):
        pl.semaphore_signal(barrier, inc=1, device_id=group_place(step)[1], device_id_type=MESH)

    @pl.loop(1, lat_count)
    def _(step):
        pl.semaphore_signal(barrier, inc=1, device_id=lat_place(step)[1], device_id_type=MESH)

    pl.semaphore_wait(barrier, groups + lat_count)

    def weight_copy(step):
        other, place = group_place(step)
        return pltpu.make_async_remote_copy(
            src_ref=weight_ref.at[other],
            dst_ref=weight_out.at[group],
            send_sem=weight_send.at[step],
            recv_sem=weight_recv.at[step],
            device_id=place,
            device_id_type=MESH,
        )

    def halo_copy(side):
        return pltpu.make_async_remote_copy(
            src_ref=halo,
            dst_ref=(before, after)[side],
            send_sem=halo_send.at[side],
            recv_sem=halo_recv.at[side],
            device_id=(following, previous)[side],
            device_id_type=MESH,
        )

    has_next, has_previous = line < devices - 1, line > 0

    def lat_copy(step):
        other, place = lat_place(step)
        return pltpu.make_async_remote_copy(
            src_ref=mine_ref.at[other],
            dst_ref=coef_out.at[group, lat],
            send_sem=lat_send.at[step],
            recv_sem=lat_recv.at[step],
            device_id=place,
            device_id_type=MESH,
        )

    def sec_copy(step):
        return pltpu.make_async_remote_copy(
            src_ref=coef_out.at[group],
            dst_ref=coef_out.at[group],
            send_sem=sec_send.at[step],
            recv_sem=sec_recv.at[step],
            device_id={"sec": (sec + step) % sec_count, "lat": lat, "col": col},
            device_id_type=MESH,
        )

    def col_copy(back, step):
        block = (sec + sec_count - back) % sec_count * col_count + col
        return pltpu.make_async_remote_copy(
            src_ref=coef_out.at[block],
            dst_ref=coef_out.at[block],
            send_sem=col_send.at[back, step],
            recv_sem=col_recv.at[back, step],
            device_id={"sec": sec, "lat": lat, "col": (col + step) % col_count},
            device_id_type=MESH,
        )

    own_weights = pltpu.make_async_copy(weight_ref.at[group], weight_out.at[group], local_sem.at[0])
    own_weights.start()

    @pl.loop(1, groups)
    def _(step):
        weight_copy(step).start()

    @pl.when(has_next)
    def _():
        halo_copy(0).start()

    @pl.when(has_previous)
    def _():
        halo_copy(1).start()

    points = points_ref[0]
    waves = table_ref.shape[2]
    fields = x_ref.shape[0]
    chunks = x_ref.shape[1] // CHUNK
    low_c, low_s = table_ref[0, :LOW], table_ref[1, :LOW]
    for b in range(CHUNK // LOW):
        mid_c = table_ref[0, LOW + b : LOW + b + 1]
        mid_s = table_ref[1, LOW + b : LOW + b + 1]
        base_ref[0, b * LOW : (b + 1) * LOW] = low_c * mid_c - low_s * mid_s
        base_ref[1, b * LOW : (b + 1) * LOW] = low_c * mid_s + low_s * mid_c
    acc_ref[...] = jnp.zeros_like(acc_ref)
    top = LOW + CHUNK // LOW

    @pl.loop(0, chunks)
    def _(a):
        start = pl.multiple_of(a * CHUNK, CHUNK)
        position = start + lax.broadcasted_iota(jnp.int32, (fields, CHUNK), 1)
        block = x_ref[:, pl.ds(start, CHUNK)].astype(jnp.float32)
        block = jnp.where(position < points, block, 0.0).astype(jnp.bfloat16)
        high_c = table_ref[0, pl.ds(top + a, 1)]
        high_s = table_ref[1, pl.ds(top + a, 1)]
        for w in range(0, waves, 128):
            cut = slice(w, w + 128)
            base_c, base_s = base_ref[0, :, cut], base_ref[1, :, cut]
            turn_c, turn_s = high_c[:, cut], high_s[:, cut]
            real = (base_c * turn_c - base_s * turn_s).astype(jnp.bfloat16)
            imag = (base_c * turn_s + base_s * turn_c).astype(jnp.bfloat16)
            both = jnp.concatenate([real, imag], axis=1)
            part = jnp.dot(block, both, preferred_element_type=jnp.float32)
            acc_ref[:fields, cut] += part[:, :128]
            acc_ref[fields:, cut] += part[:, 128:]

    wave = lax.broadcasted_iota(jnp.int32, acc_ref.shape, 1)
    coefs = jnp.where(wave < points // 2, acc_ref[...], 0.0).astype(jnp.bfloat16)
    padded = mine_ref.shape[1]

    def fill(other):
        held = slots_ref[pl.ds(pl.multiple_of(other * padded, 16), padded)]
        pick = held == lax.broadcasted_iota(jnp.int32, (padded, waves), 1)
        pick = jnp.where(pick, 1.0, 0.0).astype(jnp.bfloat16)
        mine_ref[other] = lax.dot_general(
            pick, coefs, (((1,), (1,)), ((), ())), preferred_element_type=jnp.float32
        ).astype(jnp.bfloat16)

    @pl.loop(1, lat_count)
    def _(step):
        fill((lat + step) % lat_count)
        lat_copy(step).start()

    fill(lat)
    own_coefs = pltpu.make_async_copy(mine_ref.at[lat], coef_out.at[group, lat], local_sem.at[1])
    own_coefs.start()
    own_coefs.wait()

    @pl.loop(1, lat_count)
    def _(step):
        lat_copy(step).wait_recv()

    @pl.loop(1, sec_count)
    def _(step):
        sec_copy(step).start()

    @pl.loop(1, col_count)
    def _(step):
        col_copy(0, step).start()

    @pl.loop(1, sec_count)
    def _(back):
        sec_copy(back).wait_recv()

        @pl.loop(1, col_count)
        def _(step):
            col_copy(back, step).start()

    @pl.when(has_next)
    def _():
        halo_copy(0).wait_send()
        halo_copy(1).wait_recv()

    @pl.when(has_previous)
    def _():
        halo_copy(1).wait_send()
        halo_copy(0).wait_recv()

    own_weights.wait()

    @pl.loop(1, groups)
    def _(step):
        weight_copy(step).wait()

    @pl.loop(1, lat_count)
    def _(step):
        lat_copy(step).wait_send()

    @pl.loop(1, sec_count)
    def _(step):
        sec_copy(step).wait_send()

    @pl.loop(0, sec_count)
    def _(back):
        @pl.loop(1, col_count)
        def _(step):
            col_copy(back, step).wait()


def exchange(sizes, points, table, slots, state, weights, halo):
    fields, width = state.shape
    waves = table.shape[2]
    sec_count, lat_count, col_count = sizes
    groups = sec_count * col_count
    padded = weights.shape[1]
    anywhere = pl.BlockSpec(memory_space=pl.ANY)
    inside = pl.BlockSpec(memory_space=pltpu.VMEM)
    halo_shape = jax.ShapeDtypeStruct(halo.shape, halo.dtype)
    out = pl.pallas_call(
        functools.partial(exchange_kernel, sizes),
        out_shape=[
            jax.ShapeDtypeStruct((groups, lat_count, padded, 2 * fields), jnp.bfloat16),
            jax.ShapeDtypeStruct(weights.shape, jnp.bfloat16),
            halo_shape,
            halo_shape,
        ],
        in_specs=[pl.BlockSpec(memory_space=pltpu.SMEM), inside, inside, inside, anywhere, anywhere],
        out_specs=[anywhere] * 4,
        scratch_shapes=[
            pltpu.VMEM((2, CHUNK, waves), jnp.float32),
            pltpu.VMEM((2 * fields, waves), jnp.float32),
            pltpu.VMEM((lat_count, padded, 2 * fields), jnp.bfloat16),
            pltpu.SemaphoreType.DMA((2,)),
            pltpu.SemaphoreType.DMA((groups,)),
            pltpu.SemaphoreType.DMA((groups,)),
            pltpu.SemaphoreType.DMA((2,)),
            pltpu.SemaphoreType.DMA((2,)),
            pltpu.SemaphoreType.DMA((lat_count,)),
            pltpu.SemaphoreType.DMA((lat_count,)),
            pltpu.SemaphoreType.DMA((sec_count,)),
            pltpu.SemaphoreType.DMA((sec_count,)),
            pltpu.SemaphoreType.DMA((sec_count, col_count)),
            pltpu.SemaphoreType.DMA((sec_count, col_count)),
        ],
        compiler_params=pltpu.CompilerParams(
            vmem_limit_bytes=24 * 2**20, collective_id=0, has_side_effects=True
        ),
        cost_estimate=pl.CostEstimate(
            flops=4 * fields * waves * width, bytes_accessed=8 * 2**20, transcendentals=0
        ),
    )(points, table, slots, state, weights, halo)
    return out


REACH = (-2, -1, 1, 2)


def flux_kernel(sizes, row_ref, out_ref, send_sem, recv_sem):
    sec_count, lat_count, col_count = sizes
    devices = sec_count * lat_count * col_count
    sec, lat, col = (lax.axis_index(name) for name in LINE)
    line = (sec * lat_count + lat) * col_count + col
    places = [place_of((line + devices - step) % devices, lat_count, col_count) for step in REACH]
    barrier = pltpu.get_barrier_semaphore()
    for place in places:
        pl.semaphore_signal(barrier, inc=1, device_id=place, device_id_type=MESH)
    pl.semaphore_wait(barrier, len(REACH))
    copies = [
        pltpu.make_async_remote_copy(
            src_ref=row_ref,
            dst_ref=out_ref.at[k],
            send_sem=send_sem.at[k],
            recv_sem=recv_sem.at[k],
            device_id=place,
            device_id_type=MESH,
        )
        for k, place in enumerate(places)
    ]
    for copy in copies:
        copy.start()
    for copy in copies:
        copy.wait()


def near_rows(sizes, row):
    shape = (8, row.shape[0] // 8)
    out = pl.pallas_call(
        functools.partial(flux_kernel, sizes),
        out_shape=jax.ShapeDtypeStruct((len(REACH),) + shape, row.dtype),
        in_specs=[pl.BlockSpec(memory_space=pltpu.VMEM)],
        out_specs=pl.BlockSpec(memory_space=pltpu.VMEM),
        scratch_shapes=[pltpu.SemaphoreType.DMA((len(REACH),))] * 2,
        compiler_params=pltpu.CompilerParams(
            vmem_limit_bytes=2**20, collective_id=1, has_side_effects=True
        ),
    )(row.reshape(shape))
    return out.reshape(len(REACH), row.shape[0])


def legendre_kernel(degree_ref, slots_ref, weight_ref, coef_ref, out_ref):
    groups, lines, pair, width = coef_ref.shape
    rows = groups * lines
    packed = weight_ref.shape[2]
    degrees = out_ref.shape[1]
    first = degree_ref[0]
    for half in range(pair // 8):
        cut = slice(half * 8, half * 8 + 8)
        held = weight_ref[:, cut, :].astype(jnp.float32).reshape(groups * 8, packed)
        parts = [
            pltpu.roll(held, (packed - q * degrees) % packed, 1)[:, :128] if q else held[:, :128]
            for q in range(lines)
        ]
        values = jnp.concatenate(parts, axis=0).T[:degrees]
        lane_slot = lax.broadcasted_iota(jnp.int32, (degrees, rows * 8), 1) % 8
        coefs = jnp.concatenate(
            [
                coef_ref[:, q, cut, :].astype(jnp.float32).reshape(groups * 8, width)
                for q in range(lines)
            ],
            axis=0,
        ).astype(jnp.bfloat16)
        degree = first + lax.broadcasted_iota(jnp.int32, (degrees, width), 0)
        for s in range(8):
            wave = slots_ref[pl.program_id(0) * pair + half * 8 + s]
            left = jnp.where(lane_slot == s, values, 0.0).astype(jnp.bfloat16)
            summed = jnp.dot(left, coefs, preferred_element_type=jnp.float32)
            out_ref[half * 8 + s] = jnp.where(degree >= wave, summed, 0.0)


def legendre(weights, coefs, slots, first_degree, slot_count, degrees):
    groups, lines, padded, width = coefs.shape
    rows = groups * lines
    return pl.pallas_call(
        legendre_kernel,
        grid=(padded // SLOT_PAD,),
        out_shape=jax.ShapeDtypeStruct((slot_count, degrees, width), jnp.float32),
        in_specs=[
            pl.BlockSpec(memory_space=pltpu.SMEM),
            pl.BlockSpec(memory_space=pltpu.SMEM),
            pl.BlockSpec((groups, SLOT_PAD, weights.shape[2]), lambda i: (0, i, 0)),
            pl.BlockSpec((groups, lines, SLOT_PAD, width), lambda i: (0, 0, i, 0)),
        ],
        out_specs=pl.BlockSpec((SLOT_PAD, degrees, width), lambda i: (i, 0, 0)),
        compiler_params=pltpu.CompilerParams(vmem_limit_bytes=(8 if rows <= 64 else 32) * 2**20),
        cost_estimate=pl.CostEstimate(
            flops=2 * rows * padded * width * degrees * 8,
            bytes_accessed=4 * slot_count * degrees * width + 4 * rows * padded * width,
            transcendentals=0,
        ),
    )(first_degree, slots, weights, coefs)


def split_two(values):
    top = lax.reduce_precision(values, 8, 7)
    return [top.astype(jnp.bfloat16), (values - top).astype(jnp.bfloat16)]


def pick_points(arrays, index):
    length = arrays[0].shape[0]
    tiles = -(-length // 128)
    matrix = jnp.stack(arrays).reshape(len(arrays), tiles, 128)
    chosen = (jnp.arange(tiles, dtype=jnp.int32)[:, None] == index[None, :] // 128).astype(jnp.bfloat16)
    spread = jnp.einsum("kta,tx->kax", matrix, chosen, preferred_element_type=jnp.float32)
    lane = jnp.arange(128, dtype=jnp.int32)[:, None] == index[None, :] % 128
    return jnp.where(lane[None], spread, 0.0).sum(axis=1)


def advance_coupled_model(
    bordered_array,
    meridian_exchange_factor,
    zonal_exchange_factor,
    depthwise_exchange_factor,
    boundary_warming_term,
):
    centre = bordered_array[:, 1:-1]
    meridional = meridian_exchange_factor[1:] * (
        bordered_array[:, 2:] - centre
    ) - meridian_exchange_factor[:-1] * (centre - bordered_array[:, :-2])
    east_flux = zonal_exchange_factor * (jnp.roll(centre, -1, axis=2) - centre)
    zonal_div = east_flux - jnp.roll(east_flux, 1, axis=2)
    vertical_flux = depthwise_exchange_factor * (centre[1:] - centre[:-1])
    zero_layer = jnp.zeros_like(vertical_flux[:1])
    vertical = jnp.concatenate([vertical_flux, zero_layer], 0) - jnp.concatenate(
        [zero_layer, vertical_flux], 0
    )
    forced = jnp.concatenate([boundary_warming_term[None], jnp.zeros_like(centre[1:])], 0)
    return centre + meridional + zonal_div + vertical + forced


def body(
    physical_state,
    parallel_lengths,
    zonal_mode_assignment,
    weighted_associated_polynomials,
    marine_tracer_state,
    lateral_diffusivity,
    depthwise_diffusivity,
    water_indicator,
    overlying_parallel,
    underlying_marine_parallel,
):
    lat_count = lax.axis_size("lat")
    groups = lax.axis_size("sec") * lax.axis_size("col")
    devices = groups * lat_count
    grid_width = physical_state.shape[2]
    strata = physical_state.shape[1] // 4
    slot_count, wave_count, row_count = weighted_associated_polynomials.shape
    block_degrees = wave_count // groups
    padded = -(-slot_count // SLOT_PAD) * SLOT_PAD
    linear_index = (
        lax.axis_index("sec") * lat_count + lax.axis_index("lat")
    ) * lax.axis_size("col") + lax.axis_index("col")
    group_index = lax.axis_index("sec") * lax.axis_size("col") + lax.axis_index("col")
    points = parallel_lengths[0]

    rows = marine_tracer_state.shape[1]
    span = marine_tracer_state.shape[2]
    layers = marine_tracer_state.shape[0]
    relative = overlying_parallel - linear_index
    payload = jnp.concatenate(
        [
            marine_tracer_state,
            lateral_diffusivity[None],
            depthwise_diffusivity[None],
            water_indicator.astype(jnp.float32)[None],
            jnp.broadcast_to(relative.astype(jnp.float32)[:, None], (rows, span))[None],
        ],
        axis=0,
    )
    halo = payload.astype(jnp.bfloat16).reshape((layers + 4) * rows, span)

    send = weighted_associated_polynomials.reshape(slot_count, groups, block_degrees, row_count)
    send = jnp.transpose(send, (1, 0, 3, 2)).reshape(groups, slot_count, row_count * block_degrees)
    lanes = -(-send.shape[2] // 128) * 128
    send = jnp.pad(send, ((0, 0), (0, padded - slot_count), (0, lanes - send.shape[2])))
    slots = zonal_mode_assignment.reshape(lat_count, slot_count)
    slots = jnp.pad(slots, ((0, 0), (0, padded - slot_count)), constant_values=wave_count)
    coefs, weights, before, after = exchange(
        (lax.axis_size("sec"), lat_count, lax.axis_size("col")),
        parallel_lengths,
        angle_tables(points, wave_count, grid_width),
        slots.reshape(-1, 1),
        physical_state[0],
        send,
        halo,
    )
    first, last = linear_index == 0, linear_index == devices - 1
    before = jnp.where(first, jnp.zeros_like(before), before).astype(jnp.float32)
    after = jnp.where(last, jnp.zeros_like(after), after).astype(jnp.float32)
    before = before.reshape(payload.shape)
    after = after.reshape(payload.shape)

    surface = jnp.concatenate([before[0], marine_tracer_state[0], after[0]], axis=0)
    under = underlying_marine_parallel[0] - (linear_index - 1) * rows
    skin = jnp.where(jnp.arange(3 * rows)[:, None] == under, surface, 0.0).sum(axis=0)
    ocean_points = jnp.arange(span, dtype=jnp.int32)
    column = ocean_points * points // span
    sea_column = jnp.minimum(column * span // points, span - 1)
    skin_hi, skin_lo = split_two(skin)
    mapped = pick_points([skin_hi, skin_lo], sea_column)
    bottom = strata - 1
    zonal_wind = physical_state[0, bottom].astype(jnp.float32)
    meridional_wind = physical_state[0, strata + bottom].astype(jnp.float32)
    speed = thermal_transfer_factor * jnp.sqrt(
        zonal_wind * zonal_wind + meridional_wind * meridional_wind + 1.0
    )
    speed_hi, speed_lo = split_two(speed)
    picked = pick_points([speed_hi, speed_lo, physical_state[0, 2 * strata + bottom]], column)
    flux = (picked[0] + picked[1]) * (mapped[0] + mapped[1] - picked[2])
    near = near_rows((lax.axis_size("sec"), lat_count, lax.axis_size("col")), flux)
    flux_near = {0: flux, **{step: near[k] for k, step in enumerate(REACH)}}

    whole = jnp.concatenate([before, payload, after], axis=1)
    thermal = whole[:layers]
    kappa, depth, sea, relative = (whole[layers + k] for k in range(4))
    owner = jnp.arange(3 * rows, dtype=jnp.int32)[:, None] // rows - 1
    target = relative + owner.astype(jnp.float32)
    forcing = jnp.zeros_like(sea)
    for step, row in flux_near.items():
        forcing = jnp.where(target == step, row[None], forcing)
    source = force_coef * sea * forcing
    depthwise = depth * sea
    faces = 0.5 * (kappa[:-1] + kappa[1:]) * sea[:-1] * sea[1:]
    east = 0.5 * (kappa + jnp.roll(kappa, -1, axis=1)) * sea * jnp.roll(sea, -1, axis=1)
    total = 3 * rows
    for iteration in range(OSTEPS):
        a, b = iteration + 1, total - iteration - 1
        thermal = advance_coupled_model(
            thermal, faces[a - 1 : b], east[a:b], depthwise[a:b], source[a:b]
        )

    own_waves = lax.dynamic_slice_in_dim(
        slots.reshape(-1), lax.axis_index("lat") * padded, padded
    )
    first_degree = jnp.reshape(group_index * block_degrees, (1,)).astype(jnp.int32)
    harmonic = legendre(weights, coefs, own_waves, first_degree, slot_count, block_degrees)
    return (jnp.transpose(harmonic, (1, 0, 2)), thermal)


def fast_kernel(
    sizes,
    points_hbm,
    over_hbm,
    under_hbm,
    slots_hbm,
    x_hbm,
    weight_ref,
    kappa_ref,
    depth_ref,
    water_ref,
    ocean_ref,
    coef_out,
    weight_out,
    thermal_out,
    points_ref,
    over_ref,
    under_ref,
    slots_ref,
    x_ref,
    table_ref,
    strip_ref,
    msg_ref,
    base_ref,
    xm_ref,
    z_ref,
    coefs_ref,
    mine_ref,
    halo_ref,
    before_ref,
    after_ref,
    plane_ref,
    heat_ref,
    face_ref,
    east_ref,
    down_ref,
    source_ref,
    local_ref,
    flux_ref,
    input_sem,
    ocean_sem,
    local_sem,
    weight_send,
    weight_recv,
    halo_send,
    halo_recv,
    flux_send,
    flux_recv,
    lat_send,
    lat_recv,
    direct_send,
    direct_recv,
    diag_send,
    diag_recv,
    chip_send,
    chip_recv,
):
    sec_count, lat_count, col_count = sizes
    groups = sec_count * col_count
    devices = groups * lat_count
    sec, lat, col = (lax.axis_index(name) for name in LINE)
    group = sec * col_count + col
    line = (sec * lat_count + lat) * col_count + col
    rows, layers, span = thermal_out.shape
    following = place_of((line + 1) % devices, lat_count, col_count)
    previous = place_of((line + devices - 1) % devices, lat_count, col_count)
    has_next, has_previous = line < devices - 1, line > 0
    sides = (sec + 1 - 2 * (sec % 2), (sec + 2) % 4)
    corner = 3 - sec

    ocean_copies = [
        pltpu.make_async_copy(ocean_ref.at[:, r, :], heat_ref.at[0, rows + r], ocean_sem.at[r])
        for r in range(rows)
    ]
    inputs = [
        pltpu.make_async_copy(source, target, input_sem.at[k])
        for k, (source, target) in enumerate(
            (
                (points_hbm, points_ref),
                (over_hbm, over_ref),
                (under_hbm, under_ref),
                (slots_hbm, slots_ref),
                (x_hbm, x_ref),
            )
        )
    ]
    for copy in ocean_copies + inputs:
        copy.start()

    def group_place(step):
        other = (group + step) % groups
        return other, {"sec": other // col_count, "lat": lat, "col": other % col_count}

    def lat_place(step):
        other = (lat + step) % lat_count
        return other, {"sec": sec, "lat": other, "col": col}

    flux_places = [place_of((line + devices - step) % devices, lat_count, col_count) for step in REACH]
    barrier = pltpu.get_barrier_semaphore()
    for place in flux_places:
        pl.semaphore_signal(barrier, inc=1, device_id=place, device_id_type=MESH)

    @pl.loop(1, groups)
    def _(step):
        pl.semaphore_signal(barrier, inc=1, device_id=group_place(step)[1], device_id_type=MESH)

    @pl.loop(1, lat_count)
    def _(step):
        pl.semaphore_signal(barrier, inc=1, device_id=lat_place(step)[1], device_id_type=MESH)

    def weight_copy(step):
        other, place = group_place(step)
        return pltpu.make_async_remote_copy(
            src_ref=msg_ref.at[other],
            dst_ref=weight_out.at[group],
            send_sem=weight_send.at[step],
            recv_sem=weight_recv.at[step],
            device_id=place,
            device_id_type=MESH,
        )

    def halo_copy(side):
        return pltpu.make_async_remote_copy(
            src_ref=halo_ref,
            dst_ref=(before_ref, after_ref)[side],
            send_sem=halo_send.at[side],
            recv_sem=halo_recv.at[side],
            device_id=(following, previous)[side],
            device_id_type=MESH,
        )

    def flux_copy(k):
        return pltpu.make_async_remote_copy(
            src_ref=flux_ref.at[len(REACH)],
            dst_ref=flux_ref.at[k],
            send_sem=flux_send.at[k],
            recv_sem=flux_recv.at[k],
            device_id=flux_places[k],
            device_id_type=MESH,
        )

    def lat_copy(step):
        other, place = lat_place(step)
        return pltpu.make_async_remote_copy(
            src_ref=mine_ref.at[other],
            dst_ref=coef_out.at[group, lat],
            send_sem=lat_send.at[step],
            recv_sem=lat_recv.at[step],
            device_id=place,
            device_id_type=MESH,
        )

    def direct_copy(side, line_row):
        piece = coef_out.at[group, line_row]
        return pltpu.make_async_remote_copy(
            src_ref=piece,
            dst_ref=piece,
            send_sem=direct_send.at[side, line_row],
            recv_sem=direct_recv.at[side, line_row],
            device_id={"sec": sides[side], "lat": lat, "col": col},
            device_id_type=MESH,
        )

    def diag_copy(side, line_row):
        piece = coef_out.at[sides[side] * col_count + col, line_row]
        return pltpu.make_async_remote_copy(
            src_ref=piece,
            dst_ref=piece,
            send_sem=diag_send.at[line_row],
            recv_sem=diag_recv.at[line_row],
            device_id={"sec": sides[1 - side], "lat": lat, "col": col},
            device_id_type=MESH,
        )

    def chip_copy(which, line_row):
        origin = (sec, sides[0], sides[1], corner)[which]
        piece = coef_out.at[origin * col_count + col, line_row]
        return pltpu.make_async_remote_copy(
            src_ref=piece,
            dst_ref=piece,
            send_sem=chip_send.at[which, line_row],
            recv_sem=chip_recv.at[which, line_row],
            device_id={"sec": sec, "lat": lat, "col": 1 - col},
            device_id_type=MESH,
        )

    band = msg_ref.shape[1]
    degrees = msg_ref.shape[2] // groups
    halves = weight_ref.shape[1] // band
    for g in range(groups):
        for p in range(groups):
            t, h = p // halves, p % halves
            msg_ref[g, :, p * degrees : (p + 1) * degrees] = weight_ref[
                t, h * band : (h + 1) * band, g * degrees : (g + 1) * degrees
            ]

    pl.semaphore_wait(barrier, len(REACH) + groups - 1 + lat_count - 1)

    @pl.loop(1, groups)
    def _(step):
        weight_copy(step).start()

    own_weights = pltpu.make_async_copy(msg_ref.at[group], weight_out.at[group], local_sem.at[0])
    own_weights.start()

    for copy in inputs[:-1] + ocean_copies:
        copy.wait()
    sea = water_ref[...].astype(jnp.float32)
    plane_ref[:rows] = kappa_ref[...] * sea
    plane_ref[rows:] = depth_ref[...] * sea
    deep = rows * layers
    part = span // 2
    for side in range(2):
        cut = slice(side * part, side * part + part)
        for r in range(0, rows, 2):
            pair = jnp.concatenate(
                [heat_ref[0, rows + r, :, cut], heat_ref[0, rows + r + 1, :, cut]], axis=0
            )
            first = side * deep + r * layers
            halo_ref[first : first + 2 * layers] = pair.astype(jnp.bfloat16)
    halo_ref[2 * deep :] = jnp.concatenate(
        [plane_ref[:, :part], plane_ref[:, part:]], axis=0
    ).astype(jnp.bfloat16)

    @pl.when(has_next)
    def _():
        halo_copy(0).start()

    @pl.when(has_previous)
    def _():
        halo_copy(1).start()

    points = points_ref[0]
    waves = table_ref.shape[2]
    fields = x_ref.shape[0]
    chunks = x_ref.shape[1] // CHUNK
    top = LOW + CHUNK // LOW
    shape = table_ref.shape[1:]
    place = lax.broadcasted_iota(jnp.int32, shape, 0)
    place = jnp.where(
        place < LOW, place, jnp.where(place < top, (place - LOW) * LOW, (place - top) * CHUNK)
    )
    product = place.astype(jnp.float32) * lax.broadcasted_iota(jnp.int32, shape, 1).astype(jnp.float32)
    count = jnp.full(shape, points, jnp.int32).astype(jnp.float32)
    angle = (product - jnp.round(product / count) * count) * (two_pi / count)
    scale = jnp.where(lax.broadcasted_iota(jnp.int32, shape, 0) >= top, 1.0 / jnp.sqrt(count), 1.0)
    table_ref[0] = jnp.cos(angle) * scale
    table_ref[1] = -jnp.sin(angle) * scale
    low_c, low_s = table_ref[0, :LOW], table_ref[1, :LOW]
    for w in range(waves // 128):
        cut = slice(w * 128, w * 128 + 128)
        for b in range(0, CHUNK // LOW, 2):
            real, imag = [], []
            for q in (b, b + 1):
                mid_c = table_ref[0, LOW + q : LOW + q + 1, cut]
                mid_s = table_ref[1, LOW + q : LOW + q + 1, cut]
                real.append(low_c[:, cut] * mid_c - low_s[:, cut] * mid_s)
                imag.append(low_c[:, cut] * mid_s + low_s[:, cut] * mid_c)
            real = jnp.concatenate(real, axis=0).astype(jnp.bfloat16)
            imag = jnp.concatenate(imag, axis=0).astype(jnp.bfloat16)
            base_ref[w, b * LOW : (b + 2) * LOW, :128] = real
            base_ref[w, b * LOW : (b + 2) * LOW, 128:] = imag
    inputs[-1].wait()
    for a in range(chunks):
        position = a * CHUNK + lax.broadcasted_iota(jnp.int32, (fields, CHUNK), 1)
        block = x_ref[:, a * CHUNK : (a + 1) * CHUNK].astype(jnp.float32)
        xm_ref[a * fields : (a + 1) * fields] = jnp.where(position < points, block, 0.0).astype(
            jnp.bfloat16
        )
    for w in range(waves // 128):
        cut = slice(w * 128, w * 128 + 128)
        z_ref[...] = jnp.dot(xm_ref[...], base_ref[w], preferred_element_type=jnp.float32)
        real = jnp.zeros((fields, 128), jnp.float32)
        imag = jnp.zeros((fields, 128), jnp.float32)
        for a in range(chunks):
            turn_c = table_ref[0, top + a : top + a + 1, cut]
            turn_s = table_ref[1, top + a : top + a + 1, cut]
            part_r = z_ref[a * fields : (a + 1) * fields, :128]
            part_i = z_ref[a * fields : (a + 1) * fields, 128:]
            real = real + part_r * turn_c - part_i * turn_s
            imag = imag + part_r * turn_s + part_i * turn_c
        wave = w * 128 + lax.broadcasted_iota(jnp.int32, (fields, 128), 1)
        kept = wave < points // 2
        coefs_ref[:fields, cut] = jnp.where(kept, real, 0.0).astype(jnp.bfloat16)
        coefs_ref[fields:, cut] = jnp.where(kept, imag, 0.0).astype(jnp.bfloat16)
    padded = mine_ref.shape[1]

    slot_total = slots_ref.shape[0]
    slot_count = slot_total // lat_count
    ring = strip_ref.shape[1]
    lanes = -(-padded // 128) * 128
    strip_ref[...] = jnp.full_like(strip_ref, waves)
    strip_ref[0:1, :slot_total] = slots_ref[...].reshape(1, slot_total)

    def fill(other):
        held = pltpu.roll(strip_ref[...], ring - other * slot_count, 1)[0:1, :lanes]
        held = jnp.where(lax.broadcasted_iota(jnp.int32, (1, lanes), 1) < slot_count, held, waves)
        pick = held == lax.broadcasted_iota(jnp.int32, (waves, lanes), 0)
        pick = jnp.where(pick, 1.0, 0.0).astype(jnp.bfloat16)
        chosen = jnp.dot(coefs_ref[...], pick, preferred_element_type=jnp.float32)
        mine_ref[other] = chosen.T[:padded].astype(jnp.bfloat16)

    @pl.loop(1, lat_count)
    def _(step):
        fill((lat + step) % lat_count)
        lat_copy(step).start()

    fill(lat)
    own_coefs = pltpu.make_async_copy(mine_ref.at[lat], coef_out.at[group, lat], local_sem.at[1])
    own_coefs.start()

    def spread_piece(line_row):
        direct_copy(0, line_row).start()
        direct_copy(1, line_row).start()
        chip_copy(0, line_row).start()

    own_coefs.wait()
    spread_piece(lat)

    strata = fields // 4
    bottom = strata - 1
    wide = 512
    shift = span.bit_length() - 1

    def halves_of(value):
        upper = value.astype(jnp.bfloat16).astype(jnp.float32)
        return upper, value - upper

    def columns_of(start):
        place = start + lax.broadcasted_iota(jnp.int32, (1, wide), 1)
        return lax.shift_right_logical(place * points, shift)

    def pick(table, index):
        tiles = table.shape[1]
        one = lax.broadcasted_iota(jnp.int32, (tiles, wide), 0) == lax.shift_right_logical(index, 7)
        one = jnp.where(one, 1.0, 0.0).astype(jnp.bfloat16)
        lane = lax.broadcasted_iota(jnp.int32, (128, wide), 0) == (index & 127)
        spread = jnp.dot(table, one, preferred_element_type=jnp.float32)
        return [
            jnp.sum(jnp.where(lane, spread[k * 128 : (k + 1) * 128], 0.0), axis=0, keepdims=True)
            for k in range(table.shape[0] // 128)
        ]

    def table_of(values):
        tiles = values[0].shape[1] // 128
        return jnp.concatenate([v.reshape(tiles, 128).T for v in values], axis=0).astype(jnp.bfloat16)

    zonal = x_ref[bottom : bottom + 1].astype(jnp.float32)
    meridional = x_ref[strata + bottom : strata + bottom + 1].astype(jnp.float32)
    air = x_ref[2 * strata + bottom : 2 * strata + bottom + 1].astype(jnp.float32)
    speed = thermal_transfer_factor * jnp.sqrt(zonal * zonal + meridional * meridional + 1.0)
    table = table_of([*halves_of(speed), air])

    @pl.loop(0, span // wide)
    def _(k):
        start = pl.multiple_of(k * wide, wide)
        upper, lower, below = pick(table, columns_of(start))
        local_ref[0:1, pl.ds(start, wide)] = upper + lower
        local_ref[1:2, pl.ds(start, wide)] = below

    @pl.when(has_next)
    def _():
        halo_copy(0).wait_send()
        halo_copy(1).wait_recv()

    @pl.when(has_previous)
    def _():
        halo_copy(1).wait_send()
        halo_copy(0).wait_recv()

    @pl.when(jnp.logical_not(has_next))
    def _():
        after_ref[...] = jnp.zeros_like(after_ref)

    @pl.when(jnp.logical_not(has_previous))
    def _():
        before_ref[...] = jnp.zeros_like(before_ref)

    for start, held in ((0, before_ref), (2 * rows, after_ref)):
        for side in range(2):
            for r in range(0, rows, 2):
                first = side * deep + r * layers
                pair = held[first : first + 2 * layers].astype(jnp.float32)
                cut = slice(side * part, side * part + part)
                heat_ref[0, start + r, :, cut] = pair[:layers]
                heat_ref[0, start + r + 1, :, cut] = pair[layers:]

    under = under_ref[0] - (line - 1) * rows
    skin = jnp.zeros((1, span), jnp.float32)
    for r in range(3 * rows):
        skin = jnp.where(under == r, heat_ref[0, r, 0:1, :], skin)
    skin_table = table_of(halves_of(skin))
    inverse = 1.0 / jnp.full((1, wide), points, jnp.int32).astype(jnp.float32)

    @pl.loop(0, span // wide)
    def _(k):
        start = pl.multiple_of(k * wide, wide)
        scaled = columns_of(start) << shift
        index = (scaled.astype(jnp.float32) * inverse).astype(jnp.int32)
        rest = scaled - index * points
        index = jnp.where(rest < 0, index - 1, jnp.where(rest >= points, index + 1, index))
        index = jnp.minimum(index, span - 1)
        upper, lower = pick(skin_table, index)
        cut = pl.ds(start, wide)
        flux_ref[len(REACH), 0:1, cut] = local_ref[0:1, cut] * (upper + lower - local_ref[1:2, cut])

    lane = lax.broadcasted_iota(jnp.int32, (1, 128), 1)
    relative = jnp.zeros((1, 128), jnp.float32)
    for r in range(rows):
        relative = jnp.where(lane == r, (over_ref[r] - line).astype(jnp.float32), relative)
    flux_ref[len(REACH), 0:1, span:] = relative
    for k in range(len(REACH)):
        flux_copy(k).start()

    @pl.loop(1, lat_count)
    def _(step):
        lat_copy(step).wait_recv()
        spread_piece((lat + lat_count - step) % lat_count)

    edges = []
    for held in (before_ref, after_ref):
        coarse = held[2 * deep :].astype(jnp.float32)
        edges.append(jnp.concatenate([coarse[: 2 * rows], coarse[2 * rows :]], axis=1))
    kappa = jnp.concatenate([edges[0][:rows], plane_ref[:rows], edges[1][:rows]], axis=0)
    depth = jnp.concatenate([edges[0][rows:], plane_ref[rows:], edges[1][rows:]], axis=0)
    total = 3 * rows
    layer = lax.broadcasted_iota(jnp.int32, (layers, span), 0)
    beside = pltpu.roll(kappa, span - 1, 1)
    east = jnp.where((kappa > 0.0) & (beside > 0.0), 0.5 * (kappa + beside), 0.0)
    upper, lower = kappa[:-1], kappa[1:]
    faces = jnp.where((upper > 0.0) & (lower > 0.0), 0.5 * (upper + lower), 0.0)
    for r in range(1, total):
        face_ref[r] = jnp.broadcast_to(faces[r - 1 : r], (layers, span))
    for r in range(1, total - 1):
        east_ref[r] = jnp.broadcast_to(east[r : r + 1], (layers, span))
        down_ref[r] = jnp.where(layer < layers - 1, depth[r : r + 1], 0.0)

    for k in range(len(REACH)):
        flux_copy(k).wait()
    near = REACH + (0,)
    for r in range(1, total - 1):
        owner = r // rows - 1
        target = flux_ref[near.index(owner), 0:1, span + r % rows : span + r % rows + 1] + float(owner)
        row = jnp.zeros((1, span), jnp.float32)
        for k, step in enumerate(near):
            row = jnp.where(target == float(step), flux_ref[k, 0:1, :span], row)
        row = jnp.where(kappa[r : r + 1] > 0.0, force_coef * row, 0.0)
        source_ref[r] = jnp.where(layer == 0, row, 0.0)

    def ocean_step(step):
        held, made = step % 2, (step + 1) % 2

        @pl.loop(step + 1, total - step - 1)
        def _(r):
            mid = heat_ref[held, r]
            flow = face_ref[r + 1] * (heat_ref[held, r + 1] - mid) - face_ref[r] * (mid - heat_ref[held, r - 1])
            lateral = east_ref[r] * (pltpu.roll(mid, span - 1, 1) - mid)
            flow = flow + (lateral - pltpu.roll(lateral, 1, 1))
            sinking = down_ref[r] * (pltpu.roll(mid, layers - 1, 0) - mid)
            flow = flow + (sinking - pltpu.roll(sinking, 1, 0))
            fresh = mid + flow + source_ref[r]
            if step < OSTEPS - 1:
                heat_ref[made, r] = fresh
            else:
                thermal_out[r - rows] = fresh

    ocean_step(0)
    ocean_step(1)

    @pl.loop(0, lat_count)
    def _(step):
        line_row = (lat + lat_count - step) % lat_count
        direct_copy(0, line_row).wait_recv()

        @pl.when(line_row % 2 == 0)
        def _():
            diag_copy(0, line_row).start()

        chip_copy(1, line_row).start()
        direct_copy(1, line_row).wait_recv()

        @pl.when(line_row % 2 == 1)
        def _():
            diag_copy(1, line_row).start()

        chip_copy(2, line_row).start()

    ocean_step(2)
    ocean_step(3)

    @pl.loop(0, lat_count)
    def _(step):
        line_row = (lat + lat_count - step) % lat_count
        diag_copy(0, line_row).wait_recv()
        chip_copy(3, line_row).start()

    own_weights.wait()

    @pl.loop(1, lat_count)
    def _(step):
        lat_copy(step).wait_send()

    @pl.loop(0, lat_count)
    def _(line_row):
        direct_copy(0, line_row).wait_send()
        direct_copy(1, line_row).wait_send()
        diag_copy(0, line_row).wait_send()
        for which in range(4):
            chip_copy(which, line_row).wait_send()

    @pl.loop(1, groups)
    def _(step):
        weight_copy(step).wait()

    @pl.loop(0, lat_count)
    def _(line_row):
        for which in range(4):
            chip_copy(which, line_row).wait_recv()


def fast_exchange(sizes, points, over, under, slots, state, weights, kappa, depth, water, ocean):
    sec_count, lat_count, col_count = sizes
    groups = sec_count * col_count
    fields, width = state.shape
    waves = weights.shape[2]
    table_rows = -(-(LOW + CHUNK // LOW + width // CHUNK) // 8) * 8
    layers, rows, span = ocean.shape
    padded = weights.shape[1]
    band = lat_count * padded // groups
    chunks = width // CHUNK
    halo_rows = 2 * rows * (layers + 2)
    inside = pl.BlockSpec(memory_space=pltpu.VMEM)
    outside = pl.BlockSpec(memory_space=pl.ANY)
    near = len(REACH)
    dma = pltpu.SemaphoreType.DMA
    return pl.pallas_call(
        functools.partial(fast_kernel, sizes),
        out_shape=[
            jax.ShapeDtypeStruct((groups, lat_count, padded, 2 * fields), jnp.bfloat16),
            jax.ShapeDtypeStruct((groups, band, waves), jnp.bfloat16),
            jax.ShapeDtypeStruct((rows, layers, span), jnp.float32),
        ],
        in_specs=[outside] * 5 + [inside] * 4 + [outside],
        out_specs=[inside] * 3,
        scratch_shapes=[
            pltpu.SMEM(points.shape, jnp.int32),
            pltpu.SMEM(over.shape, jnp.int32),
            pltpu.SMEM(under.shape, jnp.int32),
            pltpu.VMEM(slots.shape, jnp.int32),
            pltpu.VMEM(state.shape, state.dtype),
            pltpu.VMEM((2, table_rows, waves), jnp.float32),
            pltpu.VMEM((8, -(-(slots.shape[0] + 256) // 128) * 128), jnp.int32),
            pltpu.VMEM((groups, band, waves), jnp.bfloat16),
            pltpu.VMEM((waves // 128, CHUNK, 256), jnp.bfloat16),
            pltpu.VMEM((chunks * fields, CHUNK), jnp.bfloat16),
            pltpu.VMEM((chunks * fields, 256), jnp.float32),
            pltpu.VMEM((2 * fields, waves), jnp.bfloat16),
            pltpu.VMEM((lat_count, padded, 2 * fields), jnp.bfloat16),
            pltpu.VMEM((halo_rows, span // 2), jnp.bfloat16),
            pltpu.VMEM((halo_rows, span // 2), jnp.bfloat16),
            pltpu.VMEM((halo_rows, span // 2), jnp.bfloat16),
            pltpu.VMEM((2 * rows, span), jnp.float32),
            pltpu.VMEM((2, 3 * rows, layers, span), jnp.float32),
            pltpu.VMEM((3 * rows, layers, span), jnp.float32),
            pltpu.VMEM((3 * rows, layers, span), jnp.float32),
            pltpu.VMEM((3 * rows, layers, span), jnp.float32),
            pltpu.VMEM((3 * rows, layers, span), jnp.float32),
            pltpu.VMEM((2, span), jnp.float32),
            pltpu.VMEM((near + 1, 1, span + 128), jnp.float32),
            dma((5,)),
            dma((rows,)),
            dma((2,)),
            dma((groups,)),
            dma((groups,)),
            dma((2,)),
            dma((2,)),
            dma((near,)),
            dma((near,)),
            dma((lat_count,)),
            dma((lat_count,)),
            dma((2, lat_count)),
            dma((2, lat_count)),
            dma((lat_count,)),
            dma((lat_count,)),
            dma((4, lat_count)),
            dma((4, lat_count)),
        ],
        compiler_params=pltpu.CompilerParams(
            vmem_limit_bytes=28 * 2**20, collective_id=2, has_side_effects=True
        ),
        cost_estimate=pl.CostEstimate(
            flops=4 * fields * waves * width, bytes_accessed=8 * 2**20, transcendentals=0
        ),
    )(points, over, under, slots, state, weights, kappa, depth, water, ocean)


def fast_legendre_kernel(
    col_count,
    slots_hbm,
    weight_ref,
    coef_ref,
    ocean_ref,
    out_ref,
    ocean_out,
    slots_ref,
    turned_ref,
    made_ref,
    made_sem,
    ocean_sem,
    slots_sem,
):
    groups, lines, padded, width = coef_ref.shape
    slot_count, degrees, _ = out_ref.shape
    rows = ocean_ref.shape[0]
    blocks = padded // 16
    rest = slot_count - (blocks - 1) * 16
    halves = padded // weight_ref.shape[1]
    majors = blocks // halves
    ocean_copies = [
        pltpu.make_async_copy(ocean_ref.at[r], ocean_out.at[:, r, :], ocean_sem.at[r]) for r in range(rows)
    ]
    slots_copy = pltpu.make_async_copy(slots_hbm, slots_ref, slots_sem)
    slots_copy.start()
    for copy in ocean_copies:
        copy.start()
    first_slot = lax.axis_index("lat") * slot_count
    last_slot = slots_ref.shape[0] - 1
    first_degree = (lax.axis_index("sec") * col_count + lax.axis_index("col")) * degrees

    def made_copy(block, count):
        cut = pl.ds(block * 16, count)
        return pltpu.make_async_copy(made_ref.at[cut], out_ref.at[cut], made_sem.at[block])

    degree = first_degree + lax.broadcasted_iota(jnp.int32, (degrees, width), 0)
    odd = lax.broadcasted_iota(jnp.int32, (lines * groups * 16, width), 0) % 2 == 1
    lane_pair = lax.broadcasted_iota(jnp.int32, (degrees, lines * groups * 16), 1) % 16 // 2

    slots_copy.wait()

    @pl.loop(0, majors)
    def _(major):
        held = weight_ref[:, pl.ds(pl.multiple_of(major * 16, 16), 16), :]
        turned_ref[...] = held.reshape(groups * 16, held.shape[2]).T
        for half in range(halves):
            block = half * majors + major
            values = jnp.concatenate(
                [
                    turned_ref[(t * halves + half) * degrees : (t * halves + half + 1) * degrees, :]
                    for t in range(lines)
                ],
                axis=1,
            )
            cut = pl.ds(pl.multiple_of(block * 16, 16), 16)
            coefs = jnp.concatenate(
                [coef_ref[:, t, cut, :].reshape(groups * 16, width) for t in range(lines)], axis=0
            )
            nothing = jnp.zeros_like(coefs)
            both = jnp.concatenate(
                [jnp.where(odd, nothing, coefs), jnp.where(odd, coefs, nothing)], axis=1
            )
            left = jnp.concatenate(
                [jnp.where(lane_pair == j, values, jnp.zeros_like(values)) for j in range(8)], axis=0
            )
            summed = jnp.dot(left, both, preferred_element_type=jnp.float32)
            for s in range(16):
                wave = slots_ref[jnp.minimum(first_slot + block * 16 + s, last_slot)]
                part = summed[
                    s // 2 * degrees : (s // 2 + 1) * degrees, s % 2 * width : (s % 2 + 1) * width
                ]
                made_ref[block * 16 + s] = jnp.where(degree >= wave, part, 0.0)

            @pl.when(block < blocks - 1)
            def _():
                made_copy(block, 16).start()

            @pl.when(block == blocks - 1)
            def _():
                made_copy(block, rest).start()

    @pl.loop(0, blocks - 1)
    def _(block):
        made_copy(block, 16).wait()

    made_copy(blocks - 1, rest).wait()
    for copy in ocean_copies:
        copy.wait()


def fast_legendre(col_count, weights, coefs, ocean, slots, slot_count, degrees):
    groups, lines, padded, width = coefs.shape
    rows, layers, span = ocean.shape
    inside = pl.BlockSpec(memory_space=pltpu.VMEM)
    outside = pl.BlockSpec(memory_space=pl.ANY)
    anywhere = pl.BlockSpec(memory_space=pl.ANY)
    return pl.pallas_call(
        functools.partial(fast_legendre_kernel, col_count),
        out_shape=[
            jax.ShapeDtypeStruct((slot_count, degrees, width), jnp.float32),
            jax.ShapeDtypeStruct((layers, rows, span), jnp.float32),
        ],
        in_specs=[outside, inside, inside, inside],
        out_specs=[anywhere, anywhere],
        scratch_shapes=[
            pltpu.SMEM(slots.shape, jnp.int32),
            pltpu.VMEM((weights.shape[2], groups * 16), jnp.bfloat16),
            pltpu.VMEM((padded, degrees, width), jnp.float32),
            pltpu.SemaphoreType.DMA((padded // 16,)),
            pltpu.SemaphoreType.DMA((rows,)),
            pltpu.SemaphoreType.DMA,
        ],
        compiler_params=pltpu.CompilerParams(vmem_limit_bytes=32 * 2**20),
        cost_estimate=pl.CostEstimate(
            flops=2 * groups * lines * padded * width * degrees * 8,
            bytes_accessed=4 * slot_count * degrees * width,
            transcendentals=0,
        ),
    )(slots, weights, coefs, ocean)


def fast_body(
    physical_state,
    parallel_lengths,
    zonal_mode_assignment,
    weighted_associated_polynomials,
    marine_tracer_state,
    lateral_diffusivity,
    depthwise_diffusivity,
    water_indicator,
    overlying_parallel,
    underlying_marine_parallel,
):
    sizes = tuple(lax.axis_size(name) for name in LINE)
    sec_count, lat_count, col_count = sizes
    groups = sec_count * col_count
    slot_count, wave_count, _ = weighted_associated_polynomials.shape
    block_degrees = wave_count // groups
    padded = -(-slot_count // 32) * 32
    weights = jnp.transpose(weighted_associated_polynomials, (2, 0, 1))
    weights = jnp.pad(weights, ((0, 0), (0, padded - slot_count), (0, 0)))
    coefs, packed, ocean = fast_exchange(
        sizes,
        parallel_lengths,
        overlying_parallel,
        underlying_marine_parallel,
        zonal_mode_assignment,
        physical_state[0],
        weights,
        lateral_diffusivity,
        depthwise_diffusivity,
        water_indicator,
        marine_tracer_state,
    )
    harmonic, thermal = fast_legendre(
        col_count, packed, coefs, ocean, zonal_mode_assignment, slot_count, block_degrees
    )
    return (jnp.transpose(harmonic, (1, 0, 2)), thermal)


def compact(mesh):
    return mesh.shape["sec"] == 4 and mesh.shape["lat"] == 4 and mesh.shape["col"] == 2


def solution(mesh):
    return jax.shard_map(
        fast_body if compact(mesh) else body,
        mesh=mesh,
        in_specs=(
            P(LINE, None, None),
            P(LINE),
            P(),
            P("lat", None, GROUP),
            P(None, LINE, None),
            P(LINE, None),
            P(LINE, None),
            P(LINE, None),
            P(LINE),
            P(LINE),
        ),
        out_specs=(P(GROUP, "lat", None), P(None, LINE, None)),
        check_vma=False,
    )
```

```python
import functools

import jax
import jax.numpy as jnp
from jax import lax
from jax.experimental import pallas as pl
from jax.experimental.pallas import tpu as pltpu
from jax.sharding import PartitionSpec as P

OSTEPS = 4
LOW = 8
CHUNK = 256
SLOT_PAD = 16

two_pi = 6.283185307179586
thermal_transfer_factor = 0.8
force_coef = 0.1

GROUP = ("sec", "col")
LINE = ("sec", "lat", "col")


def angle_tables(points, wave_count, grid_width):
    low = jnp.arange(LOW, dtype=jnp.float32)
    mid = jnp.arange(CHUNK // LOW, dtype=jnp.float32) * LOW
    high = jnp.arange(grid_width // CHUNK, dtype=jnp.float32) * CHUNK
    place = jnp.concatenate([low, mid, high])
    count = points.astype(jnp.float32)
    product = place[:, None] * jnp.arange(wave_count, dtype=jnp.float32)[None, :]
    residue = product - jnp.round(product / count) * count
    angle = residue * (jnp.float32(two_pi) / count)
    scale = jnp.where(jnp.arange(place.shape[0]) >= LOW + CHUNK // LOW, 1.0 / jnp.sqrt(count), 1.0)
    return jnp.stack([jnp.cos(angle), -jnp.sin(angle)]) * scale[None, :, None]


MESH = pl.DeviceIdType.MESH


def place_of(index, lat_count, col_count):
    return {
        "sec": index // (lat_count * col_count),
        "lat": index // col_count % lat_count,
        "col": index % col_count,
    }


def exchange_kernel(
    sizes,
    points_ref,
    table_ref,
    slots_ref,
    x_ref,
    weight_ref,
    *refs,
):
    sec_count, lat_count, col_count = sizes
    halo, coef_out, weight_out, before, after = refs[:5]
    (base_ref, acc_ref, mine_ref, local_sem, weight_send, weight_recv, halo_send, halo_recv,
     lat_send, lat_recv, sec_send, sec_recv, col_send, col_recv) = refs[5:]
    groups = sec_count * col_count
    devices = groups * lat_count
    sec, lat, col = (lax.axis_index(name) for name in LINE)
    group = sec * col_count + col
    line = (sec * lat_count + lat) * col_count + col
    following = place_of((line + 1) % devices, lat_count, col_count)
    previous = place_of((line + devices - 1) % devices, lat_count, col_count)

    def group_place(step):
        other = (group + step) % groups
        return other, {"sec": other // col_count, "lat": lat, "col": other % col_count}

    def lat_place(step):
        other = (lat + step) % lat_count
        return other, {"sec": sec, "lat": other, "col": col}

    barrier = pltpu.get_barrier_semaphore()
    for place in (following, previous):
        pl.semaphore_signal(barrier, inc=1, device_id=place, device_id_type=MESH)

    @pl.loop(1, groups)
    def _(step):
        pl.semaphore_signal(barrier, inc=1, device_id=group_place(step)[1], device_id_type=MESH)

    @pl.loop(1, lat_count)
    def _(step):
        pl.semaphore_signal(barrier, inc=1, device_id=lat_place(step)[1], device_id_type=MESH)

    pl.semaphore_wait(barrier, groups + lat_count)

    def weight_copy(step):
        other, place = group_place(step)
        return pltpu.make_async_remote_copy(
            src_ref=weight_ref.at[other],
            dst_ref=weight_out.at[group],
            send_sem=weight_send.at[step],
            recv_sem=weight_recv.at[step],
            device_id=place,
            device_id_type=MESH,
        )

    def halo_copy(side):
        return pltpu.make_async_remote_copy(
            src_ref=halo,
            dst_ref=(before, after)[side],
            send_sem=halo_send.at[side],
            recv_sem=halo_recv.at[side],
            device_id=(following, previous)[side],
            device_id_type=MESH,
        )

    has_next, has_previous = line < devices - 1, line > 0

    def lat_copy(step):
        other, place = lat_place(step)
        return pltpu.make_async_remote_copy(
            src_ref=mine_ref.at[other],
            dst_ref=coef_out.at[group, lat],
            send_sem=lat_send.at[step],
            recv_sem=lat_recv.at[step],
            device_id=place,
            device_id_type=MESH,
        )

    def sec_copy(step):
        return pltpu.make_async_remote_copy(
            src_ref=coef_out.at[group],
            dst_ref=coef_out.at[group],
            send_sem=sec_send.at[step],
            recv_sem=sec_recv.at[step],
            device_id={"sec": (sec + step) % sec_count, "lat": lat, "col": col},
            device_id_type=MESH,
        )

    def col_copy(back, step):
        block = (sec + sec_count - back) % sec_count * col_count + col
        return pltpu.make_async_remote_copy(
            src_ref=coef_out.at[block],
            dst_ref=coef_out.at[block],
            send_sem=col_send.at[back, step],
            recv_sem=col_recv.at[back, step],
            device_id={"sec": sec, "lat": lat, "col": (col + step) % col_count},
            device_id_type=MESH,
        )

    own_weights = pltpu.make_async_copy(weight_ref.at[group], weight_out.at[group], local_sem.at[0])
    own_weights.start()

    @pl.loop(1, groups)
    def _(step):
        weight_copy(step).start()

    @pl.when(has_next)
    def _():
        halo_copy(0).start()

    @pl.when(has_previous)
    def _():
        halo_copy(1).start()

    points = points_ref[0]
    waves = table_ref.shape[2]
    fields = x_ref.shape[0]
    chunks = x_ref.shape[1] // CHUNK
    low_c, low_s = table_ref[0, :LOW], table_ref[1, :LOW]
    for b in range(CHUNK // LOW):
        mid_c = table_ref[0, LOW + b : LOW + b + 1]
        mid_s = table_ref[1, LOW + b : LOW + b + 1]
        base_ref[0, b * LOW : (b + 1) * LOW] = low_c * mid_c - low_s * mid_s
        base_ref[1, b * LOW : (b + 1) * LOW] = low_c * mid_s + low_s * mid_c
    acc_ref[...] = jnp.zeros_like(acc_ref)
    top = LOW + CHUNK // LOW

    @pl.loop(0, chunks)
    def _(a):
        start = pl.multiple_of(a * CHUNK, CHUNK)
        position = start + lax.broadcasted_iota(jnp.int32, (fields, CHUNK), 1)
        block = x_ref[:, pl.ds(start, CHUNK)].astype(jnp.float32)
        block = jnp.where(position < points, block, 0.0).astype(jnp.bfloat16)
        high_c = table_ref[0, pl.ds(top + a, 1)]
        high_s = table_ref[1, pl.ds(top + a, 1)]
        for w in range(0, waves, 128):
            cut = slice(w, w + 128)
            base_c, base_s = base_ref[0, :, cut], base_ref[1, :, cut]
            turn_c, turn_s = high_c[:, cut], high_s[:, cut]
            real = (base_c * turn_c - base_s * turn_s).astype(jnp.bfloat16)
            imag = (base_c * turn_s + base_s * turn_c).astype(jnp.bfloat16)
            both = jnp.concatenate([real, imag], axis=1)
            part = jnp.dot(block, both, preferred_element_type=jnp.float32)
            acc_ref[:fields, cut] += part[:, :128]
            acc_ref[fields:, cut] += part[:, 128:]

    wave = lax.broadcasted_iota(jnp.int32, acc_ref.shape, 1)
    coefs = jnp.where(wave < points // 2, acc_ref[...], 0.0).astype(jnp.bfloat16)
    padded = mine_ref.shape[1]

    def fill(other):
        held = slots_ref[pl.ds(pl.multiple_of(other * padded, 16), padded)]
        pick = held == lax.broadcasted_iota(jnp.int32, (padded, waves), 1)
        pick = jnp.where(pick, 1.0, 0.0).astype(jnp.bfloat16)
        mine_ref[other] = lax.dot_general(
            pick, coefs, (((1,), (1,)), ((), ())), preferred_element_type=jnp.float32
        ).astype(jnp.bfloat16)

    @pl.loop(1, lat_count)
    def _(step):
        fill((lat + step) % lat_count)
        lat_copy(step).start()

    fill(lat)
    own_coefs = pltpu.make_async_copy(mine_ref.at[lat], coef_out.at[group, lat], local_sem.at[1])
    own_coefs.start()
    own_coefs.wait()

    @pl.loop(1, lat_count)
    def _(step):
        lat_copy(step).wait_recv()

    @pl.loop(1, sec_count)
    def _(step):
        sec_copy(step).start()

    @pl.loop(1, col_count)
    def _(step):
        col_copy(0, step).start()

    @pl.loop(1, sec_count)
    def _(back):
        sec_copy(back).wait_recv()

        @pl.loop(1, col_count)
        def _(step):
            col_copy(back, step).start()

    @pl.when(has_next)
    def _():
        halo_copy(0).wait_send()
        halo_copy(1).wait_recv()

    @pl.when(has_previous)
    def _():
        halo_copy(1).wait_send()
        halo_copy(0).wait_recv()

    own_weights.wait()

    @pl.loop(1, groups)
    def _(step):
        weight_copy(step).wait()

    @pl.loop(1, lat_count)
    def _(step):
        lat_copy(step).wait_send()

    @pl.loop(1, sec_count)
    def _(step):
        sec_copy(step).wait_send()

    @pl.loop(0, sec_count)
    def _(back):
        @pl.loop(1, col_count)
        def _(step):
            col_copy(back, step).wait()


def exchange(sizes, points, table, slots, state, weights, halo):
    fields, width = state.shape
    waves = table.shape[2]
    sec_count, lat_count, col_count = sizes
    groups = sec_count * col_count
    padded = weights.shape[1]
    anywhere = pl.BlockSpec(memory_space=pl.ANY)
    inside = pl.BlockSpec(memory_space=pltpu.VMEM)
    halo_shape = jax.ShapeDtypeStruct(halo.shape, halo.dtype)
    out = pl.pallas_call(
        functools.partial(exchange_kernel, sizes),
        out_shape=[
            jax.ShapeDtypeStruct((groups, lat_count, padded, 2 * fields), jnp.bfloat16),
            jax.ShapeDtypeStruct(weights.shape, jnp.bfloat16),
            halo_shape,
            halo_shape,
        ],
        in_specs=[pl.BlockSpec(memory_space=pltpu.SMEM), inside, inside, inside, anywhere, anywhere],
        out_specs=[anywhere] * 4,
        scratch_shapes=[
            pltpu.VMEM((2, CHUNK, waves), jnp.float32),
            pltpu.VMEM((2 * fields, waves), jnp.float32),
            pltpu.VMEM((lat_count, padded, 2 * fields), jnp.bfloat16),
            pltpu.SemaphoreType.DMA((2,)),
            pltpu.SemaphoreType.DMA((groups,)),
            pltpu.SemaphoreType.DMA((groups,)),
            pltpu.SemaphoreType.DMA((2,)),
            pltpu.SemaphoreType.DMA((2,)),
            pltpu.SemaphoreType.DMA((lat_count,)),
            pltpu.SemaphoreType.DMA((lat_count,)),
            pltpu.SemaphoreType.DMA((sec_count,)),
            pltpu.SemaphoreType.DMA((sec_count,)),
            pltpu.SemaphoreType.DMA((sec_count, col_count)),
            pltpu.SemaphoreType.DMA((sec_count, col_count)),
        ],
        compiler_params=pltpu.CompilerParams(
            vmem_limit_bytes=24 * 2**20, collective_id=0, has_side_effects=True
        ),
        cost_estimate=pl.CostEstimate(
            flops=4 * fields * waves * width, bytes_accessed=8 * 2**20, transcendentals=0
        ),
    )(points, table, slots, state, weights, halo)
    return out


REACH = (-2, -1, 1, 2)


def flux_kernel(sizes, row_ref, out_ref, send_sem, recv_sem):
    sec_count, lat_count, col_count = sizes
    devices = sec_count * lat_count * col_count
    sec, lat, col = (lax.axis_index(name) for name in LINE)
    line = (sec * lat_count + lat) * col_count + col
    places = [place_of((line + devices - step) % devices, lat_count, col_count) for step in REACH]
    barrier = pltpu.get_barrier_semaphore()
    for place in places:
        pl.semaphore_signal(barrier, inc=1, device_id=place, device_id_type=MESH)
    pl.semaphore_wait(barrier, len(REACH))
    copies = [
        pltpu.make_async_remote_copy(
            src_ref=row_ref,
            dst_ref=out_ref.at[k],
            send_sem=send_sem.at[k],
            recv_sem=recv_sem.at[k],
            device_id=place,
            device_id_type=MESH,
        )
        for k, place in enumerate(places)
    ]
    for copy in copies:
        copy.start()
    for copy in copies:
        copy.wait()


def near_rows(sizes, row):
    shape = (8, row.shape[0] // 8)
    out = pl.pallas_call(
        functools.partial(flux_kernel, sizes),
        out_shape=jax.ShapeDtypeStruct((len(REACH),) + shape, row.dtype),
        in_specs=[pl.BlockSpec(memory_space=pltpu.VMEM)],
        out_specs=pl.BlockSpec(memory_space=pltpu.VMEM),
        scratch_shapes=[pltpu.SemaphoreType.DMA((len(REACH),))] * 2,
        compiler_params=pltpu.CompilerParams(
            vmem_limit_bytes=2**20, collective_id=1, has_side_effects=True
        ),
    )(row.reshape(shape))
    return out.reshape(len(REACH), row.shape[0])


def legendre_kernel(degree_ref, slots_ref, weight_ref, coef_ref, out_ref):
    groups, lines, pair, width = coef_ref.shape
    rows = groups * lines
    packed = weight_ref.shape[2]
    degrees = out_ref.shape[1]
    first = degree_ref[0]
    for half in range(pair // 8):
        cut = slice(half * 8, half * 8 + 8)
        held = weight_ref[:, cut, :].astype(jnp.float32).reshape(groups * 8, packed)
        parts = [
            pltpu.roll(held, (packed - q * degrees) % packed, 1)[:, :128] if q else held[:, :128]
            for q in range(lines)
        ]
        values = jnp.concatenate(parts, axis=0).T[:degrees]
        lane_slot = lax.broadcasted_iota(jnp.int32, (degrees, rows * 8), 1) % 8
        coefs = jnp.concatenate(
            [
                coef_ref[:, q, cut, :].astype(jnp.float32).reshape(groups * 8, width)
                for q in range(lines)
            ],
            axis=0,
        ).astype(jnp.bfloat16)
        degree = first + lax.broadcasted_iota(jnp.int32, (degrees, width), 0)
        for s in range(8):
            wave = slots_ref[pl.program_id(0) * pair + half * 8 + s]
            left = jnp.where(lane_slot == s, values, 0.0).astype(jnp.bfloat16)
            summed = jnp.dot(left, coefs, preferred_element_type=jnp.float32)
            out_ref[half * 8 + s] = jnp.where(degree >= wave, summed, 0.0)


def legendre(weights, coefs, slots, first_degree, slot_count, degrees):
    groups, lines, padded, width = coefs.shape
    rows = groups * lines
    return pl.pallas_call(
        legendre_kernel,
        grid=(padded // SLOT_PAD,),
        out_shape=jax.ShapeDtypeStruct((slot_count, degrees, width), jnp.float32),
        in_specs=[
            pl.BlockSpec(memory_space=pltpu.SMEM),
            pl.BlockSpec(memory_space=pltpu.SMEM),
            pl.BlockSpec((groups, SLOT_PAD, weights.shape[2]), lambda i: (0, i, 0)),
            pl.BlockSpec((groups, lines, SLOT_PAD, width), lambda i: (0, 0, i, 0)),
        ],
        out_specs=pl.BlockSpec((SLOT_PAD, degrees, width), lambda i: (i, 0, 0)),
        compiler_params=pltpu.CompilerParams(vmem_limit_bytes=(8 if rows <= 64 else 32) * 2**20),
        cost_estimate=pl.CostEstimate(
            flops=2 * rows * padded * width * degrees * 8,
            bytes_accessed=4 * slot_count * degrees * width + 4 * rows * padded * width,
            transcendentals=0,
        ),
    )(first_degree, slots, weights, coefs)


def split_two(values):
    top = lax.reduce_precision(values, 8, 7)
    return [top.astype(jnp.bfloat16), (values - top).astype(jnp.bfloat16)]


def pick_points(arrays, index):
    length = arrays[0].shape[0]
    tiles = -(-length // 128)
    matrix = jnp.stack(arrays).reshape(len(arrays), tiles, 128)
    chosen = (jnp.arange(tiles, dtype=jnp.int32)[:, None] == index[None, :] // 128).astype(jnp.bfloat16)
    spread = jnp.einsum("kta,tx->kax", matrix, chosen, preferred_element_type=jnp.float32)
    lane = jnp.arange(128, dtype=jnp.int32)[:, None] == index[None, :] % 128
    return jnp.where(lane[None], spread, 0.0).sum(axis=1)


def advance_coupled_model(
    bordered_array,
    meridian_exchange_factor,
    zonal_exchange_factor,
    depthwise_exchange_factor,
    boundary_warming_term,
):
    centre = bordered_array[:, 1:-1]
    meridional = meridian_exchange_factor[1:] * (
        bordered_array[:, 2:] - centre
    ) - meridian_exchange_factor[:-1] * (centre - bordered_array[:, :-2])
    east_flux = zonal_exchange_factor * (jnp.roll(centre, -1, axis=2) - centre)
    zonal_div = east_flux - jnp.roll(east_flux, 1, axis=2)
    vertical_flux = depthwise_exchange_factor * (centre[1:] - centre[:-1])
    zero_layer = jnp.zeros_like(vertical_flux[:1])
    vertical = jnp.concatenate([vertical_flux, zero_layer], 0) - jnp.concatenate(
        [zero_layer, vertical_flux], 0
    )
    forced = jnp.concatenate([boundary_warming_term[None], jnp.zeros_like(centre[1:])], 0)
    return centre + meridional + zonal_div + vertical + forced


def body(
    physical_state,
    parallel_lengths,
    zonal_mode_assignment,
    weighted_associated_polynomials,
    marine_tracer_state,
    lateral_diffusivity,
    depthwise_diffusivity,
    water_indicator,
    overlying_parallel,
    underlying_marine_parallel,
):
    lat_count = lax.axis_size("lat")
    groups = lax.axis_size("sec") * lax.axis_size("col")
    devices = groups * lat_count
    grid_width = physical_state.shape[2]
    strata = physical_state.shape[1] // 4
    slot_count, wave_count, row_count = weighted_associated_polynomials.shape
    block_degrees = wave_count // groups
    padded = -(-slot_count // SLOT_PAD) * SLOT_PAD
    linear_index = (
        lax.axis_index("sec") * lat_count + lax.axis_index("lat")
    ) * lax.axis_size("col") + lax.axis_index("col")
    group_index = lax.axis_index("sec") * lax.axis_size("col") + lax.axis_index("col")
    points = parallel_lengths[0]

    rows = marine_tracer_state.shape[1]
    span = marine_tracer_state.shape[2]
    layers = marine_tracer_state.shape[0]
    relative = overlying_parallel - linear_index
    payload = jnp.concatenate(
        [
            marine_tracer_state,
            lateral_diffusivity[None],
            depthwise_diffusivity[None],
            water_indicator.astype(jnp.float32)[None],
            jnp.broadcast_to(relative.astype(jnp.float32)[:, None], (rows, span))[None],
        ],
        axis=0,
    )
    halo = payload.astype(jnp.bfloat16).reshape((layers + 4) * rows, span)

    send = weighted_associated_polynomials.reshape(slot_count, groups, block_degrees, row_count)
    send = jnp.transpose(send, (1, 0, 3, 2)).reshape(groups, slot_count, row_count * block_degrees)
    lanes = -(-send.shape[2] // 128) * 128
    send = jnp.pad(send, ((0, 0), (0, padded - slot_count), (0, lanes - send.shape[2])))
    slots = zonal_mode_assignment.reshape(lat_count, slot_count)
    slots = jnp.pad(slots, ((0, 0), (0, padded - slot_count)), constant_values=wave_count)
    coefs, weights, before, after = exchange(
        (lax.axis_size("sec"), lat_count, lax.axis_size("col")),
        parallel_lengths,
        angle_tables(points, wave_count, grid_width),
        slots.reshape(-1, 1),
        physical_state[0],
        send,
        halo,
    )
    first, last = linear_index == 0, linear_index == devices - 1
    before = jnp.where(first, jnp.zeros_like(before), before).astype(jnp.float32)
    after = jnp.where(last, jnp.zeros_like(after), after).astype(jnp.float32)
    before = before.reshape(payload.shape)
    after = after.reshape(payload.shape)

    surface = jnp.concatenate([before[0], marine_tracer_state[0], after[0]], axis=0)
    under = underlying_marine_parallel[0] - (linear_index - 1) * rows
    skin = jnp.where(jnp.arange(3 * rows)[:, None] == under, surface, 0.0).sum(axis=0)
    ocean_points = jnp.arange(span, dtype=jnp.int32)
    column = ocean_points * points // span
    sea_column = jnp.minimum(column * span // points, span - 1)
    skin_hi, skin_lo = split_two(skin)
    mapped = pick_points([skin_hi, skin_lo], sea_column)
    bottom = strata - 1
    zonal_wind = physical_state[0, bottom].astype(jnp.float32)
    meridional_wind = physical_state[0, strata + bottom].astype(jnp.float32)
    speed = thermal_transfer_factor * jnp.sqrt(
        zonal_wind * zonal_wind + meridional_wind * meridional_wind + 1.0
    )
    speed_hi, speed_lo = split_two(speed)
    picked = pick_points([speed_hi, speed_lo, physical_state[0, 2 * strata + bottom]], column)
    flux = (picked[0] + picked[1]) * (mapped[0] + mapped[1] - picked[2])
    near = near_rows((lax.axis_size("sec"), lat_count, lax.axis_size("col")), flux)
    flux_near = {0: flux, **{step: near[k] for k, step in enumerate(REACH)}}

    whole = jnp.concatenate([before, payload, after], axis=1)
    thermal = whole[:layers]
    kappa, depth, sea, relative = (whole[layers + k] for k in range(4))
    owner = jnp.arange(3 * rows, dtype=jnp.int32)[:, None] // rows - 1
    target = relative + owner.astype(jnp.float32)
    forcing = jnp.zeros_like(sea)
    for step, row in flux_near.items():
        forcing = jnp.where(target == step, row[None], forcing)
    source = force_coef * sea * forcing
    depthwise = depth * sea
    faces = 0.5 * (kappa[:-1] + kappa[1:]) * sea[:-1] * sea[1:]
    east = 0.5 * (kappa + jnp.roll(kappa, -1, axis=1)) * sea * jnp.roll(sea, -1, axis=1)
    total = 3 * rows
    for iteration in range(OSTEPS):
        a, b = iteration + 1, total - iteration - 1
        thermal = advance_coupled_model(
            thermal, faces[a - 1 : b], east[a:b], depthwise[a:b], source[a:b]
        )

    own_waves = lax.dynamic_slice_in_dim(
        slots.reshape(-1), lax.axis_index("lat") * padded, padded
    )
    first_degree = jnp.reshape(group_index * block_degrees, (1,)).astype(jnp.int32)
    harmonic = legendre(weights, coefs, own_waves, first_degree, slot_count, block_degrees)
    return (jnp.transpose(harmonic, (1, 0, 2)), thermal)


def fast_kernel(
    sizes,
    points_hbm,
    over_hbm,
    under_hbm,
    slots_hbm,
    x_hbm,
    weight_ref,
    kappa_ref,
    depth_ref,
    water_ref,
    ocean_ref,
    coef_out,
    weight_out,
    thermal_out,
    points_ref,
    over_ref,
    under_ref,
    slots_ref,
    x_ref,
    table_ref,
    strip_ref,
    msg_ref,
    base_ref,
    xm_ref,
    z_ref,
    coefs_ref,
    mine_ref,
    halo_ref,
    before_ref,
    after_ref,
    plane_ref,
    heat_ref,
    face_ref,
    east_ref,
    down_ref,
    source_ref,
    local_ref,
    flux_ref,
    input_sem,
    ocean_sem,
    local_sem,
    weight_send,
    weight_recv,
    halo_send,
    halo_recv,
    flux_send,
    flux_recv,
    lat_send,
    lat_recv,
    direct_send,
    direct_recv,
    diag_send,
    diag_recv,
    chip_send,
    chip_recv,
):
    sec_count, lat_count, col_count = sizes
    groups = sec_count * col_count
    devices = groups * lat_count
    sec, lat, col = (lax.axis_index(name) for name in LINE)
    group = sec * col_count + col
    line = (sec * lat_count + lat) * col_count + col
    rows, layers, span = thermal_out.shape
    following = place_of((line + 1) % devices, lat_count, col_count)
    previous = place_of((line + devices - 1) % devices, lat_count, col_count)
    has_next, has_previous = line < devices - 1, line > 0
    sides = (sec + 1 - 2 * (sec % 2), (sec + 2) % 4)
    corner = 3 - sec

    ocean_copies = [
        pltpu.make_async_copy(ocean_ref.at[:, r, :], heat_ref.at[0, rows + r], ocean_sem.at[r])
        for r in range(rows)
    ]
    inputs = [
        pltpu.make_async_copy(source, target, input_sem.at[k])
        for k, (source, target) in enumerate(
            (
                (points_hbm, points_ref),
                (over_hbm, over_ref),
                (under_hbm, under_ref),
                (slots_hbm, slots_ref),
                (x_hbm, x_ref),
            )
        )
    ]
    for copy in ocean_copies + inputs:
        copy.start()

    def group_place(step):
        bit0 = (group % 2 + step % 2) % 2
        bit1 = (group // 2 % 2 + step // 2 % 2) % 2
        bit2 = (group // 4 + step // 4) % 2
        other = 4 * bit2 + 2 * bit1 + bit0
        return other, {"sec": other // col_count, "lat": lat, "col": other % col_count}

    def lat_place(step):
        other = (lat + step) % lat_count
        return other, {"sec": sec, "lat": other, "col": col}

    flux_places = [place_of((line + devices - step) % devices, lat_count, col_count) for step in REACH]
    barrier = pltpu.get_barrier_semaphore()
    for place in flux_places:
        pl.semaphore_signal(barrier, inc=1, device_id=place, device_id_type=MESH)

    @pl.loop(1, groups)
    def _(step):
        pl.semaphore_signal(barrier, inc=1, device_id=group_place(step)[1], device_id_type=MESH)

    @pl.loop(1, lat_count)
    def _(step):
        pl.semaphore_signal(barrier, inc=1, device_id=lat_place(step)[1], device_id_type=MESH)

    def weight_copy(step):
        other, place = group_place(step)
        return pltpu.make_async_remote_copy(
            src_ref=msg_ref.at[other],
            dst_ref=weight_out.at[group],
            send_sem=weight_send.at[step],
            recv_sem=weight_recv.at[step],
            device_id=place,
            device_id_type=MESH,
        )

    def halo_copy(side):
        return pltpu.make_async_remote_copy(
            src_ref=halo_ref,
            dst_ref=(before_ref, after_ref)[side],
            send_sem=halo_send.at[side],
            recv_sem=halo_recv.at[side],
            device_id=(following, previous)[side],
            device_id_type=MESH,
        )

    def flux_copy(k):
        return pltpu.make_async_remote_copy(
            src_ref=flux_ref.at[len(REACH)],
            dst_ref=flux_ref.at[k],
            send_sem=flux_send.at[k],
            recv_sem=flux_recv.at[k],
            device_id=flux_places[k],
            device_id_type=MESH,
        )

    def lat_copy(step):
        other, place = lat_place(step)
        return pltpu.make_async_remote_copy(
            src_ref=mine_ref.at[other],
            dst_ref=coef_out.at[group, lat],
            send_sem=lat_send.at[step],
            recv_sem=lat_recv.at[step],
            device_id=place,
            device_id_type=MESH,
        )

    def direct_copy(side, line_row):
        piece = coef_out.at[group, line_row]
        return pltpu.make_async_remote_copy(
            src_ref=piece,
            dst_ref=piece,
            send_sem=direct_send.at[side, line_row],
            recv_sem=direct_recv.at[side, line_row],
            device_id={"sec": sides[side], "lat": lat, "col": col},
            device_id_type=MESH,
        )

    def diag_copy(side, line_row):
        piece = coef_out.at[sides[side] * col_count + col, line_row]
        return pltpu.make_async_remote_copy(
            src_ref=piece,
            dst_ref=piece,
            send_sem=diag_send.at[line_row],
            recv_sem=diag_recv.at[line_row],
            device_id={"sec": sides[1 - side], "lat": lat, "col": col},
            device_id_type=MESH,
        )

    def chip_copy(which, line_row):
        origin = (sec, sides[0], sides[1], corner)[which]
        piece = coef_out.at[origin * col_count + col, line_row]
        return pltpu.make_async_remote_copy(
            src_ref=piece,
            dst_ref=piece,
            send_sem=chip_send.at[which, line_row],
            recv_sem=chip_recv.at[which, line_row],
            device_id={"sec": sec, "lat": lat, "col": 1 - col},
            device_id_type=MESH,
        )

    band = msg_ref.shape[1]
    degrees = msg_ref.shape[2] // groups
    halves = weight_ref.shape[1] // band
    for g in range(groups):
        for p in range(groups):
            t, h = p // halves, p % halves
            msg_ref[g, :, p * degrees : (p + 1) * degrees] = weight_ref[
                t, h * band : (h + 1) * band, g * degrees : (g + 1) * degrees
            ]

    for copy in inputs[:-1] + ocean_copies:
        copy.wait()
    sea = water_ref[...].astype(jnp.float32)
    plane_ref[:rows] = kappa_ref[...] * sea
    plane_ref[rows:] = depth_ref[...] * sea
    deep = rows * layers
    part = span // 2
    for side in range(2):
        cut = slice(side * part, side * part + part)
        for r in range(0, rows, 2):
            pair = jnp.concatenate(
                [heat_ref[0, rows + r, :, cut], heat_ref[0, rows + r + 1, :, cut]], axis=0
            )
            first = side * deep + r * layers
            halo_ref[first : first + 2 * layers] = pair.astype(jnp.bfloat16)
    halo_ref[2 * deep :] = jnp.concatenate(
        [plane_ref[:, :part], plane_ref[:, part:]], axis=0
    ).astype(jnp.bfloat16)

    pl.semaphore_wait(barrier, len(REACH) + groups - 1 + lat_count - 1)

    @pl.when(has_next)
    def _():
        halo_copy(0).start()

    @pl.when(has_previous)
    def _():
        halo_copy(1).start()

    @pl.loop(1, 7)
    def _(step):
        weight_copy(step).start()

    own_weights = pltpu.make_async_copy(msg_ref.at[group], weight_out.at[group], local_sem.at[0])
    own_weights.start()

    points = points_ref[0]
    waves = table_ref.shape[2]
    fields = x_ref.shape[0]
    chunks = x_ref.shape[1] // CHUNK
    top = LOW + CHUNK // LOW
    shape = table_ref.shape[1:]
    place = lax.broadcasted_iota(jnp.int32, shape, 0)
    place = jnp.where(
        place < LOW, place, jnp.where(place < top, (place - LOW) * LOW, (place - top) * CHUNK)
    )
    product = place.astype(jnp.float32) * lax.broadcasted_iota(jnp.int32, shape, 1).astype(jnp.float32)
    count = jnp.full(shape, points, jnp.int32).astype(jnp.float32)
    angle = (product - jnp.round(product / count) * count) * (two_pi / count)
    scale = jnp.where(lax.broadcasted_iota(jnp.int32, shape, 0) >= top, 1.0 / jnp.sqrt(count), 1.0)
    table_ref[0] = jnp.cos(angle) * scale
    table_ref[1] = -jnp.sin(angle) * scale
    low_c, low_s = table_ref[0, :LOW], table_ref[1, :LOW]
    for w in range(waves // 128):
        cut = slice(w * 128, w * 128 + 128)
        for b in range(0, CHUNK // LOW, 2):
            real, imag = [], []
            for q in (b, b + 1):
                mid_c = table_ref[0, LOW + q : LOW + q + 1, cut]
                mid_s = table_ref[1, LOW + q : LOW + q + 1, cut]
                real.append(low_c[:, cut] * mid_c - low_s[:, cut] * mid_s)
                imag.append(low_c[:, cut] * mid_s + low_s[:, cut] * mid_c)
            real = jnp.concatenate(real, axis=0).astype(jnp.bfloat16)
            imag = jnp.concatenate(imag, axis=0).astype(jnp.bfloat16)
            base_ref[w, b * LOW : (b + 2) * LOW, :128] = real
            base_ref[w, b * LOW : (b + 2) * LOW, 128:] = imag
    inputs[-1].wait()
    for a in range(chunks):
        position = a * CHUNK + lax.broadcasted_iota(jnp.int32, (fields, CHUNK), 1)
        block = x_ref[:, a * CHUNK : (a + 1) * CHUNK].astype(jnp.float32)
        xm_ref[a * fields : (a + 1) * fields] = jnp.where(position < points, block, 0.0).astype(
            jnp.bfloat16
        )
    for w in range(waves // 128):
        cut = slice(w * 128, w * 128 + 128)
        z_ref[...] = jnp.dot(xm_ref[...], base_ref[w], preferred_element_type=jnp.float32)
        real = jnp.zeros((fields, 128), jnp.float32)
        imag = jnp.zeros((fields, 128), jnp.float32)
        for a in range(chunks):
            turn_c = table_ref[0, top + a : top + a + 1, cut]
            turn_s = table_ref[1, top + a : top + a + 1, cut]
            part_r = z_ref[a * fields : (a + 1) * fields, :128]
            part_i = z_ref[a * fields : (a + 1) * fields, 128:]
            real = real + part_r * turn_c - part_i * turn_s
            imag = imag + part_r * turn_s + part_i * turn_c
        wave = w * 128 + lax.broadcasted_iota(jnp.int32, (fields, 128), 1)
        kept = wave < points // 2
        coefs_ref[:fields, cut] = jnp.where(kept, real, 0.0).astype(jnp.bfloat16)
        coefs_ref[fields:, cut] = jnp.where(kept, imag, 0.0).astype(jnp.bfloat16)
    padded = mine_ref.shape[1]

    slot_total = slots_ref.shape[0]
    slot_count = slot_total // lat_count
    ring = strip_ref.shape[1]
    lanes = -(-padded // 128) * 128
    strip_ref[...] = jnp.full_like(strip_ref, waves)
    strip_ref[0:1, :slot_total] = slots_ref[...].reshape(1, slot_total)

    def fill(other):
        held = pltpu.roll(strip_ref[...], ring - other * slot_count, 1)[0:1, :lanes]
        held = jnp.where(lax.broadcasted_iota(jnp.int32, (1, lanes), 1) < slot_count, held, waves)
        pick = held == lax.broadcasted_iota(jnp.int32, (waves, lanes), 0)
        pick = jnp.where(pick, 1.0, 0.0).astype(jnp.bfloat16)
        chosen = jnp.dot(coefs_ref[...], pick, preferred_element_type=jnp.float32)
        mine_ref[other] = chosen.T[:padded].astype(jnp.bfloat16)

    @pl.loop(1, lat_count)
    def _(step):
        fill((lat + step) % lat_count)
        lat_copy(step).start()

    fill(lat)
    own_coefs = pltpu.make_async_copy(mine_ref.at[lat], coef_out.at[group, lat], local_sem.at[1])
    own_coefs.start()

    def spread_piece(line_row):
        direct_copy(0, line_row).start()
        direct_copy(1, line_row).start()
        chip_copy(0, line_row).start()

    own_coefs.wait()
    spread_piece(lat)

    strata = fields // 4
    bottom = strata - 1
    wide = 512
    shift = span.bit_length() - 1

    def halves_of(value):
        upper = value.astype(jnp.bfloat16).astype(jnp.float32)
        return upper, value - upper

    def columns_of(start):
        place = start + lax.broadcasted_iota(jnp.int32, (1, wide), 1)
        return lax.shift_right_logical(place * points, shift)

    def pick(table, index):
        tiles = table.shape[1]
        one = lax.broadcasted_iota(jnp.int32, (tiles, wide), 0) == lax.shift_right_logical(index, 7)
        one = jnp.where(one, 1.0, 0.0).astype(jnp.bfloat16)
        lane = lax.broadcasted_iota(jnp.int32, (128, wide), 0) == (index & 127)
        spread = jnp.dot(table, one, preferred_element_type=jnp.float32)
        return [
            jnp.sum(jnp.where(lane, spread[k * 128 : (k + 1) * 128], 0.0), axis=0, keepdims=True)
            for k in range(table.shape[0] // 128)
        ]

    def table_of(values):
        tiles = values[0].shape[1] // 128
        return jnp.concatenate([v.reshape(tiles, 128).T for v in values], axis=0).astype(jnp.bfloat16)

    zonal = x_ref[bottom : bottom + 1].astype(jnp.float32)
    meridional = x_ref[strata + bottom : strata + bottom + 1].astype(jnp.float32)
    air = x_ref[2 * strata + bottom : 2 * strata + bottom + 1].astype(jnp.float32)
    speed = thermal_transfer_factor * jnp.sqrt(zonal * zonal + meridional * meridional + 1.0)
    table = table_of([*halves_of(speed), air])

    @pl.loop(0, span // wide)
    def _(k):
        start = pl.multiple_of(k * wide, wide)
        upper, lower, below = pick(table, columns_of(start))
        local_ref[0:1, pl.ds(start, wide)] = upper + lower
        local_ref[1:2, pl.ds(start, wide)] = below

    @pl.when(has_next)
    def _():
        halo_copy(0).wait_send()
        halo_copy(1).wait_recv()

    @pl.when(has_previous)
    def _():
        halo_copy(1).wait_send()
        halo_copy(0).wait_recv()

    @pl.when(jnp.logical_not(has_next))
    def _():
        after_ref[...] = jnp.zeros_like(after_ref)

    @pl.when(jnp.logical_not(has_previous))
    def _():
        before_ref[...] = jnp.zeros_like(before_ref)

    for start, held in ((0, before_ref), (2 * rows, after_ref)):
        for side in range(2):
            for r in range(0, rows, 2):
                first = side * deep + r * layers
                pair = held[first : first + 2 * layers].astype(jnp.float32)
                cut = slice(side * part, side * part + part)
                heat_ref[0, start + r, :, cut] = pair[:layers]
                heat_ref[0, start + r + 1, :, cut] = pair[layers:]

    under = under_ref[0] - (line - 1) * rows
    skin = jnp.zeros((1, span), jnp.float32)
    for r in range(3 * rows):
        skin = jnp.where(under == r, heat_ref[0, r, 0:1, :], skin)
    skin_table = table_of(halves_of(skin))
    inverse = 1.0 / jnp.full((1, wide), points, jnp.int32).astype(jnp.float32)

    @pl.loop(0, span // wide)
    def _(k):
        start = pl.multiple_of(k * wide, wide)
        scaled = columns_of(start) << shift
        index = (scaled.astype(jnp.float32) * inverse).astype(jnp.int32)
        rest = scaled - index * points
        index = jnp.where(rest < 0, index - 1, jnp.where(rest >= points, index + 1, index))
        index = jnp.minimum(index, span - 1)
        upper, lower = pick(skin_table, index)
        cut = pl.ds(start, wide)
        flux_ref[len(REACH), 0:1, cut] = local_ref[0:1, cut] * (upper + lower - local_ref[1:2, cut])

    lane = lax.broadcasted_iota(jnp.int32, (1, 128), 1)
    relative = jnp.zeros((1, 128), jnp.float32)
    for r in range(rows):
        relative = jnp.where(lane == r, (over_ref[r] - line).astype(jnp.float32), relative)
    flux_ref[len(REACH), 0:1, span:] = relative
    for k in range(len(REACH)):
        flux_copy(k).start()

    @pl.loop(1, lat_count)
    def _(step):
        lat_copy(step).wait_recv()
        spread_piece((lat + lat_count - step) % lat_count)

    weight_copy(7).start()

    edges = []
    for held in (before_ref, after_ref):
        coarse = held[2 * deep :].astype(jnp.float32)
        edges.append(jnp.concatenate([coarse[: 2 * rows], coarse[2 * rows :]], axis=1))
    kappa = jnp.concatenate([edges[0][:rows], plane_ref[:rows], edges[1][:rows]], axis=0)
    depth = jnp.concatenate([edges[0][rows:], plane_ref[rows:], edges[1][rows:]], axis=0)
    total = 3 * rows
    layer = lax.broadcasted_iota(jnp.int32, (layers, span), 0)
    beside = pltpu.roll(kappa, span - 1, 1)
    east = jnp.where((kappa > 0.0) & (beside > 0.0), 0.5 * (kappa + beside), 0.0)
    upper, lower = kappa[:-1], kappa[1:]
    faces = jnp.where((upper > 0.0) & (lower > 0.0), 0.5 * (upper + lower), 0.0)
    for r in range(1, total):
        face_ref[r] = jnp.broadcast_to(faces[r - 1 : r], (layers, span))
    for r in range(1, total - 1):
        east_ref[r] = jnp.broadcast_to(east[r : r + 1], (layers, span))
        down_ref[r] = jnp.where(layer < layers - 1, depth[r : r + 1], 0.0)

    for k in range(len(REACH)):
        flux_copy(k).wait()
    near = REACH + (0,)
    for r in range(1, total - 1):
        owner = r // rows - 1
        target = flux_ref[near.index(owner), 0:1, span + r % rows : span + r % rows + 1] + float(owner)
        row = jnp.zeros((1, span), jnp.float32)
        for k, step in enumerate(near):
            row = jnp.where(target == float(step), flux_ref[k, 0:1, :span], row)
        row = jnp.where(kappa[r : r + 1] > 0.0, force_coef * row, 0.0)
        source_ref[r] = jnp.where(layer == 0, row, 0.0)

    def ocean_step(step):
        held, made = step % 2, (step + 1) % 2

        @pl.loop(step + 1, total - step - 1)
        def _(r):
            mid = heat_ref[held, r]
            flow = face_ref[r + 1] * (heat_ref[held, r + 1] - mid) - face_ref[r] * (mid - heat_ref[held, r - 1])
            lateral = east_ref[r] * (pltpu.roll(mid, span - 1, 1) - mid)
            flow = flow + (lateral - pltpu.roll(lateral, 1, 1))
            sinking = down_ref[r] * (pltpu.roll(mid, layers - 1, 0) - mid)
            flow = flow + (sinking - pltpu.roll(sinking, 1, 0))
            fresh = mid + flow + source_ref[r]
            if step < OSTEPS - 1:
                heat_ref[made, r] = fresh
            else:
                thermal_out[r - rows] = fresh

    ocean_step(0)
    ocean_step(1)

    @pl.loop(0, lat_count)
    def _(step):
        line_row = (lat + lat_count - step) % lat_count
        direct_copy(0, line_row).wait_recv()

        @pl.when(line_row % 2 == 0)
        def _():
            diag_copy(0, line_row).start()

        chip_copy(1, line_row).start()
        direct_copy(1, line_row).wait_recv()

        @pl.when(line_row % 2 == 1)
        def _():
            diag_copy(1, line_row).start()

        chip_copy(2, line_row).start()

    ocean_step(2)
    ocean_step(3)

    @pl.loop(0, lat_count)
    def _(step):
        line_row = (lat + lat_count - step) % lat_count
        diag_copy(0, line_row).wait_recv()
        chip_copy(3, line_row).start()

    own_weights.wait()

    @pl.loop(1, lat_count)
    def _(step):
        lat_copy(step).wait_send()

    @pl.loop(0, lat_count)
    def _(line_row):
        direct_copy(0, line_row).wait_send()
        direct_copy(1, line_row).wait_send()
        diag_copy(0, line_row).wait_send()
        for which in range(4):
            chip_copy(which, line_row).wait_send()

    @pl.loop(1, groups)
    def _(step):
        weight_copy(step).wait()

    @pl.loop(0, lat_count)
    def _(line_row):
        for which in range(4):
            chip_copy(which, line_row).wait_recv()


def fast_exchange(sizes, points, over, under, slots, state, weights, kappa, depth, water, ocean):
    sec_count, lat_count, col_count = sizes
    groups = sec_count * col_count
    fields, width = state.shape
    waves = weights.shape[2]
    table_rows = -(-(LOW + CHUNK // LOW + width // CHUNK) // 8) * 8
    layers, rows, span = ocean.shape
    padded = weights.shape[1]
    band = lat_count * padded // groups
    chunks = width // CHUNK
    halo_rows = 2 * rows * (layers + 2)
    inside = pl.BlockSpec(memory_space=pltpu.VMEM)
    outside = pl.BlockSpec(memory_space=pl.ANY)
    near = len(REACH)
    dma = pltpu.SemaphoreType.DMA
    return pl.pallas_call(
        functools.partial(fast_kernel, sizes),
        out_shape=[
            jax.ShapeDtypeStruct((groups, lat_count, padded, 2 * fields), jnp.bfloat16),
            jax.ShapeDtypeStruct((groups, band, waves), jnp.bfloat16),
            jax.ShapeDtypeStruct((rows, layers, span), jnp.float32),
        ],
        in_specs=[outside] * 5 + [inside] * 4 + [outside],
        out_specs=[inside] * 3,
        scratch_shapes=[
            pltpu.SMEM(points.shape, jnp.int32),
            pltpu.SMEM(over.shape, jnp.int32),
            pltpu.SMEM(under.shape, jnp.int32),
            pltpu.VMEM(slots.shape, jnp.int32),
            pltpu.VMEM(state.shape, state.dtype),
            pltpu.VMEM((2, table_rows, waves), jnp.float32),
            pltpu.VMEM((8, -(-(slots.shape[0] + 256) // 128) * 128), jnp.int32),
            pltpu.VMEM((groups, band, waves), jnp.bfloat16),
            pltpu.VMEM((waves // 128, CHUNK, 256), jnp.bfloat16),
            pltpu.VMEM((chunks * fields, CHUNK), jnp.bfloat16),
            pltpu.VMEM((chunks * fields, 256), jnp.float32),
            pltpu.VMEM((2 * fields, waves), jnp.bfloat16),
            pltpu.VMEM((lat_count, padded, 2 * fields), jnp.bfloat16),
            pltpu.VMEM((halo_rows, span // 2), jnp.bfloat16),
            pltpu.VMEM((halo_rows, span // 2), jnp.bfloat16),
            pltpu.VMEM((halo_rows, span // 2), jnp.bfloat16),
            pltpu.VMEM((2 * rows, span), jnp.float32),
            pltpu.VMEM((2, 3 * rows, layers, span), jnp.float32),
            pltpu.VMEM((3 * rows, layers, span), jnp.float32),
            pltpu.VMEM((3 * rows, layers, span), jnp.float32),
            pltpu.VMEM((3 * rows, layers, span), jnp.float32),
            pltpu.VMEM((3 * rows, layers, span), jnp.float32),
            pltpu.VMEM((2, span), jnp.float32),
            pltpu.VMEM((near + 1, 1, span + 128), jnp.float32),
            dma((5,)),
            dma((rows,)),
            dma((2,)),
            dma((groups,)),
            dma((groups,)),
            dma((2,)),
            dma((2,)),
            dma((near,)),
            dma((near,)),
            dma((lat_count,)),
            dma((lat_count,)),
            dma((2, lat_count)),
            dma((2, lat_count)),
            dma((lat_count,)),
            dma((lat_count,)),
            dma((4, lat_count)),
            dma((4, lat_count)),
        ],
        compiler_params=pltpu.CompilerParams(
            vmem_limit_bytes=28 * 2**20, collective_id=2, has_side_effects=True
        ),
        cost_estimate=pl.CostEstimate(
            flops=4 * fields * waves * width, bytes_accessed=8 * 2**20, transcendentals=0
        ),
    )(points, over, under, slots, state, weights, kappa, depth, water, ocean)


def fast_legendre_kernel(
    col_count,
    slots_hbm,
    weight_ref,
    coef_ref,
    ocean_ref,
    out_ref,
    ocean_out,
    slots_ref,
    turned_ref,
    made_ref,
    made_sem,
    ocean_sem,
    slots_sem,
):
    groups, lines, padded, width = coef_ref.shape
    slot_count, degrees, _ = out_ref.shape
    rows = ocean_ref.shape[0]
    blocks = padded // 16
    rest = slot_count - (blocks - 1) * 16
    halves = padded // weight_ref.shape[1]
    majors = blocks // halves
    ocean_copies = [
        pltpu.make_async_copy(ocean_ref.at[r], ocean_out.at[:, r, :], ocean_sem.at[r]) for r in range(rows)
    ]
    slots_copy = pltpu.make_async_copy(slots_hbm, slots_ref, slots_sem)
    slots_copy.start()
    for copy in ocean_copies:
        copy.start()
    first_slot = lax.axis_index("lat") * slot_count
    last_slot = slots_ref.shape[0] - 1
    first_degree = (lax.axis_index("sec") * col_count + lax.axis_index("col")) * degrees

    def made_copy(block, count):
        cut = pl.ds(block * 16, count)
        return pltpu.make_async_copy(made_ref.at[cut], out_ref.at[cut], made_sem.at[block])

    degree = first_degree + lax.broadcasted_iota(jnp.int32, (degrees, width), 0)
    odd = lax.broadcasted_iota(jnp.int32, (lines * groups * 16, width), 0) % 2 == 1
    lane_pair = lax.broadcasted_iota(jnp.int32, (degrees, lines * groups * 16), 1) % 16 // 2

    slots_copy.wait()

    for major in range(majors):
        held = weight_ref[:, major * 16 : major * 16 + 16, :]
        turned_ref[major % 2] = held.reshape(groups * 16, held.shape[2]).T
        for half in range(halves):
            block = half * majors + major
            values = jnp.concatenate(
                [
                    turned_ref[major % 2, (t * halves + half) * degrees : (t * halves + half + 1) * degrees, :]
                    for t in range(lines)
                ],
                axis=1,
            )
            cut = slice(block * 16, block * 16 + 16)
            coefs = jnp.concatenate(
                [coef_ref[:, t, cut, :].reshape(groups * 16, width) for t in range(lines)], axis=0
            )
            nothing = jnp.zeros_like(coefs)
            both = jnp.concatenate(
                [jnp.where(odd, nothing, coefs), jnp.where(odd, coefs, nothing)], axis=1
            )
            left = jnp.concatenate(
                [jnp.where(lane_pair == j, values, jnp.zeros_like(values)) for j in range(8)], axis=0
            )
            summed = jnp.dot(left, both, preferred_element_type=jnp.float32)
            for s in range(16):
                wave = slots_ref[jnp.minimum(first_slot + block * 16 + s, last_slot)]
                part = summed[
                    s // 2 * degrees : (s // 2 + 1) * degrees, s % 2 * width : (s % 2 + 1) * width
                ]
                made_ref[block * 16 + s] = jnp.where(degree >= wave, part, 0.0)

            made_copy(block, 16 if block < blocks - 1 else rest).start()

    @pl.loop(0, blocks - 1)
    def _(block):
        made_copy(block, 16).wait()

    made_copy(blocks - 1, rest).wait()
    for copy in ocean_copies:
        copy.wait()


def fast_legendre(col_count, weights, coefs, ocean, slots, slot_count, degrees):
    groups, lines, padded, width = coefs.shape
    rows, layers, span = ocean.shape
    inside = pl.BlockSpec(memory_space=pltpu.VMEM)
    outside = pl.BlockSpec(memory_space=pl.ANY)
    anywhere = pl.BlockSpec(memory_space=pl.ANY)
    return pl.pallas_call(
        functools.partial(fast_legendre_kernel, col_count),
        out_shape=[
            jax.ShapeDtypeStruct((slot_count, degrees, width), jnp.float32),
            jax.ShapeDtypeStruct((layers, rows, span), jnp.float32),
        ],
        in_specs=[outside, inside, inside, inside],
        out_specs=[anywhere, anywhere],
        scratch_shapes=[
            pltpu.SMEM(slots.shape, jnp.int32),
            pltpu.VMEM((2, weights.shape[2], groups * 16), jnp.bfloat16),
            pltpu.VMEM((padded, degrees, width), jnp.float32),
            pltpu.SemaphoreType.DMA((padded // 16,)),
            pltpu.SemaphoreType.DMA((rows,)),
            pltpu.SemaphoreType.DMA,
        ],
        compiler_params=pltpu.CompilerParams(vmem_limit_bytes=32 * 2**20),
        cost_estimate=pl.CostEstimate(
            flops=2 * groups * lines * padded * width * degrees * 8,
            bytes_accessed=4 * slot_count * degrees * width,
            transcendentals=0,
        ),
    )(slots, weights, coefs, ocean)


def fast_body(
    physical_state,
    parallel_lengths,
    zonal_mode_assignment,
    weighted_associated_polynomials,
    marine_tracer_state,
    lateral_diffusivity,
    depthwise_diffusivity,
    water_indicator,
    overlying_parallel,
    underlying_marine_parallel,
):
    sizes = tuple(lax.axis_size(name) for name in LINE)
    sec_count, lat_count, col_count = sizes
    groups = sec_count * col_count
    slot_count, wave_count, _ = weighted_associated_polynomials.shape
    block_degrees = wave_count // groups
    padded = -(-slot_count // 32) * 32
    weights = jnp.transpose(weighted_associated_polynomials, (2, 0, 1))
    weights = jnp.pad(weights, ((0, 0), (0, padded - slot_count), (0, 0)))
    coefs, packed, ocean = fast_exchange(
        sizes,
        parallel_lengths,
        overlying_parallel,
        underlying_marine_parallel,
        zonal_mode_assignment,
        physical_state[0],
        weights,
        lateral_diffusivity,
        depthwise_diffusivity,
        water_indicator,
        marine_tracer_state,
    )
    harmonic, thermal = fast_legendre(
        col_count, packed, coefs, ocean, zonal_mode_assignment, slot_count, block_degrees
    )
    return (jnp.transpose(harmonic, (1, 0, 2)), thermal)


def compact(mesh):
    return mesh.shape["sec"] == 4 and mesh.shape["lat"] == 4 and mesh.shape["col"] == 2


def solution(mesh):
    return jax.shard_map(
        fast_body if compact(mesh) else body,
        mesh=mesh,
        in_specs=(
            P(LINE, None, None),
            P(LINE),
            P(),
            P("lat", None, GROUP),
            P(None, LINE, None),
            P(LINE, None),
            P(LINE, None),
            P(LINE, None),
            P(LINE),
            P(LINE),
        ),
        out_specs=(P(GROUP, "lat", None), P(None, LINE, None)),
        check_vma=False,
    )
```

```python
import functools

import jax
import jax.numpy as jnp
from jax import lax
from jax.experimental import pallas as pl
from jax.experimental.pallas import tpu as pltpu
from jax.sharding import PartitionSpec as P

OSTEPS = 4
LOW = 8
CHUNK = 256
SLOT_PAD = 16

two_pi = 6.283185307179586
thermal_transfer_factor = 0.8
force_coef = 0.1

GROUP = ("sec", "col")
LINE = ("sec", "lat", "col")


def angle_tables(points, wave_count, grid_width):
    low = jnp.arange(LOW, dtype=jnp.float32)
    mid = jnp.arange(CHUNK // LOW, dtype=jnp.float32) * LOW
    high = jnp.arange(grid_width // CHUNK, dtype=jnp.float32) * CHUNK
    place = jnp.concatenate([low, mid, high])
    count = points.astype(jnp.float32)
    product = place[:, None] * jnp.arange(wave_count, dtype=jnp.float32)[None, :]
    residue = product - jnp.round(product / count) * count
    angle = residue * (jnp.float32(two_pi) / count)
    scale = jnp.where(jnp.arange(place.shape[0]) >= LOW + CHUNK // LOW, 1.0 / jnp.sqrt(count), 1.0)
    return jnp.stack([jnp.cos(angle), -jnp.sin(angle)]) * scale[None, :, None]


MESH = pl.DeviceIdType.MESH


def place_of(index, lat_count, col_count):
    return {
        "sec": index // (lat_count * col_count),
        "lat": index // col_count % lat_count,
        "col": index % col_count,
    }


def exchange_kernel(
    sizes,
    points_ref,
    table_ref,
    slots_ref,
    x_ref,
    weight_ref,
    *refs,
):
    sec_count, lat_count, col_count = sizes
    halo, coef_out, weight_out, before, after = refs[:5]
    (base_ref, acc_ref, mine_ref, local_sem, weight_send, weight_recv, halo_send, halo_recv,
     lat_send, lat_recv, sec_send, sec_recv, col_send, col_recv) = refs[5:]
    groups = sec_count * col_count
    devices = groups * lat_count
    sec, lat, col = (lax.axis_index(name) for name in LINE)
    group = sec * col_count + col
    line = (sec * lat_count + lat) * col_count + col
    following = place_of((line + 1) % devices, lat_count, col_count)
    previous = place_of((line + devices - 1) % devices, lat_count, col_count)

    def group_place(step):
        other = (group + step) % groups
        return other, {"sec": other // col_count, "lat": lat, "col": other % col_count}

    def lat_place(step):
        other = (lat + step) % lat_count
        return other, {"sec": sec, "lat": other, "col": col}

    barrier = pltpu.get_barrier_semaphore()
    for place in (following, previous):
        pl.semaphore_signal(barrier, inc=1, device_id=place, device_id_type=MESH)

    @pl.loop(1, groups)
    def _(step):
        pl.semaphore_signal(barrier, inc=1, device_id=group_place(step)[1], device_id_type=MESH)

    @pl.loop(1, lat_count)
    def _(step):
        pl.semaphore_signal(barrier, inc=1, device_id=lat_place(step)[1], device_id_type=MESH)

    pl.semaphore_wait(barrier, groups + lat_count)

    def weight_copy(step):
        other, place = group_place(step)
        return pltpu.make_async_remote_copy(
            src_ref=weight_ref.at[other],
            dst_ref=weight_out.at[group],
            send_sem=weight_send.at[step],
            recv_sem=weight_recv.at[step],
            device_id=place,
            device_id_type=MESH,
        )

    def halo_copy(side):
        return pltpu.make_async_remote_copy(
            src_ref=halo,
            dst_ref=(before, after)[side],
            send_sem=halo_send.at[side],
            recv_sem=halo_recv.at[side],
            device_id=(following, previous)[side],
            device_id_type=MESH,
        )

    has_next, has_previous = line < devices - 1, line > 0

    def lat_copy(step):
        other, place = lat_place(step)
        return pltpu.make_async_remote_copy(
            src_ref=mine_ref.at[other],
            dst_ref=coef_out.at[group, lat],
            send_sem=lat_send.at[step],
            recv_sem=lat_recv.at[step],
            device_id=place,
            device_id_type=MESH,
        )

    def sec_copy(step):
        return pltpu.make_async_remote_copy(
            src_ref=coef_out.at[group],
            dst_ref=coef_out.at[group],
            send_sem=sec_send.at[step],
            recv_sem=sec_recv.at[step],
            device_id={"sec": (sec + step) % sec_count, "lat": lat, "col": col},
            device_id_type=MESH,
        )

    def col_copy(back, step):
        block = (sec + sec_count - back) % sec_count * col_count + col
        return pltpu.make_async_remote_copy(
            src_ref=coef_out.at[block],
            dst_ref=coef_out.at[block],
            send_sem=col_send.at[back, step],
            recv_sem=col_recv.at[back, step],
            device_id={"sec": sec, "lat": lat, "col": (col + step) % col_count},
            device_id_type=MESH,
        )

    own_weights = pltpu.make_async_copy(weight_ref.at[group], weight_out.at[group], local_sem.at[0])
    own_weights.start()

    @pl.loop(1, groups)
    def _(step):
        weight_copy(step).start()

    @pl.when(has_next)
    def _():
        halo_copy(0).start()

    @pl.when(has_previous)
    def _():
        halo_copy(1).start()

    points = points_ref[0]
    waves = table_ref.shape[2]
    fields = x_ref.shape[0]
    chunks = x_ref.shape[1] // CHUNK
    low_c, low_s = table_ref[0, :LOW], table_ref[1, :LOW]
    for b in range(CHUNK // LOW):
        mid_c = table_ref[0, LOW + b : LOW + b + 1]
        mid_s = table_ref[1, LOW + b : LOW + b + 1]
        base_ref[0, b * LOW : (b + 1) * LOW] = low_c * mid_c - low_s * mid_s
        base_ref[1, b * LOW : (b + 1) * LOW] = low_c * mid_s + low_s * mid_c
    acc_ref[...] = jnp.zeros_like(acc_ref)
    top = LOW + CHUNK // LOW

    @pl.loop(0, chunks)
    def _(a):
        start = pl.multiple_of(a * CHUNK, CHUNK)
        position = start + lax.broadcasted_iota(jnp.int32, (fields, CHUNK), 1)
        block = x_ref[:, pl.ds(start, CHUNK)].astype(jnp.float32)
        block = jnp.where(position < points, block, 0.0).astype(jnp.bfloat16)
        high_c = table_ref[0, pl.ds(top + a, 1)]
        high_s = table_ref[1, pl.ds(top + a, 1)]
        for w in range(0, waves, 128):
            cut = slice(w, w + 128)
            base_c, base_s = base_ref[0, :, cut], base_ref[1, :, cut]
            turn_c, turn_s = high_c[:, cut], high_s[:, cut]
            real = (base_c * turn_c - base_s * turn_s).astype(jnp.bfloat16)
            imag = (base_c * turn_s + base_s * turn_c).astype(jnp.bfloat16)
            both = jnp.concatenate([real, imag], axis=1)
            part = jnp.dot(block, both, preferred_element_type=jnp.float32)
            acc_ref[:fields, cut] += part[:, :128]
            acc_ref[fields:, cut] += part[:, 128:]

    wave = lax.broadcasted_iota(jnp.int32, acc_ref.shape, 1)
    coefs = jnp.where(wave < points // 2, acc_ref[...], 0.0).astype(jnp.bfloat16)
    padded = mine_ref.shape[1]

    def fill(other):
        held = slots_ref[pl.ds(pl.multiple_of(other * padded, 16), padded)]
        pick = held == lax.broadcasted_iota(jnp.int32, (padded, waves), 1)
        pick = jnp.where(pick, 1.0, 0.0).astype(jnp.bfloat16)
        mine_ref[other] = lax.dot_general(
            pick, coefs, (((1,), (1,)), ((), ())), preferred_element_type=jnp.float32
        ).astype(jnp.bfloat16)

    @pl.loop(1, lat_count)
    def _(step):
        fill((lat + step) % lat_count)
        lat_copy(step).start()

    fill(lat)
    own_coefs = pltpu.make_async_copy(mine_ref.at[lat], coef_out.at[group, lat], local_sem.at[1])
    own_coefs.start()
    own_coefs.wait()

    @pl.loop(1, lat_count)
    def _(step):
        lat_copy(step).wait_recv()

    @pl.loop(1, sec_count)
    def _(step):
        sec_copy(step).start()

    @pl.loop(1, col_count)
    def _(step):
        col_copy(0, step).start()

    @pl.loop(1, sec_count)
    def _(back):
        sec_copy(back).wait_recv()

        @pl.loop(1, col_count)
        def _(step):
            col_copy(back, step).start()

    @pl.when(has_next)
    def _():
        halo_copy(0).wait_send()
        halo_copy(1).wait_recv()

    @pl.when(has_previous)
    def _():
        halo_copy(1).wait_send()
        halo_copy(0).wait_recv()

    own_weights.wait()

    @pl.loop(1, groups)
    def _(step):
        weight_copy(step).wait()

    @pl.loop(1, lat_count)
    def _(step):
        lat_copy(step).wait_send()

    @pl.loop(1, sec_count)
    def _(step):
        sec_copy(step).wait_send()

    @pl.loop(0, sec_count)
    def _(back):
        @pl.loop(1, col_count)
        def _(step):
            col_copy(back, step).wait()


def exchange(sizes, points, table, slots, state, weights, halo):
    fields, width = state.shape
    waves = table.shape[2]
    sec_count, lat_count, col_count = sizes
    groups = sec_count * col_count
    padded = weights.shape[1]
    anywhere = pl.BlockSpec(memory_space=pl.ANY)
    inside = pl.BlockSpec(memory_space=pltpu.VMEM)
    halo_shape = jax.ShapeDtypeStruct(halo.shape, halo.dtype)
    out = pl.pallas_call(
        functools.partial(exchange_kernel, sizes),
        out_shape=[
            jax.ShapeDtypeStruct((groups, lat_count, padded, 2 * fields), jnp.bfloat16),
            jax.ShapeDtypeStruct(weights.shape, jnp.bfloat16),
            halo_shape,
            halo_shape,
        ],
        in_specs=[pl.BlockSpec(memory_space=pltpu.SMEM), inside, inside, inside, anywhere, anywhere],
        out_specs=[anywhere] * 4,
        scratch_shapes=[
            pltpu.VMEM((2, CHUNK, waves), jnp.float32),
            pltpu.VMEM((2 * fields, waves), jnp.float32),
            pltpu.VMEM((lat_count, padded, 2 * fields), jnp.bfloat16),
            pltpu.SemaphoreType.DMA((2,)),
            pltpu.SemaphoreType.DMA((groups,)),
            pltpu.SemaphoreType.DMA((groups,)),
            pltpu.SemaphoreType.DMA((2,)),
            pltpu.SemaphoreType.DMA((2,)),
            pltpu.SemaphoreType.DMA((lat_count,)),
            pltpu.SemaphoreType.DMA((lat_count,)),
            pltpu.SemaphoreType.DMA((sec_count,)),
            pltpu.SemaphoreType.DMA((sec_count,)),
            pltpu.SemaphoreType.DMA((sec_count, col_count)),
            pltpu.SemaphoreType.DMA((sec_count, col_count)),
        ],
        compiler_params=pltpu.CompilerParams(
            vmem_limit_bytes=24 * 2**20, collective_id=0, has_side_effects=True
        ),
        cost_estimate=pl.CostEstimate(
            flops=4 * fields * waves * width, bytes_accessed=8 * 2**20, transcendentals=0
        ),
    )(points, table, slots, state, weights, halo)
    return out


REACH = (-2, -1, 1, 2)


def flux_kernel(sizes, row_ref, out_ref, send_sem, recv_sem):
    sec_count, lat_count, col_count = sizes
    devices = sec_count * lat_count * col_count
    sec, lat, col = (lax.axis_index(name) for name in LINE)
    line = (sec * lat_count + lat) * col_count + col
    places = [place_of((line + devices - step) % devices, lat_count, col_count) for step in REACH]
    barrier = pltpu.get_barrier_semaphore()
    for place in places:
        pl.semaphore_signal(barrier, inc=1, device_id=place, device_id_type=MESH)
    pl.semaphore_wait(barrier, len(REACH))
    copies = [
        pltpu.make_async_remote_copy(
            src_ref=row_ref,
            dst_ref=out_ref.at[k],
            send_sem=send_sem.at[k],
            recv_sem=recv_sem.at[k],
            device_id=place,
            device_id_type=MESH,
        )
        for k, place in enumerate(places)
    ]
    for copy in copies:
        copy.start()
    for copy in copies:
        copy.wait()


def near_rows(sizes, row):
    shape = (8, row.shape[0] // 8)
    out = pl.pallas_call(
        functools.partial(flux_kernel, sizes),
        out_shape=jax.ShapeDtypeStruct((len(REACH),) + shape, row.dtype),
        in_specs=[pl.BlockSpec(memory_space=pltpu.VMEM)],
        out_specs=pl.BlockSpec(memory_space=pltpu.VMEM),
        scratch_shapes=[pltpu.SemaphoreType.DMA((len(REACH),))] * 2,
        compiler_params=pltpu.CompilerParams(
            vmem_limit_bytes=2**20, collective_id=1, has_side_effects=True
        ),
    )(row.reshape(shape))
    return out.reshape(len(REACH), row.shape[0])


def legendre_kernel(degree_ref, slots_ref, weight_ref, coef_ref, out_ref):
    groups, lines, pair, width = coef_ref.shape
    rows = groups * lines
    packed = weight_ref.shape[2]
    degrees = out_ref.shape[1]
    first = degree_ref[0]
    for half in range(pair // 8):
        cut = slice(half * 8, half * 8 + 8)
        held = weight_ref[:, cut, :].astype(jnp.float32).reshape(groups * 8, packed)
        parts = [
            pltpu.roll(held, (packed - q * degrees) % packed, 1)[:, :128] if q else held[:, :128]
            for q in range(lines)
        ]
        values = jnp.concatenate(parts, axis=0).T[:degrees]
        lane_slot = lax.broadcasted_iota(jnp.int32, (degrees, rows * 8), 1) % 8
        coefs = jnp.concatenate(
            [
                coef_ref[:, q, cut, :].astype(jnp.float32).reshape(groups * 8, width)
                for q in range(lines)
            ],
            axis=0,
        ).astype(jnp.bfloat16)
        degree = first + lax.broadcasted_iota(jnp.int32, (degrees, width), 0)
        for s in range(8):
            wave = slots_ref[pl.program_id(0) * pair + half * 8 + s]
            left = jnp.where(lane_slot == s, values, 0.0).astype(jnp.bfloat16)
            summed = jnp.dot(left, coefs, preferred_element_type=jnp.float32)
            out_ref[half * 8 + s] = jnp.where(degree >= wave, summed, 0.0)


def legendre(weights, coefs, slots, first_degree, slot_count, degrees):
    groups, lines, padded, width = coefs.shape
    rows = groups * lines
    return pl.pallas_call(
        legendre_kernel,
        grid=(padded // SLOT_PAD,),
        out_shape=jax.ShapeDtypeStruct((slot_count, degrees, width), jnp.float32),
        in_specs=[
            pl.BlockSpec(memory_space=pltpu.SMEM),
            pl.BlockSpec(memory_space=pltpu.SMEM),
            pl.BlockSpec((groups, SLOT_PAD, weights.shape[2]), lambda i: (0, i, 0)),
            pl.BlockSpec((groups, lines, SLOT_PAD, width), lambda i: (0, 0, i, 0)),
        ],
        out_specs=pl.BlockSpec((SLOT_PAD, degrees, width), lambda i: (i, 0, 0)),
        compiler_params=pltpu.CompilerParams(vmem_limit_bytes=(8 if rows <= 64 else 32) * 2**20),
        cost_estimate=pl.CostEstimate(
            flops=2 * rows * padded * width * degrees * 8,
            bytes_accessed=4 * slot_count * degrees * width + 4 * rows * padded * width,
            transcendentals=0,
        ),
    )(first_degree, slots, weights, coefs)


def split_two(values):
    top = lax.reduce_precision(values, 8, 7)
    return [top.astype(jnp.bfloat16), (values - top).astype(jnp.bfloat16)]


def pick_points(arrays, index):
    length = arrays[0].shape[0]
    tiles = -(-length // 128)
    matrix = jnp.stack(arrays).reshape(len(arrays), tiles, 128)
    chosen = (jnp.arange(tiles, dtype=jnp.int32)[:, None] == index[None, :] // 128).astype(jnp.bfloat16)
    spread = jnp.einsum("kta,tx->kax", matrix, chosen, preferred_element_type=jnp.float32)
    lane = jnp.arange(128, dtype=jnp.int32)[:, None] == index[None, :] % 128
    return jnp.where(lane[None], spread, 0.0).sum(axis=1)


def advance_coupled_model(
    bordered_array,
    meridian_exchange_factor,
    zonal_exchange_factor,
    depthwise_exchange_factor,
    boundary_warming_term,
):
    centre = bordered_array[:, 1:-1]
    meridional = meridian_exchange_factor[1:] * (
        bordered_array[:, 2:] - centre
    ) - meridian_exchange_factor[:-1] * (centre - bordered_array[:, :-2])
    east_flux = zonal_exchange_factor * (jnp.roll(centre, -1, axis=2) - centre)
    zonal_div = east_flux - jnp.roll(east_flux, 1, axis=2)
    vertical_flux = depthwise_exchange_factor * (centre[1:] - centre[:-1])
    zero_layer = jnp.zeros_like(vertical_flux[:1])
    vertical = jnp.concatenate([vertical_flux, zero_layer], 0) - jnp.concatenate(
        [zero_layer, vertical_flux], 0
    )
    forced = jnp.concatenate([boundary_warming_term[None], jnp.zeros_like(centre[1:])], 0)
    return centre + meridional + zonal_div + vertical + forced


def body(
    physical_state,
    parallel_lengths,
    zonal_mode_assignment,
    weighted_associated_polynomials,
    marine_tracer_state,
    lateral_diffusivity,
    depthwise_diffusivity,
    water_indicator,
    overlying_parallel,
    underlying_marine_parallel,
):
    lat_count = lax.axis_size("lat")
    groups = lax.axis_size("sec") * lax.axis_size("col")
    devices = groups * lat_count
    grid_width = physical_state.shape[2]
    strata = physical_state.shape[1] // 4
    slot_count, wave_count, row_count = weighted_associated_polynomials.shape
    block_degrees = wave_count // groups
    padded = -(-slot_count // SLOT_PAD) * SLOT_PAD
    linear_index = (
        lax.axis_index("sec") * lat_count + lax.axis_index("lat")
    ) * lax.axis_size("col") + lax.axis_index("col")
    group_index = lax.axis_index("sec") * lax.axis_size("col") + lax.axis_index("col")
    points = parallel_lengths[0]

    rows = marine_tracer_state.shape[1]
    span = marine_tracer_state.shape[2]
    layers = marine_tracer_state.shape[0]
    relative = overlying_parallel - linear_index
    payload = jnp.concatenate(
        [
            marine_tracer_state,
            lateral_diffusivity[None],
            depthwise_diffusivity[None],
            water_indicator.astype(jnp.float32)[None],
            jnp.broadcast_to(relative.astype(jnp.float32)[:, None], (rows, span))[None],
        ],
        axis=0,
    )
    halo = payload.astype(jnp.bfloat16).reshape((layers + 4) * rows, span)

    send = weighted_associated_polynomials.reshape(slot_count, groups, block_degrees, row_count)
    send = jnp.transpose(send, (1, 0, 3, 2)).reshape(groups, slot_count, row_count * block_degrees)
    lanes = -(-send.shape[2] // 128) * 128
    send = jnp.pad(send, ((0, 0), (0, padded - slot_count), (0, lanes - send.shape[2])))
    slots = zonal_mode_assignment.reshape(lat_count, slot_count)
    slots = jnp.pad(slots, ((0, 0), (0, padded - slot_count)), constant_values=wave_count)
    coefs, weights, before, after = exchange(
        (lax.axis_size("sec"), lat_count, lax.axis_size("col")),
        parallel_lengths,
        angle_tables(points, wave_count, grid_width),
        slots.reshape(-1, 1),
        physical_state[0],
        send,
        halo,
    )
    first, last = linear_index == 0, linear_index == devices - 1
    before = jnp.where(first, jnp.zeros_like(before), before).astype(jnp.float32)
    after = jnp.where(last, jnp.zeros_like(after), after).astype(jnp.float32)
    before = before.reshape(payload.shape)
    after = after.reshape(payload.shape)

    surface = jnp.concatenate([before[0], marine_tracer_state[0], after[0]], axis=0)
    under = underlying_marine_parallel[0] - (linear_index - 1) * rows
    skin = jnp.where(jnp.arange(3 * rows)[:, None] == under, surface, 0.0).sum(axis=0)
    ocean_points = jnp.arange(span, dtype=jnp.int32)
    column = ocean_points * points // span
    sea_column = jnp.minimum(column * span // points, span - 1)
    skin_hi, skin_lo = split_two(skin)
    mapped = pick_points([skin_hi, skin_lo], sea_column)
    bottom = strata - 1
    zonal_wind = physical_state[0, bottom].astype(jnp.float32)
    meridional_wind = physical_state[0, strata + bottom].astype(jnp.float32)
    speed = thermal_transfer_factor * jnp.sqrt(
        zonal_wind * zonal_wind + meridional_wind * meridional_wind + 1.0
    )
    speed_hi, speed_lo = split_two(speed)
    picked = pick_points([speed_hi, speed_lo, physical_state[0, 2 * strata + bottom]], column)
    flux = (picked[0] + picked[1]) * (mapped[0] + mapped[1] - picked[2])
    near = near_rows((lax.axis_size("sec"), lat_count, lax.axis_size("col")), flux)
    flux_near = {0: flux, **{step: near[k] for k, step in enumerate(REACH)}}

    whole = jnp.concatenate([before, payload, after], axis=1)
    thermal = whole[:layers]
    kappa, depth, sea, relative = (whole[layers + k] for k in range(4))
    owner = jnp.arange(3 * rows, dtype=jnp.int32)[:, None] // rows - 1
    target = relative + owner.astype(jnp.float32)
    forcing = jnp.zeros_like(sea)
    for step, row in flux_near.items():
        forcing = jnp.where(target == step, row[None], forcing)
    source = force_coef * sea * forcing
    depthwise = depth * sea
    faces = 0.5 * (kappa[:-1] + kappa[1:]) * sea[:-1] * sea[1:]
    east = 0.5 * (kappa + jnp.roll(kappa, -1, axis=1)) * sea * jnp.roll(sea, -1, axis=1)
    total = 3 * rows
    for iteration in range(OSTEPS):
        a, b = iteration + 1, total - iteration - 1
        thermal = advance_coupled_model(
            thermal, faces[a - 1 : b], east[a:b], depthwise[a:b], source[a:b]
        )

    own_waves = lax.dynamic_slice_in_dim(
        slots.reshape(-1), lax.axis_index("lat") * padded, padded
    )
    first_degree = jnp.reshape(group_index * block_degrees, (1,)).astype(jnp.int32)
    harmonic = legendre(weights, coefs, own_waves, first_degree, slot_count, block_degrees)
    return (jnp.transpose(harmonic, (1, 0, 2)), thermal)


def fast_kernel(
    sizes,
    points_hbm,
    over_hbm,
    under_hbm,
    slots_hbm,
    x_hbm,
    weight_ref,
    kappa_ref,
    depth_ref,
    water_ref,
    ocean_ref,
    coef_out,
    weight_out,
    thermal_out,
    points_ref,
    over_ref,
    under_ref,
    slots_ref,
    x_ref,
    table_ref,
    strip_ref,
    msg_ref,
    base_ref,
    xm_ref,
    z_ref,
    coefs_ref,
    mine_ref,
    halo_ref,
    before_ref,
    after_ref,
    plane_ref,
    heat_ref,
    face_ref,
    east_ref,
    down_ref,
    source_ref,
    local_ref,
    flux_ref,
    input_sem,
    ocean_sem,
    local_sem,
    weight_send,
    weight_recv,
    halo_send,
    halo_recv,
    flux_send,
    flux_recv,
    lat_send,
    lat_recv,
    direct_send,
    direct_recv,
    diag_send,
    diag_recv,
    chip_send,
    chip_recv,
):
    sec_count, lat_count, col_count = sizes
    groups = sec_count * col_count
    devices = groups * lat_count
    sec, lat, col = (lax.axis_index(name) for name in LINE)
    group = sec * col_count + col
    line = (sec * lat_count + lat) * col_count + col
    rows, layers, span = thermal_out.shape
    following = place_of((line + 1) % devices, lat_count, col_count)
    previous = place_of((line + devices - 1) % devices, lat_count, col_count)
    has_next, has_previous = line < devices - 1, line > 0
    sides = (sec + 1 - 2 * (sec % 2), (sec + 2) % 4)
    corner = 3 - sec

    ocean_copies = [
        pltpu.make_async_copy(ocean_ref.at[:, r, :], heat_ref.at[0, rows + r], ocean_sem.at[r])
        for r in range(rows)
    ]
    inputs = [
        pltpu.make_async_copy(source, target, input_sem.at[k])
        for k, (source, target) in enumerate(
            (
                (points_hbm, points_ref),
                (over_hbm, over_ref),
                (under_hbm, under_ref),
                (slots_hbm, slots_ref),
                (x_hbm, x_ref),
            )
        )
    ]
    for copy in ocean_copies + inputs:
        copy.start()

    def group_place(step):
        bit0 = (group % 2 + step % 2) % 2
        bit1 = (group // 2 % 2 + step // 2 % 2) % 2
        bit2 = (group // 4 + step // 4) % 2
        other = 4 * bit2 + 2 * bit1 + bit0
        return other, {"sec": other // col_count, "lat": lat, "col": other % col_count}

    def lat_place(step):
        other = (lat + step) % lat_count
        return other, {"sec": sec, "lat": other, "col": col}

    flux_places = [place_of((line + devices - step) % devices, lat_count, col_count) for step in REACH]
    barrier = pltpu.get_barrier_semaphore()
    for place in flux_places:
        pl.semaphore_signal(barrier, inc=1, device_id=place, device_id_type=MESH)

    @pl.loop(1, groups)
    def _(step):
        pl.semaphore_signal(barrier, inc=1, device_id=group_place(step)[1], device_id_type=MESH)

    @pl.loop(1, lat_count)
    def _(step):
        pl.semaphore_signal(barrier, inc=1, device_id=lat_place(step)[1], device_id_type=MESH)

    def weight_copy(step):
        other, place = group_place(step)
        return pltpu.make_async_remote_copy(
            src_ref=msg_ref.at[other],
            dst_ref=weight_out.at[group],
            send_sem=weight_send.at[step],
            recv_sem=weight_recv.at[step],
            device_id=place,
            device_id_type=MESH,
        )

    def halo_copy(side):
        return pltpu.make_async_remote_copy(
            src_ref=halo_ref,
            dst_ref=(before_ref, after_ref)[side],
            send_sem=halo_send.at[side],
            recv_sem=halo_recv.at[side],
            device_id=(following, previous)[side],
            device_id_type=MESH,
        )

    def flux_copy(k):
        return pltpu.make_async_remote_copy(
            src_ref=flux_ref.at[len(REACH)],
            dst_ref=flux_ref.at[k],
            send_sem=flux_send.at[k],
            recv_sem=flux_recv.at[k],
            device_id=flux_places[k],
            device_id_type=MESH,
        )

    def lat_copy(step):
        other, place = lat_place(step)
        return pltpu.make_async_remote_copy(
            src_ref=mine_ref.at[other],
            dst_ref=coef_out.at[group, lat],
            send_sem=lat_send.at[step],
            recv_sem=lat_recv.at[step],
            device_id=place,
            device_id_type=MESH,
        )

    def direct_copy(side, line_row):
        piece = coef_out.at[group, line_row]
        return pltpu.make_async_remote_copy(
            src_ref=piece,
            dst_ref=piece,
            send_sem=direct_send.at[side, line_row],
            recv_sem=direct_recv.at[side, line_row],
            device_id={"sec": sides[side], "lat": lat, "col": col},
            device_id_type=MESH,
        )

    def diag_copy(side, line_row):
        piece = coef_out.at[sides[side] * col_count + col, line_row]
        return pltpu.make_async_remote_copy(
            src_ref=piece,
            dst_ref=piece,
            send_sem=diag_send.at[line_row],
            recv_sem=diag_recv.at[line_row],
            device_id={"sec": sides[1 - side], "lat": lat, "col": col},
            device_id_type=MESH,
        )

    def chip_copy(which, line_row):
        origin = (sec, sides[0], sides[1], corner)[which]
        piece = coef_out.at[origin * col_count + col, line_row]
        return pltpu.make_async_remote_copy(
            src_ref=piece,
            dst_ref=piece,
            send_sem=chip_send.at[which, line_row],
            recv_sem=chip_recv.at[which, line_row],
            device_id={"sec": sec, "lat": lat, "col": 1 - col},
            device_id_type=MESH,
        )

    band = msg_ref.shape[1]
    degrees = msg_ref.shape[2] // groups
    halves = weight_ref.shape[1] // band
    for g in range(groups):
        for p in range(groups):
            t, h = p // halves, p % halves
            msg_ref[g, :, p * degrees : (p + 1) * degrees] = weight_ref[
                t, h * band : (h + 1) * band, g * degrees : (g + 1) * degrees
            ]

    for copy in inputs[:-1] + ocean_copies:
        copy.wait()
    sea = water_ref[...].astype(jnp.float32)
    plane_ref[:rows] = kappa_ref[...] * sea
    plane_ref[rows:] = depth_ref[...] * sea
    deep = rows * layers
    part = span // 2
    for side in range(2):
        cut = slice(side * part, side * part + part)
        for r in range(0, rows, 2):
            pair = jnp.concatenate(
                [heat_ref[0, rows + r, :, cut], heat_ref[0, rows + r + 1, :, cut]], axis=0
            )
            first = side * deep + r * layers
            halo_ref[first : first + 2 * layers] = pair.astype(jnp.bfloat16)
    halo_ref[2 * deep :] = jnp.concatenate(
        [plane_ref[:, :part], plane_ref[:, part:]], axis=0
    ).astype(jnp.bfloat16)

    pl.semaphore_wait(barrier, len(REACH) + groups - 1 + lat_count - 1)

    @pl.when(has_next)
    def _():
        halo_copy(0).start()

    @pl.when(has_previous)
    def _():
        halo_copy(1).start()

    @pl.loop(1, 7)
    def _(step):
        weight_copy(step).start()

    own_weights = pltpu.make_async_copy(msg_ref.at[group], weight_out.at[group], local_sem.at[0])
    own_weights.start()

    points = points_ref[0]
    waves = table_ref.shape[2]
    fields = x_ref.shape[0]
    chunks = x_ref.shape[1] // CHUNK
    top = LOW + CHUNK // LOW
    shape = table_ref.shape[1:]
    place = lax.broadcasted_iota(jnp.int32, shape, 0)
    place = jnp.where(
        place < LOW, place, jnp.where(place < top, (place - LOW) * LOW, (place - top) * CHUNK)
    )
    product = place.astype(jnp.float32) * lax.broadcasted_iota(jnp.int32, shape, 1).astype(jnp.float32)
    count = jnp.full(shape, points, jnp.int32).astype(jnp.float32)
    angle = (product - jnp.round(product / count) * count) * (two_pi / count)
    scale = jnp.where(lax.broadcasted_iota(jnp.int32, shape, 0) >= top, 1.0 / jnp.sqrt(count), 1.0)
    table_ref[0] = jnp.cos(angle) * scale
    table_ref[1] = -jnp.sin(angle) * scale
    low_c, low_s = table_ref[0, :LOW], table_ref[1, :LOW]
    for w in range(waves // 128):
        cut = slice(w * 128, w * 128 + 128)
        for b in range(0, CHUNK // LOW, 2):
            real, imag = [], []
            for q in (b, b + 1):
                mid_c = table_ref[0, LOW + q : LOW + q + 1, cut]
                mid_s = table_ref[1, LOW + q : LOW + q + 1, cut]
                real.append(low_c[:, cut] * mid_c - low_s[:, cut] * mid_s)
                imag.append(low_c[:, cut] * mid_s + low_s[:, cut] * mid_c)
            real = jnp.concatenate(real, axis=0).astype(jnp.bfloat16)
            imag = jnp.concatenate(imag, axis=0).astype(jnp.bfloat16)
            base_ref[w, b * LOW : (b + 2) * LOW, :128] = real
            base_ref[w, b * LOW : (b + 2) * LOW, 128:] = imag
    inputs[-1].wait()
    for a in range(chunks):
        position = a * CHUNK + lax.broadcasted_iota(jnp.int32, (fields, CHUNK), 1)
        block = x_ref[:, a * CHUNK : (a + 1) * CHUNK].astype(jnp.float32)
        xm_ref[a * fields : (a + 1) * fields] = jnp.where(position < points, block, 0.0).astype(
            jnp.bfloat16
        )
    for w in range(waves // 128):
        cut = slice(w * 128, w * 128 + 128)
        z_ref[...] = jnp.dot(xm_ref[...], base_ref[w], preferred_element_type=jnp.float32)
        real = jnp.zeros((fields, 128), jnp.float32)
        imag = jnp.zeros((fields, 128), jnp.float32)
        for a in range(chunks):
            turn_c = table_ref[0, top + a : top + a + 1, cut]
            turn_s = table_ref[1, top + a : top + a + 1, cut]
            part_r = z_ref[a * fields : (a + 1) * fields, :128]
            part_i = z_ref[a * fields : (a + 1) * fields, 128:]
            real = real + part_r * turn_c - part_i * turn_s
            imag = imag + part_r * turn_s + part_i * turn_c
        wave = w * 128 + lax.broadcasted_iota(jnp.int32, (fields, 128), 1)
        kept = wave < points // 2
        coefs_ref[:fields, cut] = jnp.where(kept, real, 0.0).astype(jnp.bfloat16)
        coefs_ref[fields:, cut] = jnp.where(kept, imag, 0.0).astype(jnp.bfloat16)
    padded = mine_ref.shape[1]

    slot_total = slots_ref.shape[0]
    slot_count = slot_total // lat_count
    ring = strip_ref.shape[1]
    lanes = -(-padded // 128) * 128
    strip_ref[...] = jnp.full_like(strip_ref, waves)
    strip_ref[0:1, :slot_total] = slots_ref[...].reshape(1, slot_total)

    def fill(other):
        held = pltpu.roll(strip_ref[...], ring - other * slot_count, 1)[0:1, :lanes]
        held = jnp.where(lax.broadcasted_iota(jnp.int32, (1, lanes), 1) < slot_count, held, waves)
        pick = held == lax.broadcasted_iota(jnp.int32, (waves, lanes), 0)
        pick = jnp.where(pick, 1.0, 0.0).astype(jnp.bfloat16)
        chosen = jnp.dot(coefs_ref[...], pick, preferred_element_type=jnp.float32)
        mine_ref[other] = chosen.T[:padded].astype(jnp.bfloat16)

    @pl.loop(1, lat_count)
    def _(step):
        fill((lat + step) % lat_count)
        lat_copy(step).start()

    fill(lat)
    own_coefs = pltpu.make_async_copy(mine_ref.at[lat], coef_out.at[group, lat], local_sem.at[1])
    own_coefs.start()

    def spread_piece(line_row):
        direct_copy(0, line_row).start()
        direct_copy(1, line_row).start()
        chip_copy(0, line_row).start()

    own_coefs.wait()
    spread_piece(lat)

    strata = fields // 4
    bottom = strata - 1
    wide = 512
    shift = span.bit_length() - 1

    def columns_of(start):
        place = start + lax.broadcasted_iota(jnp.int32, (1, wide), 1)
        return lax.shift_right_logical(place * points, shift)

    def pick(table, index):
        tiles = table.shape[1]
        one = lax.broadcasted_iota(jnp.int32, (tiles, wide), 0) == lax.shift_right_logical(index, 7)
        one = jnp.where(one, 1.0, 0.0).astype(jnp.bfloat16)
        lane = lax.broadcasted_iota(jnp.int32, (128, wide), 0) == (index & 127)
        spread = jnp.dot(table, one, preferred_element_type=jnp.float32)
        return [
            jnp.sum(jnp.where(lane, spread[k * 128 : (k + 1) * 128], 0.0), axis=0, keepdims=True)
            for k in range(table.shape[0] // 128)
        ]

    def table_of(values):
        tiles = values[0].shape[1] // 128
        return jnp.concatenate([v.reshape(tiles, 128).T for v in values], axis=0).astype(jnp.bfloat16)

    zonal = x_ref[bottom : bottom + 1].astype(jnp.float32)
    meridional = x_ref[strata + bottom : strata + bottom + 1].astype(jnp.float32)
    air = x_ref[2 * strata + bottom : 2 * strata + bottom + 1].astype(jnp.float32)
    speed = thermal_transfer_factor * jnp.sqrt(zonal * zonal + meridional * meridional + 1.0)
    table = table_of([speed, air])

    @pl.loop(0, span // wide)
    def _(k):
        start = pl.multiple_of(k * wide, wide)
        brisk, below = pick(table, columns_of(start))
        local_ref[0:1, pl.ds(start, wide)] = brisk
        local_ref[1:2, pl.ds(start, wide)] = below

    @pl.when(has_next)
    def _():
        halo_copy(0).wait_send()
        halo_copy(1).wait_recv()

    @pl.when(has_previous)
    def _():
        halo_copy(1).wait_send()
        halo_copy(0).wait_recv()

    @pl.when(jnp.logical_not(has_next))
    def _():
        after_ref[...] = jnp.zeros_like(after_ref)

    @pl.when(jnp.logical_not(has_previous))
    def _():
        before_ref[...] = jnp.zeros_like(before_ref)

    for start, held in ((0, before_ref), (2 * rows, after_ref)):
        for side in range(2):
            for r in range(0, rows, 2):
                first = side * deep + r * layers
                pair = held[first : first + 2 * layers].astype(jnp.float32)
                cut = slice(side * part, side * part + part)
                heat_ref[0, start + r, :, cut] = pair[:layers]
                heat_ref[0, start + r + 1, :, cut] = pair[layers:]

    under = under_ref[0] - (line - 1) * rows
    skin = jnp.zeros((1, span), jnp.float32)
    for r in range(3 * rows):
        skin = jnp.where(under == r, heat_ref[0, r, 0:1, :], skin)
    skin_table = table_of([skin])
    inverse = 1.0 / jnp.full((1, wide), points, jnp.int32).astype(jnp.float32)

    @pl.loop(0, span // wide)
    def _(k):
        start = pl.multiple_of(k * wide, wide)
        scaled = columns_of(start) << shift
        index = (scaled.astype(jnp.float32) * inverse).astype(jnp.int32)
        rest = scaled - index * points
        index = jnp.where(rest < 0, index - 1, jnp.where(rest >= points, index + 1, index))
        index = jnp.minimum(index, span - 1)
        (mapped,) = pick(skin_table, index)
        cut = pl.ds(start, wide)
        flux_ref[len(REACH), 0:1, cut] = local_ref[0:1, cut] * (mapped - local_ref[1:2, cut])

    lane = lax.broadcasted_iota(jnp.int32, (1, 128), 1)
    relative = jnp.zeros((1, 128), jnp.float32)
    for r in range(rows):
        relative = jnp.where(lane == r, (over_ref[r] - line).astype(jnp.float32), relative)
    flux_ref[len(REACH), 0:1, span:] = relative
    for k in range(len(REACH)):
        flux_copy(k).start()

    @pl.loop(1, lat_count)
    def _(step):
        lat_copy(step).wait_recv()
        spread_piece((lat + lat_count - step) % lat_count)

    weight_copy(7).start()

    edges = []
    for held in (before_ref, after_ref):
        coarse = held[2 * deep :].astype(jnp.float32)
        edges.append(jnp.concatenate([coarse[: 2 * rows], coarse[2 * rows :]], axis=1))
    kappa = jnp.concatenate([edges[0][:rows], plane_ref[:rows], edges[1][:rows]], axis=0)
    depth = jnp.concatenate([edges[0][rows:], plane_ref[rows:], edges[1][rows:]], axis=0)
    total = 3 * rows
    layer = lax.broadcasted_iota(jnp.int32, (layers, span), 0)
    beside = pltpu.roll(kappa, span - 1, 1)
    east = jnp.where((kappa > 0.0) & (beside > 0.0), 0.5 * (kappa + beside), 0.0)
    upper, lower = kappa[:-1], kappa[1:]
    faces = jnp.where((upper > 0.0) & (lower > 0.0), 0.5 * (upper + lower), 0.0)
    for r in range(1, total):
        face_ref[r] = jnp.broadcast_to(faces[r - 1 : r], (layers, span))
    for r in range(1, total - 1):
        east_ref[r] = jnp.broadcast_to(east[r : r + 1], (layers, span))
        down_ref[r] = jnp.where(layer < layers - 1, depth[r : r + 1], 0.0)

    for k in range(len(REACH)):
        flux_copy(k).wait()
    near = REACH + (0,)
    for r in range(1, total - 1):
        owner = r // rows - 1
        target = flux_ref[near.index(owner), 0:1, span + r % rows : span + r % rows + 1] + float(owner)
        row = jnp.zeros((1, span), jnp.float32)
        for k, step in enumerate(near):
            row = jnp.where(target == float(step), flux_ref[k, 0:1, :span], row)
        row = jnp.where(kappa[r : r + 1] > 0.0, force_coef * row, 0.0)
        source_ref[r] = jnp.where(layer == 0, row, 0.0)

    def ocean_step(step):
        held, made = step % 2, (step + 1) % 2

        @pl.loop(step + 1, total - step - 1)
        def _(r):
            mid = heat_ref[held, r]
            flow = face_ref[r + 1] * (heat_ref[held, r + 1] - mid) - face_ref[r] * (mid - heat_ref[held, r - 1])
            lateral = east_ref[r] * (pltpu.roll(mid, span - 1, 1) - mid)
            flow = flow + (lateral - pltpu.roll(lateral, 1, 1))
            sinking = down_ref[r] * (pltpu.roll(mid, layers - 1, 0) - mid)
            flow = flow + (sinking - pltpu.roll(sinking, 1, 0))
            fresh = mid + flow + source_ref[r]
            if step < OSTEPS - 1:
                heat_ref[made, r] = fresh
            else:
                thermal_out[r - rows] = fresh

    def forward(step):
        line_row = (lat + lat_count - step) % lat_count
        direct_copy(0, line_row).wait_recv()

        @pl.when(line_row % 2 == 0)
        def _():
            diag_copy(0, line_row).start()

        chip_copy(1, line_row).start()
        direct_copy(1, line_row).wait_recv()

        @pl.when(line_row % 2 == 1)
        def _():
            diag_copy(1, line_row).start()

        chip_copy(2, line_row).start()

    ocean_step(0)
    forward(0)
    forward(1)
    ocean_step(1)
    forward(2)
    forward(3)

    ocean_step(2)
    ocean_step(3)

    @pl.loop(0, lat_count)
    def _(step):
        line_row = (lat + lat_count - step) % lat_count
        diag_copy(0, line_row).wait_recv()
        chip_copy(3, line_row).start()

    own_weights.wait()

    @pl.loop(1, lat_count)
    def _(step):
        lat_copy(step).wait_send()

    @pl.loop(0, lat_count)
    def _(line_row):
        direct_copy(0, line_row).wait_send()
        direct_copy(1, line_row).wait_send()
        diag_copy(0, line_row).wait_send()
        for which in range(4):
            chip_copy(which, line_row).wait_send()

    @pl.loop(1, groups)
    def _(step):
        weight_copy(step).wait()

    @pl.loop(0, lat_count)
    def _(line_row):
        for which in range(4):
            chip_copy(which, line_row).wait_recv()


def fast_exchange(sizes, points, over, under, slots, state, weights, kappa, depth, water, ocean):
    sec_count, lat_count, col_count = sizes
    groups = sec_count * col_count
    fields, width = state.shape
    waves = weights.shape[2]
    table_rows = -(-(LOW + CHUNK // LOW + width // CHUNK) // 8) * 8
    layers, rows, span = ocean.shape
    padded = weights.shape[1]
    band = lat_count * padded // groups
    chunks = width // CHUNK
    halo_rows = 2 * rows * (layers + 2)
    inside = pl.BlockSpec(memory_space=pltpu.VMEM)
    outside = pl.BlockSpec(memory_space=pl.ANY)
    near = len(REACH)
    dma = pltpu.SemaphoreType.DMA
    return pl.pallas_call(
        functools.partial(fast_kernel, sizes),
        out_shape=[
            jax.ShapeDtypeStruct((groups, lat_count, padded, 2 * fields), jnp.bfloat16),
            jax.ShapeDtypeStruct((groups, band, waves), jnp.bfloat16),
            jax.ShapeDtypeStruct((rows, layers, span), jnp.float32),
        ],
        in_specs=[outside] * 5 + [inside] * 4 + [outside],
        out_specs=[inside] * 3,
        scratch_shapes=[
            pltpu.SMEM(points.shape, jnp.int32),
            pltpu.SMEM(over.shape, jnp.int32),
            pltpu.SMEM(under.shape, jnp.int32),
            pltpu.VMEM(slots.shape, jnp.int32),
            pltpu.VMEM(state.shape, state.dtype),
            pltpu.VMEM((2, table_rows, waves), jnp.float32),
            pltpu.VMEM((8, -(-(slots.shape[0] + 256) // 128) * 128), jnp.int32),
            pltpu.VMEM((groups, band, waves), jnp.bfloat16),
            pltpu.VMEM((waves // 128, CHUNK, 256), jnp.bfloat16),
            pltpu.VMEM((chunks * fields, CHUNK), jnp.bfloat16),
            pltpu.VMEM((chunks * fields, 256), jnp.float32),
            pltpu.VMEM((2 * fields, waves), jnp.bfloat16),
            pltpu.VMEM((lat_count, padded, 2 * fields), jnp.bfloat16),
            pltpu.VMEM((halo_rows, span // 2), jnp.bfloat16),
            pltpu.VMEM((halo_rows, span // 2), jnp.bfloat16),
            pltpu.VMEM((halo_rows, span // 2), jnp.bfloat16),
            pltpu.VMEM((2 * rows, span), jnp.float32),
            pltpu.VMEM((2, 3 * rows, layers, span), jnp.float32),
            pltpu.VMEM((3 * rows, layers, span), jnp.float32),
            pltpu.VMEM((3 * rows, layers, span), jnp.float32),
            pltpu.VMEM((3 * rows, layers, span), jnp.float32),
            pltpu.VMEM((3 * rows, layers, span), jnp.float32),
            pltpu.VMEM((2, span), jnp.float32),
            pltpu.VMEM((near + 1, 1, span + 128), jnp.float32),
            dma((5,)),
            dma((rows,)),
            dma((2,)),
            dma((groups,)),
            dma((groups,)),
            dma((2,)),
            dma((2,)),
            dma((near,)),
            dma((near,)),
            dma((lat_count,)),
            dma((lat_count,)),
            dma((2, lat_count)),
            dma((2, lat_count)),
            dma((lat_count,)),
            dma((lat_count,)),
            dma((4, lat_count)),
            dma((4, lat_count)),
        ],
        compiler_params=pltpu.CompilerParams(
            vmem_limit_bytes=28 * 2**20, collective_id=2, has_side_effects=True
        ),
        cost_estimate=pl.CostEstimate(
            flops=4 * fields * waves * width, bytes_accessed=8 * 2**20, transcendentals=0
        ),
    )(points, over, under, slots, state, weights, kappa, depth, water, ocean)


def fast_legendre_kernel(
    col_count,
    slots_hbm,
    weight_ref,
    coef_ref,
    ocean_ref,
    out_ref,
    ocean_out,
    slots_ref,
    turned_ref,
    made_ref,
    made_sem,
    ocean_sem,
    slots_sem,
):
    groups, lines, padded, width = coef_ref.shape
    slot_count, degrees, _ = out_ref.shape
    rows = ocean_ref.shape[0]
    blocks = padded // 16
    rest = slot_count - (blocks - 1) * 16
    halves = padded // weight_ref.shape[1]
    majors = blocks // halves
    ocean_copies = [
        pltpu.make_async_copy(ocean_ref.at[r], ocean_out.at[:, r, :], ocean_sem.at[r]) for r in range(rows)
    ]
    slots_copy = pltpu.make_async_copy(slots_hbm, slots_ref, slots_sem)
    slots_copy.start()
    for copy in ocean_copies:
        copy.start()
    first_slot = lax.axis_index("lat") * slot_count
    last_slot = slots_ref.shape[0] - 1
    first_degree = (lax.axis_index("sec") * col_count + lax.axis_index("col")) * degrees

    def made_copy(block, count):
        cut = pl.ds(block * 16, count)
        return pltpu.make_async_copy(made_ref.at[cut], out_ref.at[cut], made_sem.at[block])

    degree = first_degree + lax.broadcasted_iota(jnp.int32, (degrees, width), 0)
    odd = lax.broadcasted_iota(jnp.int32, (lines * groups * 16, width), 0) % 2 == 1
    lane_pair = lax.broadcasted_iota(jnp.int32, (degrees, lines * groups * 16), 1) % 16 // 2

    slots_copy.wait()

    for major in range(majors):
        held = weight_ref[:, major * 16 : major * 16 + 16, :]
        turned_ref[major % 2] = held.reshape(groups * 16, held.shape[2]).T
        for half in range(halves):
            block = half * majors + major
            values = jnp.concatenate(
                [
                    turned_ref[major % 2, (t * halves + half) * degrees : (t * halves + half + 1) * degrees, :]
                    for t in range(lines)
                ],
                axis=1,
            )
            cut = slice(block * 16, block * 16 + 16)
            coefs = jnp.concatenate(
                [coef_ref[:, t, cut, :].reshape(groups * 16, width) for t in range(lines)], axis=0
            )
            nothing = jnp.zeros_like(coefs)
            both = jnp.concatenate(
                [jnp.where(odd, nothing, coefs), jnp.where(odd, coefs, nothing)], axis=1
            )
            left = jnp.concatenate(
                [jnp.where(lane_pair == j, values, jnp.zeros_like(values)) for j in range(8)], axis=0
            )
            summed = jnp.dot(left, both, preferred_element_type=jnp.float32)
            for s in range(16):
                wave = slots_ref[jnp.minimum(first_slot + block * 16 + s, last_slot)]
                part = summed[
                    s // 2 * degrees : (s // 2 + 1) * degrees, s % 2 * width : (s % 2 + 1) * width
                ]
                made_ref[block * 16 + s] = jnp.where(degree >= wave, part, 0.0)

            made_copy(block, 16 if block < blocks - 1 else rest).start()

    @pl.loop(0, blocks - 1)
    def _(block):
        made_copy(block, 16).wait()

    made_copy(blocks - 1, rest).wait()
    for copy in ocean_copies:
        copy.wait()


def fast_legendre(col_count, weights, coefs, ocean, slots, slot_count, degrees):
    groups, lines, padded, width = coefs.shape
    rows, layers, span = ocean.shape
    inside = pl.BlockSpec(memory_space=pltpu.VMEM)
    outside = pl.BlockSpec(memory_space=pl.ANY)
    anywhere = pl.BlockSpec(memory_space=pl.ANY)
    return pl.pallas_call(
        functools.partial(fast_legendre_kernel, col_count),
        out_shape=[
            jax.ShapeDtypeStruct((slot_count, degrees, width), jnp.float32),
            jax.ShapeDtypeStruct((layers, rows, span), jnp.float32),
        ],
        in_specs=[outside, inside, inside, inside],
        out_specs=[anywhere, anywhere],
        scratch_shapes=[
            pltpu.SMEM(slots.shape, jnp.int32),
            pltpu.VMEM((2, weights.shape[2], groups * 16), jnp.bfloat16),
            pltpu.VMEM((padded, degrees, width), jnp.float32),
            pltpu.SemaphoreType.DMA((padded // 16,)),
            pltpu.SemaphoreType.DMA((rows,)),
            pltpu.SemaphoreType.DMA,
        ],
        compiler_params=pltpu.CompilerParams(vmem_limit_bytes=32 * 2**20),
        cost_estimate=pl.CostEstimate(
            flops=2 * groups * lines * padded * width * degrees * 8,
            bytes_accessed=4 * slot_count * degrees * width,
            transcendentals=0,
        ),
    )(slots, weights, coefs, ocean)


def fast_body(
    physical_state,
    parallel_lengths,
    zonal_mode_assignment,
    weighted_associated_polynomials,
    marine_tracer_state,
    lateral_diffusivity,
    depthwise_diffusivity,
    water_indicator,
    overlying_parallel,
    underlying_marine_parallel,
):
    sizes = tuple(lax.axis_size(name) for name in LINE)
    sec_count, lat_count, col_count = sizes
    groups = sec_count * col_count
    slot_count, wave_count, _ = weighted_associated_polynomials.shape
    block_degrees = wave_count // groups
    padded = -(-slot_count // 32) * 32
    weights = jnp.transpose(weighted_associated_polynomials, (2, 0, 1))
    weights = jnp.pad(weights, ((0, 0), (0, padded - slot_count), (0, 0)))
    coefs, packed, ocean = fast_exchange(
        sizes,
        parallel_lengths,
        overlying_parallel,
        underlying_marine_parallel,
        zonal_mode_assignment,
        physical_state[0],
        weights,
        lateral_diffusivity,
        depthwise_diffusivity,
        water_indicator,
        marine_tracer_state,
    )
    harmonic, thermal = fast_legendre(
        col_count, packed, coefs, ocean, zonal_mode_assignment, slot_count, block_degrees
    )
    return (jnp.transpose(harmonic, (1, 0, 2)), thermal)


def compact(mesh):
    return mesh.shape["sec"] == 4 and mesh.shape["lat"] == 4 and mesh.shape["col"] == 2


def solution(mesh):
    return jax.shard_map(
        fast_body if compact(mesh) else body,
        mesh=mesh,
        in_specs=(
            P(LINE, None, None),
            P(LINE),
            P(),
            P("lat", None, GROUP),
            P(None, LINE, None),
            P(LINE, None),
            P(LINE, None),
            P(LINE, None),
            P(LINE),
            P(LINE),
        ),
        out_specs=(P(GROUP, "lat", None), P(None, LINE, None)),
        check_vma=False,
    )
```

```python
import functools

import jax
import jax.numpy as jnp
from jax import lax
from jax.experimental import pallas as pl
from jax.experimental.pallas import tpu as pltpu
from jax.sharding import PartitionSpec as P

OSTEPS = 4
LOW = 8
CHUNK = 256
SLOT_PAD = 16

two_pi = 6.283185307179586
thermal_transfer_factor = 0.8
force_coef = 0.1

GROUP = ("sec", "col")
LINE = ("sec", "lat", "col")


def angle_tables(points, wave_count, grid_width):
    low = jnp.arange(LOW, dtype=jnp.float32)
    mid = jnp.arange(CHUNK // LOW, dtype=jnp.float32) * LOW
    high = jnp.arange(grid_width // CHUNK, dtype=jnp.float32) * CHUNK
    place = jnp.concatenate([low, mid, high])
    count = points.astype(jnp.float32)
    product = place[:, None] * jnp.arange(wave_count, dtype=jnp.float32)[None, :]
    residue = product - jnp.round(product / count) * count
    angle = residue * (jnp.float32(two_pi) / count)
    scale = jnp.where(jnp.arange(place.shape[0]) >= LOW + CHUNK // LOW, 1.0 / jnp.sqrt(count), 1.0)
    return jnp.stack([jnp.cos(angle), -jnp.sin(angle)]) * scale[None, :, None]


MESH = pl.DeviceIdType.MESH


def place_of(index, lat_count, col_count):
    return {
        "sec": index // (lat_count * col_count),
        "lat": index // col_count % lat_count,
        "col": index % col_count,
    }


def exchange_kernel(
    sizes,
    points_ref,
    table_ref,
    slots_ref,
    x_ref,
    weight_ref,
    *refs,
):
    sec_count, lat_count, col_count = sizes
    halo, coef_out, weight_out, before, after = refs[:5]
    (base_ref, acc_ref, mine_ref, local_sem, weight_send, weight_recv, halo_send, halo_recv,
     lat_send, lat_recv, sec_send, sec_recv, col_send, col_recv) = refs[5:]
    groups = sec_count * col_count
    devices = groups * lat_count
    sec, lat, col = (lax.axis_index(name) for name in LINE)
    group = sec * col_count + col
    line = (sec * lat_count + lat) * col_count + col
    following = place_of((line + 1) % devices, lat_count, col_count)
    previous = place_of((line + devices - 1) % devices, lat_count, col_count)

    def group_place(step):
        other = (group + step) % groups
        return other, {"sec": other // col_count, "lat": lat, "col": other % col_count}

    def lat_place(step):
        other = (lat + step) % lat_count
        return other, {"sec": sec, "lat": other, "col": col}

    barrier = pltpu.get_barrier_semaphore()
    for place in (following, previous):
        pl.semaphore_signal(barrier, inc=1, device_id=place, device_id_type=MESH)

    @pl.loop(1, groups)
    def _(step):
        pl.semaphore_signal(barrier, inc=1, device_id=group_place(step)[1], device_id_type=MESH)

    @pl.loop(1, lat_count)
    def _(step):
        pl.semaphore_signal(barrier, inc=1, device_id=lat_place(step)[1], device_id_type=MESH)

    pl.semaphore_wait(barrier, groups + lat_count)

    def weight_copy(step):
        other, place = group_place(step)
        return pltpu.make_async_remote_copy(
            src_ref=weight_ref.at[other],
            dst_ref=weight_out.at[group],
            send_sem=weight_send.at[step],
            recv_sem=weight_recv.at[step],
            device_id=place,
            device_id_type=MESH,
        )

    def halo_copy(side):
        return pltpu.make_async_remote_copy(
            src_ref=halo,
            dst_ref=(before, after)[side],
            send_sem=halo_send.at[side],
            recv_sem=halo_recv.at[side],
            device_id=(following, previous)[side],
            device_id_type=MESH,
        )

    has_next, has_previous = line < devices - 1, line > 0

    def lat_copy(step):
        other, place = lat_place(step)
        return pltpu.make_async_remote_copy(
            src_ref=mine_ref.at[other],
            dst_ref=coef_out.at[group, lat],
            send_sem=lat_send.at[step],
            recv_sem=lat_recv.at[step],
            device_id=place,
            device_id_type=MESH,
        )

    def sec_copy(step):
        return pltpu.make_async_remote_copy(
            src_ref=coef_out.at[group],
            dst_ref=coef_out.at[group],
            send_sem=sec_send.at[step],
            recv_sem=sec_recv.at[step],
            device_id={"sec": (sec + step) % sec_count, "lat": lat, "col": col},
            device_id_type=MESH,
        )

    def col_copy(back, step):
        block = (sec + sec_count - back) % sec_count * col_count + col
        return pltpu.make_async_remote_copy(
            src_ref=coef_out.at[block],
            dst_ref=coef_out.at[block],
            send_sem=col_send.at[back, step],
            recv_sem=col_recv.at[back, step],
            device_id={"sec": sec, "lat": lat, "col": (col + step) % col_count},
            device_id_type=MESH,
        )

    own_weights = pltpu.make_async_copy(weight_ref.at[group], weight_out.at[group], local_sem.at[0])
    own_weights.start()

    @pl.loop(1, groups)
    def _(step):
        weight_copy(step).start()

    @pl.when(has_next)
    def _():
        halo_copy(0).start()

    @pl.when(has_previous)
    def _():
        halo_copy(1).start()

    points = points_ref[0]
    waves = table_ref.shape[2]
    fields = x_ref.shape[0]
    chunks = x_ref.shape[1] // CHUNK
    low_c, low_s = table_ref[0, :LOW], table_ref[1, :LOW]
    for b in range(CHUNK // LOW):
        mid_c = table_ref[0, LOW + b : LOW + b + 1]
        mid_s = table_ref[1, LOW + b : LOW + b + 1]
        base_ref[0, b * LOW : (b + 1) * LOW] = low_c * mid_c - low_s * mid_s
        base_ref[1, b * LOW : (b + 1) * LOW] = low_c * mid_s + low_s * mid_c
    acc_ref[...] = jnp.zeros_like(acc_ref)
    top = LOW + CHUNK // LOW

    @pl.loop(0, chunks)
    def _(a):
        start = pl.multiple_of(a * CHUNK, CHUNK)
        position = start + lax.broadcasted_iota(jnp.int32, (fields, CHUNK), 1)
        block = x_ref[:, pl.ds(start, CHUNK)].astype(jnp.float32)
        block = jnp.where(position < points, block, 0.0).astype(jnp.bfloat16)
        high_c = table_ref[0, pl.ds(top + a, 1)]
        high_s = table_ref[1, pl.ds(top + a, 1)]
        for w in range(0, waves, 128):
            cut = slice(w, w + 128)
            base_c, base_s = base_ref[0, :, cut], base_ref[1, :, cut]
            turn_c, turn_s = high_c[:, cut], high_s[:, cut]
            real = (base_c * turn_c - base_s * turn_s).astype(jnp.bfloat16)
            imag = (base_c * turn_s + base_s * turn_c).astype(jnp.bfloat16)
            both = jnp.concatenate([real, imag], axis=1)
            part = jnp.dot(block, both, preferred_element_type=jnp.float32)
            acc_ref[:fields, cut] += part[:, :128]
            acc_ref[fields:, cut] += part[:, 128:]

    wave = lax.broadcasted_iota(jnp.int32, acc_ref.shape, 1)
    coefs = jnp.where(wave < points // 2, acc_ref[...], 0.0).astype(jnp.bfloat16)
    padded = mine_ref.shape[1]

    def fill(other):
        held = slots_ref[pl.ds(pl.multiple_of(other * padded, 16), padded)]
        pick = held == lax.broadcasted_iota(jnp.int32, (padded, waves), 1)
        pick = jnp.where(pick, 1.0, 0.0).astype(jnp.bfloat16)
        mine_ref[other] = lax.dot_general(
            pick, coefs, (((1,), (1,)), ((), ())), preferred_element_type=jnp.float32
        ).astype(jnp.bfloat16)

    @pl.loop(1, lat_count)
    def _(step):
        fill((lat + step) % lat_count)
        lat_copy(step).start()

    fill(lat)
    own_coefs = pltpu.make_async_copy(mine_ref.at[lat], coef_out.at[group, lat], local_sem.at[1])
    own_coefs.start()
    own_coefs.wait()

    @pl.loop(1, lat_count)
    def _(step):
        lat_copy(step).wait_recv()

    @pl.loop(1, sec_count)
    def _(step):
        sec_copy(step).start()

    @pl.loop(1, col_count)
    def _(step):
        col_copy(0, step).start()

    @pl.loop(1, sec_count)
    def _(back):
        sec_copy(back).wait_recv()

        @pl.loop(1, col_count)
        def _(step):
            col_copy(back, step).start()

    @pl.when(has_next)
    def _():
        halo_copy(0).wait_send()
        halo_copy(1).wait_recv()

    @pl.when(has_previous)
    def _():
        halo_copy(1).wait_send()
        halo_copy(0).wait_recv()

    own_weights.wait()

    @pl.loop(1, groups)
    def _(step):
        weight_copy(step).wait()

    @pl.loop(1, lat_count)
    def _(step):
        lat_copy(step).wait_send()

    @pl.loop(1, sec_count)
    def _(step):
        sec_copy(step).wait_send()

    @pl.loop(0, sec_count)
    def _(back):
        @pl.loop(1, col_count)
        def _(step):
            col_copy(back, step).wait()


def exchange(sizes, points, table, slots, state, weights, halo):
    fields, width = state.shape
    waves = table.shape[2]
    sec_count, lat_count, col_count = sizes
    groups = sec_count * col_count
    padded = weights.shape[1]
    anywhere = pl.BlockSpec(memory_space=pl.ANY)
    inside = pl.BlockSpec(memory_space=pltpu.VMEM)
    halo_shape = jax.ShapeDtypeStruct(halo.shape, halo.dtype)
    out = pl.pallas_call(
        functools.partial(exchange_kernel, sizes),
        out_shape=[
            jax.ShapeDtypeStruct((groups, lat_count, padded, 2 * fields), jnp.bfloat16),
            jax.ShapeDtypeStruct(weights.shape, jnp.bfloat16),
            halo_shape,
            halo_shape,
        ],
        in_specs=[pl.BlockSpec(memory_space=pltpu.SMEM), inside, inside, inside, anywhere, anywhere],
        out_specs=[anywhere] * 4,
        scratch_shapes=[
            pltpu.VMEM((2, CHUNK, waves), jnp.float32),
            pltpu.VMEM((2 * fields, waves), jnp.float32),
            pltpu.VMEM((lat_count, padded, 2 * fields), jnp.bfloat16),
            pltpu.SemaphoreType.DMA((2,)),
            pltpu.SemaphoreType.DMA((groups,)),
            pltpu.SemaphoreType.DMA((groups,)),
            pltpu.SemaphoreType.DMA((2,)),
            pltpu.SemaphoreType.DMA((2,)),
            pltpu.SemaphoreType.DMA((lat_count,)),
            pltpu.SemaphoreType.DMA((lat_count,)),
            pltpu.SemaphoreType.DMA((sec_count,)),
            pltpu.SemaphoreType.DMA((sec_count,)),
            pltpu.SemaphoreType.DMA((sec_count, col_count)),
            pltpu.SemaphoreType.DMA((sec_count, col_count)),
        ],
        compiler_params=pltpu.CompilerParams(
            vmem_limit_bytes=24 * 2**20, collective_id=0, has_side_effects=True
        ),
        cost_estimate=pl.CostEstimate(
            flops=4 * fields * waves * width, bytes_accessed=8 * 2**20, transcendentals=0
        ),
    )(points, table, slots, state, weights, halo)
    return out


REACH = (-2, -1, 1, 2)


def flux_kernel(sizes, row_ref, out_ref, send_sem, recv_sem):
    sec_count, lat_count, col_count = sizes
    devices = sec_count * lat_count * col_count
    sec, lat, col = (lax.axis_index(name) for name in LINE)
    line = (sec * lat_count + lat) * col_count + col
    places = [place_of((line + devices - step) % devices, lat_count, col_count) for step in REACH]
    barrier = pltpu.get_barrier_semaphore()
    for place in places:
        pl.semaphore_signal(barrier, inc=1, device_id=place, device_id_type=MESH)
    pl.semaphore_wait(barrier, len(REACH))
    copies = [
        pltpu.make_async_remote_copy(
            src_ref=row_ref,
            dst_ref=out_ref.at[k],
            send_sem=send_sem.at[k],
            recv_sem=recv_sem.at[k],
            device_id=place,
            device_id_type=MESH,
        )
        for k, place in enumerate(places)
    ]
    for copy in copies:
        copy.start()
    for copy in copies:
        copy.wait()


def near_rows(sizes, row):
    shape = (8, row.shape[0] // 8)
    out = pl.pallas_call(
        functools.partial(flux_kernel, sizes),
        out_shape=jax.ShapeDtypeStruct((len(REACH),) + shape, row.dtype),
        in_specs=[pl.BlockSpec(memory_space=pltpu.VMEM)],
        out_specs=pl.BlockSpec(memory_space=pltpu.VMEM),
        scratch_shapes=[pltpu.SemaphoreType.DMA((len(REACH),))] * 2,
        compiler_params=pltpu.CompilerParams(
            vmem_limit_bytes=2**20, collective_id=1, has_side_effects=True
        ),
    )(row.reshape(shape))
    return out.reshape(len(REACH), row.shape[0])


def legendre_kernel(degree_ref, slots_ref, weight_ref, coef_ref, out_ref):
    groups, lines, pair, width = coef_ref.shape
    rows = groups * lines
    packed = weight_ref.shape[2]
    degrees = out_ref.shape[1]
    first = degree_ref[0]
    for half in range(pair // 8):
        cut = slice(half * 8, half * 8 + 8)
        held = weight_ref[:, cut, :].astype(jnp.float32).reshape(groups * 8, packed)
        parts = [
            pltpu.roll(held, (packed - q * degrees) % packed, 1)[:, :128] if q else held[:, :128]
            for q in range(lines)
        ]
        values = jnp.concatenate(parts, axis=0).T[:degrees]
        lane_slot = lax.broadcasted_iota(jnp.int32, (degrees, rows * 8), 1) % 8
        coefs = jnp.concatenate(
            [
                coef_ref[:, q, cut, :].astype(jnp.float32).reshape(groups * 8, width)
                for q in range(lines)
            ],
            axis=0,
        ).astype(jnp.bfloat16)
        degree = first + lax.broadcasted_iota(jnp.int32, (degrees, width), 0)
        for s in range(8):
            wave = slots_ref[pl.program_id(0) * pair + half * 8 + s]
            left = jnp.where(lane_slot == s, values, 0.0).astype(jnp.bfloat16)
            summed = jnp.dot(left, coefs, preferred_element_type=jnp.float32)
            out_ref[half * 8 + s] = jnp.where(degree >= wave, summed, 0.0)


def legendre(weights, coefs, slots, first_degree, slot_count, degrees):
    groups, lines, padded, width = coefs.shape
    rows = groups * lines
    return pl.pallas_call(
        legendre_kernel,
        grid=(padded // SLOT_PAD,),
        out_shape=jax.ShapeDtypeStruct((slot_count, degrees, width), jnp.float32),
        in_specs=[
            pl.BlockSpec(memory_space=pltpu.SMEM),
            pl.BlockSpec(memory_space=pltpu.SMEM),
            pl.BlockSpec((groups, SLOT_PAD, weights.shape[2]), lambda i: (0, i, 0)),
            pl.BlockSpec((groups, lines, SLOT_PAD, width), lambda i: (0, 0, i, 0)),
        ],
        out_specs=pl.BlockSpec((SLOT_PAD, degrees, width), lambda i: (i, 0, 0)),
        compiler_params=pltpu.CompilerParams(vmem_limit_bytes=(8 if rows <= 64 else 32) * 2**20),
        cost_estimate=pl.CostEstimate(
            flops=2 * rows * padded * width * degrees * 8,
            bytes_accessed=4 * slot_count * degrees * width + 4 * rows * padded * width,
            transcendentals=0,
        ),
    )(first_degree, slots, weights, coefs)


def split_two(values):
    top = lax.reduce_precision(values, 8, 7)
    return [top.astype(jnp.bfloat16), (values - top).astype(jnp.bfloat16)]


def pick_points(arrays, index):
    length = arrays[0].shape[0]
    tiles = -(-length // 128)
    matrix = jnp.stack(arrays).reshape(len(arrays), tiles, 128)
    chosen = (jnp.arange(tiles, dtype=jnp.int32)[:, None] == index[None, :] // 128).astype(jnp.bfloat16)
    spread = jnp.einsum("kta,tx->kax", matrix, chosen, preferred_element_type=jnp.float32)
    lane = jnp.arange(128, dtype=jnp.int32)[:, None] == index[None, :] % 128
    return jnp.where(lane[None], spread, 0.0).sum(axis=1)


def advance_coupled_model(
    bordered_array,
    meridian_exchange_factor,
    zonal_exchange_factor,
    depthwise_exchange_factor,
    boundary_warming_term,
):
    centre = bordered_array[:, 1:-1]
    meridional = meridian_exchange_factor[1:] * (
        bordered_array[:, 2:] - centre
    ) - meridian_exchange_factor[:-1] * (centre - bordered_array[:, :-2])
    east_flux = zonal_exchange_factor * (jnp.roll(centre, -1, axis=2) - centre)
    zonal_div = east_flux - jnp.roll(east_flux, 1, axis=2)
    vertical_flux = depthwise_exchange_factor * (centre[1:] - centre[:-1])
    zero_layer = jnp.zeros_like(vertical_flux[:1])
    vertical = jnp.concatenate([vertical_flux, zero_layer], 0) - jnp.concatenate(
        [zero_layer, vertical_flux], 0
    )
    forced = jnp.concatenate([boundary_warming_term[None], jnp.zeros_like(centre[1:])], 0)
    return centre + meridional + zonal_div + vertical + forced


def body(
    physical_state,
    parallel_lengths,
    zonal_mode_assignment,
    weighted_associated_polynomials,
    marine_tracer_state,
    lateral_diffusivity,
    depthwise_diffusivity,
    water_indicator,
    overlying_parallel,
    underlying_marine_parallel,
):
    lat_count = lax.axis_size("lat")
    groups = lax.axis_size("sec") * lax.axis_size("col")
    devices = groups * lat_count
    grid_width = physical_state.shape[2]
    strata = physical_state.shape[1] // 4
    slot_count, wave_count, row_count = weighted_associated_polynomials.shape
    block_degrees = wave_count // groups
    padded = -(-slot_count // SLOT_PAD) * SLOT_PAD
    linear_index = (
        lax.axis_index("sec") * lat_count + lax.axis_index("lat")
    ) * lax.axis_size("col") + lax.axis_index("col")
    group_index = lax.axis_index("sec") * lax.axis_size("col") + lax.axis_index("col")
    points = parallel_lengths[0]

    rows = marine_tracer_state.shape[1]
    span = marine_tracer_state.shape[2]
    layers = marine_tracer_state.shape[0]
    relative = overlying_parallel - linear_index
    payload = jnp.concatenate(
        [
            marine_tracer_state,
            lateral_diffusivity[None],
            depthwise_diffusivity[None],
            water_indicator.astype(jnp.float32)[None],
            jnp.broadcast_to(relative.astype(jnp.float32)[:, None], (rows, span))[None],
        ],
        axis=0,
    )
    halo = payload.astype(jnp.bfloat16).reshape((layers + 4) * rows, span)

    send = weighted_associated_polynomials.reshape(slot_count, groups, block_degrees, row_count)
    send = jnp.transpose(send, (1, 0, 3, 2)).reshape(groups, slot_count, row_count * block_degrees)
    lanes = -(-send.shape[2] // 128) * 128
    send = jnp.pad(send, ((0, 0), (0, padded - slot_count), (0, lanes - send.shape[2])))
    slots = zonal_mode_assignment.reshape(lat_count, slot_count)
    slots = jnp.pad(slots, ((0, 0), (0, padded - slot_count)), constant_values=wave_count)
    coefs, weights, before, after = exchange(
        (lax.axis_size("sec"), lat_count, lax.axis_size("col")),
        parallel_lengths,
        angle_tables(points, wave_count, grid_width),
        slots.reshape(-1, 1),
        physical_state[0],
        send,
        halo,
    )
    first, last = linear_index == 0, linear_index == devices - 1
    before = jnp.where(first, jnp.zeros_like(before), before).astype(jnp.float32)
    after = jnp.where(last, jnp.zeros_like(after), after).astype(jnp.float32)
    before = before.reshape(payload.shape)
    after = after.reshape(payload.shape)

    surface = jnp.concatenate([before[0], marine_tracer_state[0], after[0]], axis=0)
    under = underlying_marine_parallel[0] - (linear_index - 1) * rows
    skin = jnp.where(jnp.arange(3 * rows)[:, None] == under, surface, 0.0).sum(axis=0)
    ocean_points = jnp.arange(span, dtype=jnp.int32)
    column = ocean_points * points // span
    sea_column = jnp.minimum(column * span // points, span - 1)
    skin_hi, skin_lo = split_two(skin)
    mapped = pick_points([skin_hi, skin_lo], sea_column)
    bottom = strata - 1
    zonal_wind = physical_state[0, bottom].astype(jnp.float32)
    meridional_wind = physical_state[0, strata + bottom].astype(jnp.float32)
    speed = thermal_transfer_factor * jnp.sqrt(
        zonal_wind * zonal_wind + meridional_wind * meridional_wind + 1.0
    )
    speed_hi, speed_lo = split_two(speed)
    picked = pick_points([speed_hi, speed_lo, physical_state[0, 2 * strata + bottom]], column)
    flux = (picked[0] + picked[1]) * (mapped[0] + mapped[1] - picked[2])
    near = near_rows((lax.axis_size("sec"), lat_count, lax.axis_size("col")), flux)
    flux_near = {0: flux, **{step: near[k] for k, step in enumerate(REACH)}}

    whole = jnp.concatenate([before, payload, after], axis=1)
    thermal = whole[:layers]
    kappa, depth, sea, relative = (whole[layers + k] for k in range(4))
    owner = jnp.arange(3 * rows, dtype=jnp.int32)[:, None] // rows - 1
    target = relative + owner.astype(jnp.float32)
    forcing = jnp.zeros_like(sea)
    for step, row in flux_near.items():
        forcing = jnp.where(target == step, row[None], forcing)
    source = force_coef * sea * forcing
    depthwise = depth * sea
    faces = 0.5 * (kappa[:-1] + kappa[1:]) * sea[:-1] * sea[1:]
    east = 0.5 * (kappa + jnp.roll(kappa, -1, axis=1)) * sea * jnp.roll(sea, -1, axis=1)
    total = 3 * rows
    for iteration in range(OSTEPS):
        a, b = iteration + 1, total - iteration - 1
        thermal = advance_coupled_model(
            thermal, faces[a - 1 : b], east[a:b], depthwise[a:b], source[a:b]
        )

    own_waves = lax.dynamic_slice_in_dim(
        slots.reshape(-1), lax.axis_index("lat") * padded, padded
    )
    first_degree = jnp.reshape(group_index * block_degrees, (1,)).astype(jnp.int32)
    harmonic = legendre(weights, coefs, own_waves, first_degree, slot_count, block_degrees)
    return (jnp.transpose(harmonic, (1, 0, 2)), thermal)


def fast_kernel(
    sizes,
    points_hbm,
    over_hbm,
    under_hbm,
    slots_hbm,
    x_hbm,
    weight_ref,
    kappa_ref,
    depth_ref,
    water_ref,
    ocean_ref,
    coef_out,
    weight_out,
    thermal_out,
    points_ref,
    over_ref,
    under_ref,
    slots_ref,
    x_ref,
    table_ref,
    strip_ref,
    msg_ref,
    base_ref,
    xm_ref,
    z_ref,
    coefs_ref,
    mine_ref,
    halo_ref,
    before_ref,
    after_ref,
    plane_ref,
    heat_ref,
    face_ref,
    east_ref,
    down_ref,
    source_ref,
    local_ref,
    flux_ref,
    input_sem,
    ocean_sem,
    local_sem,
    weight_send,
    weight_recv,
    halo_send,
    halo_recv,
    flux_send,
    flux_recv,
    lat_send,
    lat_recv,
    direct_send,
    direct_recv,
    diag_send,
    diag_recv,
    chip_send,
    chip_recv,
):
    sec_count, lat_count, col_count = sizes
    groups = sec_count * col_count
    devices = groups * lat_count
    sec, lat, col = (lax.axis_index(name) for name in LINE)
    group = sec * col_count + col
    line = (sec * lat_count + lat) * col_count + col
    rows, layers, span = thermal_out.shape
    following = place_of((line + 1) % devices, lat_count, col_count)
    previous = place_of((line + devices - 1) % devices, lat_count, col_count)
    has_next, has_previous = line < devices - 1, line > 0
    sides = (sec + 1 - 2 * (sec % 2), (sec + 2) % 4)
    corner = 3 - sec

    ocean_copies = [
        pltpu.make_async_copy(ocean_ref.at[:, r, :], heat_ref.at[0, rows + r], ocean_sem.at[r])
        for r in range(rows)
    ]
    inputs = [
        pltpu.make_async_copy(source, target, input_sem.at[k])
        for k, (source, target) in enumerate(
            (
                (points_hbm, points_ref),
                (over_hbm, over_ref),
                (under_hbm, under_ref),
                (slots_hbm, slots_ref),
                (x_hbm, x_ref),
            )
        )
    ]
    for copy in ocean_copies + inputs:
        copy.start()

    def group_place(step):
        bit0 = (group % 2 + step % 2) % 2
        bit1 = (group // 2 % 2 + step // 2 % 2) % 2
        bit2 = (group // 4 + step // 4) % 2
        other = 4 * bit2 + 2 * bit1 + bit0
        return other, {"sec": other // col_count, "lat": lat, "col": other % col_count}

    def lat_place(step):
        other = (lat + step) % lat_count
        return other, {"sec": sec, "lat": other, "col": col}

    flux_places = [place_of((line + devices - step) % devices, lat_count, col_count) for step in REACH]
    barrier = pltpu.get_barrier_semaphore()
    for place in flux_places:
        pl.semaphore_signal(barrier, inc=1, device_id=place, device_id_type=MESH)

    @pl.loop(1, groups)
    def _(step):
        pl.semaphore_signal(barrier, inc=1, device_id=group_place(step)[1], device_id_type=MESH)

    @pl.loop(1, lat_count)
    def _(step):
        pl.semaphore_signal(barrier, inc=1, device_id=lat_place(step)[1], device_id_type=MESH)

    def weight_copy(step):
        other, place = group_place(step)
        return pltpu.make_async_remote_copy(
            src_ref=msg_ref.at[other],
            dst_ref=weight_out.at[group],
            send_sem=weight_send.at[step],
            recv_sem=weight_recv.at[step],
            device_id=place,
            device_id_type=MESH,
        )

    def halo_copy(side):
        return pltpu.make_async_remote_copy(
            src_ref=halo_ref,
            dst_ref=(before_ref, after_ref)[side],
            send_sem=halo_send.at[side],
            recv_sem=halo_recv.at[side],
            device_id=(following, previous)[side],
            device_id_type=MESH,
        )

    def flux_copy(k):
        return pltpu.make_async_remote_copy(
            src_ref=flux_ref.at[len(REACH)],
            dst_ref=flux_ref.at[k],
            send_sem=flux_send.at[k],
            recv_sem=flux_recv.at[k],
            device_id=flux_places[k],
            device_id_type=MESH,
        )

    def lat_copy(step):
        other, place = lat_place(step)
        return pltpu.make_async_remote_copy(
            src_ref=mine_ref.at[other],
            dst_ref=coef_out.at[group, lat],
            send_sem=lat_send.at[step],
            recv_sem=lat_recv.at[step],
            device_id=place,
            device_id_type=MESH,
        )

    def direct_copy(side, line_row):
        piece = coef_out.at[group, line_row]
        return pltpu.make_async_remote_copy(
            src_ref=piece,
            dst_ref=piece,
            send_sem=direct_send.at[side, line_row],
            recv_sem=direct_recv.at[side, line_row],
            device_id={"sec": sides[side], "lat": lat, "col": col},
            device_id_type=MESH,
        )

    def diag_copy(side, line_row):
        piece = coef_out.at[sides[side] * col_count + col, line_row]
        return pltpu.make_async_remote_copy(
            src_ref=piece,
            dst_ref=piece,
            send_sem=diag_send.at[line_row],
            recv_sem=diag_recv.at[line_row],
            device_id={"sec": sides[1 - side], "lat": lat, "col": col},
            device_id_type=MESH,
        )

    def chip_copy(which, line_row):
        origin = (sec, sides[0], sides[1], corner)[which]
        piece = coef_out.at[origin * col_count + col, line_row]
        return pltpu.make_async_remote_copy(
            src_ref=piece,
            dst_ref=piece,
            send_sem=chip_send.at[which, line_row],
            recv_sem=chip_recv.at[which, line_row],
            device_id={"sec": sec, "lat": lat, "col": 1 - col},
            device_id_type=MESH,
        )

    band = msg_ref.shape[1]
    degrees = msg_ref.shape[2] // groups
    halves = weight_ref.shape[1] // band
    for g in range(groups):
        for p in range(groups):
            t, h = p // halves, p % halves
            msg_ref[g, :, p * degrees : (p + 1) * degrees] = weight_ref[
                t, h * band : (h + 1) * band, g * degrees : (g + 1) * degrees
            ]

    for copy in inputs[:-1] + ocean_copies:
        copy.wait()
    sea = water_ref[...].astype(jnp.float32)
    plane_ref[:rows] = kappa_ref[...] * sea
    plane_ref[rows:] = depth_ref[...] * sea
    deep = rows * layers
    part = span // 2
    for side in range(2):
        cut = slice(side * part, side * part + part)
        for r in range(0, rows, 2):
            pair = jnp.concatenate(
                [heat_ref[0, rows + r, :, cut], heat_ref[0, rows + r + 1, :, cut]], axis=0
            )
            first = side * deep + r * layers
            halo_ref[first : first + 2 * layers] = pair.astype(jnp.bfloat16)
    halo_ref[2 * deep :] = jnp.concatenate(
        [plane_ref[:, :part], plane_ref[:, part:]], axis=0
    ).astype(jnp.bfloat16)

    pl.semaphore_wait(barrier, len(REACH) + groups - 1 + lat_count - 1)

    @pl.when(has_next)
    def _():
        halo_copy(0).start()

    @pl.when(has_previous)
    def _():
        halo_copy(1).start()

    @pl.loop(1, 7)
    def _(step):
        weight_copy(step).start()

    own_weights = pltpu.make_async_copy(msg_ref.at[group], weight_out.at[group], local_sem.at[0])
    own_weights.start()

    points = points_ref[0]
    waves = table_ref.shape[2]
    fields = x_ref.shape[0]
    chunks = x_ref.shape[1] // CHUNK
    top = LOW + CHUNK // LOW
    shape = table_ref.shape[1:]
    place = lax.broadcasted_iota(jnp.int32, shape, 0)
    place = jnp.where(
        place < LOW, place, jnp.where(place < top, (place - LOW) * LOW, (place - top) * CHUNK)
    )
    product = place.astype(jnp.float32) * lax.broadcasted_iota(jnp.int32, shape, 1).astype(jnp.float32)
    count = jnp.full(shape, points, jnp.int32).astype(jnp.float32)
    angle = (product - jnp.round(product / count) * count) * (two_pi / count)
    scale = jnp.where(lax.broadcasted_iota(jnp.int32, shape, 0) >= top, 1.0 / jnp.sqrt(count), 1.0)
    table_ref[0] = jnp.cos(angle) * scale
    table_ref[1] = -jnp.sin(angle) * scale
    low_c, low_s = table_ref[0, :LOW], table_ref[1, :LOW]
    for w in range(waves // 128):
        cut = slice(w * 128, w * 128 + 128)
        for b in range(0, CHUNK // LOW, 2):
            real, imag = [], []
            for q in (b, b + 1):
                mid_c = table_ref[0, LOW + q : LOW + q + 1, cut]
                mid_s = table_ref[1, LOW + q : LOW + q + 1, cut]
                real.append(low_c[:, cut] * mid_c - low_s[:, cut] * mid_s)
                imag.append(low_c[:, cut] * mid_s + low_s[:, cut] * mid_c)
            real = jnp.concatenate(real, axis=0).astype(jnp.bfloat16)
            imag = jnp.concatenate(imag, axis=0).astype(jnp.bfloat16)
            base_ref[w, b * LOW : (b + 2) * LOW, :128] = real
            base_ref[w, b * LOW : (b + 2) * LOW, 128:] = imag
    inputs[-1].wait()
    for a in range(chunks):
        position = a * CHUNK + lax.broadcasted_iota(jnp.int32, (fields, CHUNK), 1)
        block = x_ref[:, a * CHUNK : (a + 1) * CHUNK].astype(jnp.float32)
        xm_ref[a * fields : (a + 1) * fields] = jnp.where(position < points, block, 0.0).astype(
            jnp.bfloat16
        )
    for w in range(waves // 128):
        cut = slice(w * 128, w * 128 + 128)
        z_ref[...] = jnp.dot(xm_ref[...], base_ref[w], preferred_element_type=jnp.float32)
        real = jnp.zeros((fields, 128), jnp.float32)
        imag = jnp.zeros((fields, 128), jnp.float32)
        for a in range(chunks):
            turn_c = table_ref[0, top + a : top + a + 1, cut]
            turn_s = table_ref[1, top + a : top + a + 1, cut]
            part_r = z_ref[a * fields : (a + 1) * fields, :128]
            part_i = z_ref[a * fields : (a + 1) * fields, 128:]
            real = real + part_r * turn_c - part_i * turn_s
            imag = imag + part_r * turn_s + part_i * turn_c
        wave = w * 128 + lax.broadcasted_iota(jnp.int32, (fields, 128), 1)
        kept = wave < points // 2
        coefs_ref[:fields, cut] = jnp.where(kept, real, 0.0).astype(jnp.bfloat16)
        coefs_ref[fields:, cut] = jnp.where(kept, imag, 0.0).astype(jnp.bfloat16)
    padded = mine_ref.shape[1]

    slot_total = slots_ref.shape[0]
    slot_count = slot_total // lat_count
    ring = strip_ref.shape[1]
    lanes = -(-padded // 128) * 128
    strip_ref[...] = jnp.full_like(strip_ref, waves)
    strip_ref[0:1, :slot_total] = slots_ref[...].reshape(1, slot_total)

    def fill(other):
        held = pltpu.roll(strip_ref[...], ring - other * slot_count, 1)[0:1, :lanes]
        held = jnp.where(lax.broadcasted_iota(jnp.int32, (1, lanes), 1) < slot_count, held, waves)
        pick = held == lax.broadcasted_iota(jnp.int32, (waves, lanes), 0)
        pick = jnp.where(pick, 1.0, 0.0).astype(jnp.bfloat16)
        chosen = jnp.dot(coefs_ref[...], pick, preferred_element_type=jnp.float32)
        mine_ref[other] = chosen.T[:padded].astype(jnp.bfloat16)

    @pl.loop(1, lat_count)
    def _(step):
        fill((lat + step) % lat_count)
        lat_copy(step).start()

    fill(lat)
    own_coefs = pltpu.make_async_copy(mine_ref.at[lat], coef_out.at[group, lat], local_sem.at[1])
    own_coefs.start()

    def spread_piece(line_row):
        direct_copy(0, line_row).start()
        direct_copy(1, line_row).start()
        chip_copy(0, line_row).start()

    own_coefs.wait()
    spread_piece(lat)

    strata = fields // 4
    bottom = strata - 1
    wide = 512
    shift = span.bit_length() - 1

    def columns_of(start):
        place = start + lax.broadcasted_iota(jnp.int32, (1, wide), 1)
        return lax.shift_right_logical(place * points, shift)

    def pick(table, index):
        tiles = table.shape[1]
        one = lax.broadcasted_iota(jnp.int32, (tiles, wide), 0) == lax.shift_right_logical(index, 7)
        one = jnp.where(one, 1.0, 0.0).astype(jnp.bfloat16)
        lane = lax.broadcasted_iota(jnp.int32, (128, wide), 0) == (index & 127)
        spread = jnp.dot(table, one, preferred_element_type=jnp.float32)
        return [
            jnp.sum(jnp.where(lane, spread[k * 128 : (k + 1) * 128], 0.0), axis=0, keepdims=True)
            for k in range(table.shape[0] // 128)
        ]

    def table_of(values):
        tiles = values[0].shape[1] // 128
        return jnp.concatenate([v.reshape(tiles, 128).T for v in values], axis=0).astype(jnp.bfloat16)

    zonal = x_ref[bottom : bottom + 1].astype(jnp.float32)
    meridional = x_ref[strata + bottom : strata + bottom + 1].astype(jnp.float32)
    air = x_ref[2 * strata + bottom : 2 * strata + bottom + 1].astype(jnp.float32)
    speed = thermal_transfer_factor * jnp.sqrt(zonal * zonal + meridional * meridional + 1.0)
    table = table_of([speed, air])

    @pl.loop(0, span // wide)
    def _(k):
        start = pl.multiple_of(k * wide, wide)
        brisk, below = pick(table, columns_of(start))
        local_ref[0:1, pl.ds(start, wide)] = brisk
        local_ref[1:2, pl.ds(start, wide)] = below

    @pl.when(has_next)
    def _():
        halo_copy(0).wait_send()
        halo_copy(1).wait_recv()

    @pl.when(has_previous)
    def _():
        halo_copy(1).wait_send()
        halo_copy(0).wait_recv()

    @pl.when(jnp.logical_not(has_next))
    def _():
        after_ref[...] = jnp.zeros_like(after_ref)

    @pl.when(jnp.logical_not(has_previous))
    def _():
        before_ref[...] = jnp.zeros_like(before_ref)

    for start, held in ((0, before_ref), (2 * rows, after_ref)):
        for side in range(2):
            for r in range(0, rows, 2):
                first = side * deep + r * layers
                pair = held[first : first + 2 * layers].astype(jnp.float32)
                cut = slice(side * part, side * part + part)
                heat_ref[0, start + r, :, cut] = pair[:layers]
                heat_ref[0, start + r + 1, :, cut] = pair[layers:]

    under = under_ref[0] - (line - 1) * rows
    skin = jnp.zeros((1, span), jnp.float32)
    for r in range(3 * rows):
        skin = jnp.where(under == r, heat_ref[0, r, 0:1, :], skin)
    skin_table = table_of([skin])
    inverse = 1.0 / jnp.full((1, wide), points, jnp.int32).astype(jnp.float32)

    @pl.loop(0, span // wide)
    def _(k):
        start = pl.multiple_of(k * wide, wide)
        scaled = columns_of(start) << shift
        index = (scaled.astype(jnp.float32) * inverse).astype(jnp.int32)
        rest = scaled - index * points
        index = jnp.where(rest < 0, index - 1, jnp.where(rest >= points, index + 1, index))
        index = jnp.minimum(index, span - 1)
        (mapped,) = pick(skin_table, index)
        cut = pl.ds(start, wide)
        flux_ref[len(REACH), 0:1, cut] = local_ref[0:1, cut] * (mapped - local_ref[1:2, cut])

    lane = lax.broadcasted_iota(jnp.int32, (1, 128), 1)
    relative = jnp.zeros((1, 128), jnp.float32)
    for r in range(rows):
        relative = jnp.where(lane == r, (over_ref[r] - line).astype(jnp.float32), relative)
    flux_ref[len(REACH), 0:1, span:] = relative
    for k in range(len(REACH)):
        flux_copy(k).start()

    @pl.loop(1, lat_count)
    def _(step):
        lat_copy(step).wait_recv()
        spread_piece((lat + lat_count - step) % lat_count)

    weight_copy(7).start()

    edges = []
    for held in (before_ref, after_ref):
        coarse = held[2 * deep :].astype(jnp.float32)
        edges.append(jnp.concatenate([coarse[: 2 * rows], coarse[2 * rows :]], axis=1))
    kappa = jnp.concatenate([edges[0][:rows], plane_ref[:rows], edges[1][:rows]], axis=0)
    depth = jnp.concatenate([edges[0][rows:], plane_ref[rows:], edges[1][rows:]], axis=0)
    total = 3 * rows
    layer = lax.broadcasted_iota(jnp.int32, (layers, span), 0)
    beside = pltpu.roll(kappa, span - 1, 1)
    east = jnp.where((kappa > 0.0) & (beside > 0.0), 0.5 * (kappa + beside), 0.0)
    upper, lower = kappa[:-1], kappa[1:]
    faces = jnp.where((upper > 0.0) & (lower > 0.0), 0.5 * (upper + lower), 0.0)
    for r in range(1, total):
        face_ref[r] = jnp.broadcast_to(faces[r - 1 : r], (layers, span))
    for r in range(1, total - 1):
        east_ref[r] = jnp.broadcast_to(east[r : r + 1], (layers, span))
        down_ref[r] = jnp.where(layer < layers - 1, depth[r : r + 1], 0.0)

    for k in range(len(REACH)):
        flux_copy(k).wait()
    near = REACH + (0,)
    for r in range(1, total - 1):
        owner = r // rows - 1
        target = flux_ref[near.index(owner), 0:1, span + r % rows : span + r % rows + 1] + float(owner)
        row = jnp.zeros((1, span), jnp.float32)
        for k, step in enumerate(near):
            row = jnp.where(target == float(step), flux_ref[k, 0:1, :span], row)
        row = jnp.where(kappa[r : r + 1] > 0.0, force_coef * row, 0.0)
        source_ref[r] = jnp.where(layer == 0, row, 0.0)

    def ocean_step(step):
        held, made = step % 2, (step + 1) % 2

        @pl.loop(step + 1, total - step - 1)
        def _(r):
            mid = heat_ref[held, r]
            flow = face_ref[r + 1] * (heat_ref[held, r + 1] - mid) - face_ref[r] * (mid - heat_ref[held, r - 1])
            lateral = east_ref[r] * (pltpu.roll(mid, span - 1, 1) - mid)
            flow = flow + (lateral - pltpu.roll(lateral, 1, 1))
            sinking = down_ref[r] * (pltpu.roll(mid, layers - 1, 0) - mid)
            flow = flow + (sinking - pltpu.roll(sinking, 1, 0))
            fresh = mid + flow + source_ref[r]
            if step < OSTEPS - 1:
                heat_ref[made, r] = fresh
            else:
                thermal_out[r - rows] = fresh

    def forward(step):
        line_row = (lat + lat_count - step) % lat_count
        direct_copy(0, line_row).wait_recv()

        @pl.when(line_row % 2 == 0)
        def _():
            diag_copy(0, line_row).start()

        chip_copy(1, line_row).start()
        direct_copy(1, line_row).wait_recv()

        @pl.when(line_row % 2 == 1)
        def _():
            diag_copy(1, line_row).start()

        chip_copy(2, line_row).start()

    ocean_step(0)
    forward(0)
    forward(1)
    ocean_step(1)
    forward(2)
    forward(3)

    ocean_step(2)
    ocean_step(3)

    @pl.loop(0, lat_count)
    def _(step):
        line_row = (lat + lat_count - step) % lat_count
        diag_copy(0, line_row).wait_recv()
        chip_copy(3, line_row).start()

    own_weights.wait()

    @pl.loop(1, lat_count)
    def _(step):
        lat_copy(step).wait_send()

    @pl.loop(0, lat_count)
    def _(line_row):
        direct_copy(0, line_row).wait_send()
        direct_copy(1, line_row).wait_send()
        diag_copy(0, line_row).wait_send()
        for which in range(4):
            chip_copy(which, line_row).wait_send()

    @pl.loop(1, groups)
    def _(step):
        weight_copy(step).wait()

    @pl.loop(0, lat_count)
    def _(line_row):
        for which in range(4):
            chip_copy(which, line_row).wait_recv()


def fast_exchange(sizes, points, over, under, slots, state, weights, kappa, depth, water, ocean):
    sec_count, lat_count, col_count = sizes
    groups = sec_count * col_count
    fields, width = state.shape
    waves = weights.shape[2]
    table_rows = -(-(LOW + CHUNK // LOW + width // CHUNK) // 8) * 8
    layers, rows, span = ocean.shape
    padded = weights.shape[1]
    band = lat_count * padded // groups
    chunks = width // CHUNK
    halo_rows = 2 * rows * (layers + 2)
    inside = pl.BlockSpec(memory_space=pltpu.VMEM)
    outside = pl.BlockSpec(memory_space=pl.ANY)
    near = len(REACH)
    dma = pltpu.SemaphoreType.DMA
    return pl.pallas_call(
        functools.partial(fast_kernel, sizes),
        out_shape=[
            jax.ShapeDtypeStruct((groups, lat_count, padded, 2 * fields), jnp.bfloat16),
            jax.ShapeDtypeStruct((groups, band, waves), jnp.bfloat16),
            jax.ShapeDtypeStruct((rows, layers, span), jnp.float32),
        ],
        in_specs=[outside] * 5 + [inside] * 4 + [outside],
        out_specs=[inside] * 3,
        scratch_shapes=[
            pltpu.SMEM(points.shape, jnp.int32),
            pltpu.SMEM(over.shape, jnp.int32),
            pltpu.SMEM(under.shape, jnp.int32),
            pltpu.VMEM(slots.shape, jnp.int32),
            pltpu.VMEM(state.shape, state.dtype),
            pltpu.VMEM((2, table_rows, waves), jnp.float32),
            pltpu.VMEM((8, -(-(slots.shape[0] + 256) // 128) * 128), jnp.int32),
            pltpu.VMEM((groups, band, waves), jnp.bfloat16),
            pltpu.VMEM((waves // 128, CHUNK, 256), jnp.bfloat16),
            pltpu.VMEM((chunks * fields, CHUNK), jnp.bfloat16),
            pltpu.VMEM((chunks * fields, 256), jnp.float32),
            pltpu.VMEM((2 * fields, waves), jnp.bfloat16),
            pltpu.VMEM((lat_count, padded, 2 * fields), jnp.bfloat16),
            pltpu.VMEM((halo_rows, span // 2), jnp.bfloat16),
            pltpu.VMEM((halo_rows, span // 2), jnp.bfloat16),
            pltpu.VMEM((halo_rows, span // 2), jnp.bfloat16),
            pltpu.VMEM((2 * rows, span), jnp.float32),
            pltpu.VMEM((2, 3 * rows, layers, span), jnp.float32),
            pltpu.VMEM((3 * rows, layers, span), jnp.float32),
            pltpu.VMEM((3 * rows, layers, span), jnp.float32),
            pltpu.VMEM((3 * rows, layers, span), jnp.float32),
            pltpu.VMEM((3 * rows, layers, span), jnp.float32),
            pltpu.VMEM((2, span), jnp.float32),
            pltpu.VMEM((near + 1, 1, span + 128), jnp.float32),
            dma((5,)),
            dma((rows,)),
            dma((2,)),
            dma((groups,)),
            dma((groups,)),
            dma((2,)),
            dma((2,)),
            dma((near,)),
            dma((near,)),
            dma((lat_count,)),
            dma((lat_count,)),
            dma((2, lat_count)),
            dma((2, lat_count)),
            dma((lat_count,)),
            dma((lat_count,)),
            dma((4, lat_count)),
            dma((4, lat_count)),
        ],
        compiler_params=pltpu.CompilerParams(
            vmem_limit_bytes=28 * 2**20, collective_id=2, has_side_effects=True
        ),
        cost_estimate=pl.CostEstimate(
            flops=4 * fields * waves * width, bytes_accessed=8 * 2**20, transcendentals=0
        ),
    )(points, over, under, slots, state, weights, kappa, depth, water, ocean)


def fast_legendre_kernel(
    col_count,
    slots_hbm,
    weight_ref,
    coef_ref,
    ocean_ref,
    out_ref,
    ocean_out,
    slots_ref,
    turned_ref,
    made_ref,
    made_sem,
    ocean_sem,
    slots_sem,
):
    groups, lines, padded, width = coef_ref.shape
    slot_count, degrees, _ = out_ref.shape
    rows = ocean_ref.shape[0]
    blocks = padded // 16
    rest = slot_count - (blocks - 1) * 16
    halves = padded // weight_ref.shape[1]
    majors = blocks // halves
    ocean_copies = [
        pltpu.make_async_copy(ocean_ref.at[r], ocean_out.at[:, r, :], ocean_sem.at[r]) for r in range(rows)
    ]
    slots_copy = pltpu.make_async_copy(slots_hbm, slots_ref, slots_sem)
    slots_copy.start()
    for copy in ocean_copies:
        copy.start()
    first_slot = lax.axis_index("lat") * slot_count
    last_slot = slots_ref.shape[0] - 1
    first_degree = (lax.axis_index("sec") * col_count + lax.axis_index("col")) * degrees

    def made_copy(block, count):
        cut = pl.ds(block * 16, count)
        return pltpu.make_async_copy(made_ref.at[cut], out_ref.at[cut], made_sem.at[block])

    degree = first_degree + lax.broadcasted_iota(jnp.int32, (degrees, width), 0)
    odd = lax.broadcasted_iota(jnp.int32, (lines * groups * 16, width), 0) % 2 == 1
    lane_pair = lax.broadcasted_iota(jnp.int32, (degrees, lines * groups * 16), 1) % 16 // 2

    slots_copy.wait()

    for major in range(majors):
        held = weight_ref[:, major * 16 : major * 16 + 16, :]
        turned_ref[major % 2] = held.reshape(groups * 16, held.shape[2]).T
        for half in range(halves):
            block = half * majors + major
            values = jnp.concatenate(
                [
                    turned_ref[major % 2, (t * halves + half) * degrees : (t * halves + half + 1) * degrees, :]
                    for t in range(lines)
                ],
                axis=1,
            )
            cut = slice(block * 16, block * 16 + 16)
            coefs = jnp.concatenate(
                [coef_ref[:, t, cut, :].reshape(groups * 16, width) for t in range(lines)], axis=0
            )
            nothing = jnp.zeros_like(coefs)
            both = jnp.concatenate(
                [jnp.where(odd, nothing, coefs), jnp.where(odd, coefs, nothing)], axis=1
            )
            for q in range(0, 8, 4):
                left = jnp.concatenate(
                    [jnp.where(lane_pair == j, values, jnp.zeros_like(values)) for j in range(q, q + 4)],
                    axis=0,
                )
                summed = jnp.dot(left, both, preferred_element_type=jnp.float32)
                for s in range(2 * q, 2 * q + 8):
                    wave = slots_ref[jnp.minimum(first_slot + block * 16 + s, last_slot)]
                    low = (s // 2 - q) * degrees
                    part = summed[low : low + degrees, s % 2 * width : (s % 2 + 1) * width]
                    made_ref[block * 16 + s] = jnp.where(degree >= wave, part, 0.0)

            made_copy(block, 16 if block < blocks - 1 else rest).start()

    @pl.loop(0, blocks - 1)
    def _(block):
        made_copy(block, 16).wait()

    made_copy(blocks - 1, rest).wait()
    for copy in ocean_copies:
        copy.wait()


def fast_legendre(col_count, weights, coefs, ocean, slots, slot_count, degrees):
    groups, lines, padded, width = coefs.shape
    rows, layers, span = ocean.shape
    inside = pl.BlockSpec(memory_space=pltpu.VMEM)
    outside = pl.BlockSpec(memory_space=pl.ANY)
    anywhere = pl.BlockSpec(memory_space=pl.ANY)
    return pl.pallas_call(
        functools.partial(fast_legendre_kernel, col_count),
        out_shape=[
            jax.ShapeDtypeStruct((slot_count, degrees, width), jnp.float32),
            jax.ShapeDtypeStruct((layers, rows, span), jnp.float32),
        ],
        in_specs=[outside, inside, inside, inside],
        out_specs=[anywhere, anywhere],
        scratch_shapes=[
            pltpu.SMEM(slots.shape, jnp.int32),
            pltpu.VMEM((2, weights.shape[2], groups * 16), jnp.bfloat16),
            pltpu.VMEM((padded, degrees, width), jnp.float32),
            pltpu.SemaphoreType.DMA((padded // 16,)),
            pltpu.SemaphoreType.DMA((rows,)),
            pltpu.SemaphoreType.DMA,
        ],
        compiler_params=pltpu.CompilerParams(vmem_limit_bytes=32 * 2**20),
        cost_estimate=pl.CostEstimate(
            flops=2 * groups * lines * padded * width * degrees * 8,
            bytes_accessed=4 * slot_count * degrees * width,
            transcendentals=0,
        ),
    )(slots, weights, coefs, ocean)


def fast_body(
    physical_state,
    parallel_lengths,
    zonal_mode_assignment,
    weighted_associated_polynomials,
    marine_tracer_state,
    lateral_diffusivity,
    depthwise_diffusivity,
    water_indicator,
    overlying_parallel,
    underlying_marine_parallel,
):
    sizes = tuple(lax.axis_size(name) for name in LINE)
    sec_count, lat_count, col_count = sizes
    groups = sec_count * col_count
    slot_count, wave_count, _ = weighted_associated_polynomials.shape
    block_degrees = wave_count // groups
    padded = -(-slot_count // 32) * 32
    weights = jnp.transpose(weighted_associated_polynomials, (2, 0, 1))
    weights = jnp.pad(weights, ((0, 0), (0, padded - slot_count), (0, 0)))
    coefs, packed, ocean = fast_exchange(
        sizes,
        parallel_lengths,
        overlying_parallel,
        underlying_marine_parallel,
        zonal_mode_assignment,
        physical_state[0],
        weights,
        lateral_diffusivity,
        depthwise_diffusivity,
        water_indicator,
        marine_tracer_state,
    )
    harmonic, thermal = fast_legendre(
        col_count, packed, coefs, ocean, zonal_mode_assignment, slot_count, block_degrees
    )
    return (jnp.transpose(harmonic, (1, 0, 2)), thermal)


def compact(mesh):
    return mesh.shape["sec"] == 4 and mesh.shape["lat"] == 4 and mesh.shape["col"] == 2


def solution(mesh):
    return jax.shard_map(
        fast_body if compact(mesh) else body,
        mesh=mesh,
        in_specs=(
            P(LINE, None, None),
            P(LINE),
            P(),
            P("lat", None, GROUP),
            P(None, LINE, None),
            P(LINE, None),
            P(LINE, None),
            P(LINE, None),
            P(LINE),
            P(LINE),
        ),
        out_specs=(P(GROUP, "lat", None), P(None, LINE, None)),
        check_vma=False,
    )
```
